32 devices in a mesh: dp: 4 (over y, x), ctx: 2 (over core), fsdp: 4 (over z).
Axes of the slice: x: 2, y: 2, z: 4, core: 2. Of those that a mesh axis runs over, the one named last changes fastest.
Arguments:
- tokens: bfloat16 [16, 768, 1024], P(('dp', 'fsdp'), 'ctx'), may hold values from -6 to 6
- cotangent: bfloat16 [16, 768, 1024], P(('dp', 'fsdp'), 'ctx'), may hold values from -6 to 6
- ln1_gain: bfloat16 [1024], P('fsdp'), may hold values from 0.5 to 1.5
- ln1_bias: bfloat16 [1024], P('fsdp'), may hold values from -1.75 to 1.75
- ln2_gain: bfloat16 [1024], P('fsdp'), may hold values from 0.5 to 1.5
- ln2_bias: bfloat16 [1024], P('fsdp'), may hold values from -1.75 to 1.75
- qkv_weight: bfloat16 [1024, 3072], P('fsdp'), may hold values from -0.1875 to 0.1875
- qkv_bias: bfloat16 [3072], P('fsdp'), may hold values from -1.75 to 1.75
- out_weight: bfloat16 [1024, 1024], P('fsdp'), may hold values from -1.5 to 1.5
- out_bias: bfloat16 [1024], P('fsdp'), may hold values from -1.75 to 1.75
- up_weight: bfloat16 [1024, 4096], P('fsdp'), may hold values from -0.1875 to 0.1875
- up_bias: bfloat16 [4096], P('fsdp'), may hold values from -1.75 to 1.75
- down_weight: bfloat16 [4096, 1024], P('fsdp'), may hold values from -0.09375 to 0.09375
- down_bias: bfloat16 [1024], P('fsdp'), may hold values from -1.75 to 1.75
Outputs:
- layer_out: bfloat16 [16, 768, 1024], P(('dp', 'fsdp'), 'ctx')
- grad_tokens: bfloat16 [16, 768, 1024], P(('dp', 'fsdp'), 'ctx')
- grad_ln1_gain: float32 [1024], P('fsdp')
- grad_ln1_bias: float32 [1024], P('fsdp')
- grad_ln2_gain: float32 [1024], P('fsdp')
- grad_ln2_bias: float32 [1024], P('fsdp')
- grad_qkv_weight: float32 [1024, 3072], P('fsdp')
- grad_qkv_bias: float32 [3072], P('fsdp')
- grad_out_weight: float32 [1024, 1024], P('fsdp')
- grad_out_bias: float32 [1024], P('fsdp')
- grad_up_weight: float32 [1024, 4096], P('fsdp')
- grad_up_bias: float32 [4096], P('fsdp')
- grad_down_weight: float32 [4096, 1024], P('fsdp')
- grad_down_bias: float32 [1024], P('fsdp')
The draws below stay inside these ranges and needn't reach their ends.
All inputs are finite; a program needn't handle non-finite values.
Results may differ from the reference program's by a relative error of at most 0.018.
Values may be sent and summed in bfloat16 or wider, within the bound.
A program may use at most 256 MiB of HBM per device.

```python
import math
import jax
import jax.numpy as jnp
from jax import lax

D = 1024
H = 16
HD = 64
ROT = 16
FF = 4096
LENGTH = 768
SEQS = 16


def block_scale(key, extent, cuts, low, top_value):
    def one(axis_at, blocks):
        steps = jax.random.uniform(jax.random.fold_in(jax.random.fold_in(key, 6), axis_at), (blocks,), jnp.float32, low / len(cuts), top_value / len(cuts))
        return jnp.repeat(jnp.exp(steps), extent[axis_at] // blocks).reshape((-1,) + (1,) * (len(extent) - axis_at - 1))

    factor_of = one(*cuts[0])
    for cut in cuts[1:]:
        factor_of = factor_of * one(*cut)
    return factor_of


def noise(own_key, shape, scale, reach, shards=(), kind=jnp.bfloat16):
    drawn = jax.random.normal(own_key, shape, jnp.float32) * scale
    if len(shards) > 0:
        drawn = block_scale(own_key, shape, shards, -0.22, 0.18) * drawn
    return jnp.clip(drawn, min=-reach, max=reach).astype(kind)


def setup_inputs(seed: int = 0) -> dict:
    key_of = jax.random.split(jax.random.key(seed), 15)
    tokens = noise(key_of[0], (SEQS, LENGTH, D), 1.0, 6.0, ((0, 16), (1, 2)))
    cotangent = noise(key_of[1], (SEQS, LENGTH, D), 1.0, 6.0, ((0, 16), (1, 2)))
    ln1_gain = jnp.clip(1.0 + 0.1 * jax.random.normal(key_of[2], (D,), jnp.float32), 0.5, 1.5).astype(jnp.bfloat16)
    ln1_bias = noise(key_of[3], (D,), 0.3, 1.75, ((0, 4),))
    ln2_gain = jnp.clip(1.0 + 0.1 * jax.random.normal(key_of[4], (D,), jnp.float32), 0.5, 1.5).astype(jnp.bfloat16)
    ln2_bias = noise(key_of[5], (D,), 0.3, 1.75, ((0, 4),))
    qkv_weight = noise(key_of[6], (D, 3 * D), D ** -0.5, 0.1875, ((0, 4),))
    qkv_bias = noise(key_of[7], (3 * D,), 0.3, 1.75, ((0, 4),))
    out_weight = noise(key_of[8], (D, D), (D // 64) ** -0.5, 1.5, ((0, 4),))
    out_bias = noise(key_of[9], (D,), 0.3, 1.75, ((0, 4),))
    up_weight = noise(key_of[10], (D, FF), D ** -0.5, 0.1875, ((0, 4),))
    up_bias = noise(key_of[11], (FF,), 0.3, 1.75, ((0, 4),))
    down_weight = noise(key_of[12], (FF, D), FF ** -0.5, 0.09375, ((0, 4),))
    down_bias = noise(key_of[13], (D,), 0.3, 1.75, ((0, 4),))
    return {"tokens": tokens, "cotangent": cotangent, "ln1_gain": ln1_gain, "ln1_bias": ln1_bias, "ln2_gain": ln2_gain, "ln2_bias": ln2_bias, "qkv_weight": qkv_weight, "qkv_bias": qkv_bias, "out_weight": out_weight, "out_bias": out_bias, "up_weight": up_weight, "up_bias": up_bias, "down_weight": down_weight, "down_bias": down_bias}


EPS = 1e-05
HIGH = lax.Precision.HIGHEST

@jax.custom_vjp
def low(v):
    return lax.optimization_barrier(v.astype(jnp.bfloat16)).astype(jnp.float32)

@jax.custom_vjp
def low_back(v):
    return v

def low_keep(v):
    return (low(v), None)

def low_pass(kept, grad):
    return (grad,)

def back_keep(v):
    return (v, None)

def back_low(kept, grad):
    return (low(grad),)
low.defvjp(low_keep, low_pass)
low_back.defvjp(back_keep, back_low)

def product(left, right):
    return jnp.dot(left, right, precision=HIGH, preferred_element_type=jnp.float32)

def normed(features, gain_vec, shift_vec):
    centre = features - lax.optimization_barrier(jnp.mean(features, axis=-1, keepdims=True))
    spread = lax.optimization_barrier(jnp.mean(centre * centre, axis=-1, keepdims=True))
    return centre * lax.rsqrt(spread + EPS) * gain_vec + shift_vec

def angles(positions):
    frequency = 10000.0 ** (-(jnp.arange(ROT // 2) * 2).astype(jnp.float32) / ROT)
    angle_rows = positions.astype(jnp.float32)[:, None] * frequency[None, :]
    angle_rows = jnp.concatenate([angle_rows, angle_rows], axis=-1)
    return (jnp.cos(angle_rows), jnp.sin(angle_rows))

def rotate(tensor, cosine, sine_table):
    half_rot = ROT // 2
    rot_part = tensor[..., :ROT]
    turned = jnp.concatenate([-rot_part[..., half_rot:], rot_part[..., :half_rot]], axis=-1)
    rotated = rot_part * cosine[:, None, :] + turned * sine_table[:, None, :]
    return jnp.concatenate([rotated, tensor[..., ROT:]], axis=-1)

def attention(queries, keys_rot, values_in):
    block_rows = math.gcd(LENGTH, 512)
    block_count = LENGTH // block_rows
    query_blocks = queries.reshape(block_count, block_rows, H, HD)
    block_starts = jnp.arange(block_count, dtype=jnp.int32) * block_rows
    key_places = jnp.arange(LENGTH, dtype=jnp.int32)
    score_scale = HD ** (-0.5)

    @jax.checkpoint
    def per_block(pair_in):
        query_block, start_row = pair_in
        scores = low_back(jnp.einsum('qhd,khd->hqk', query_block, keys_rot, precision=HIGH) * score_scale)
        query_places = start_row + jnp.arange(block_rows, dtype=jnp.int32)
        allowed = key_places[None, None, :] <= query_places[None, :, None]
        scores = jnp.where(allowed, scores, -1000000000.0)
        probabilities = low(jax.nn.softmax(scores, axis=-1))
        return jnp.einsum('hqk,khd->qhd', probabilities, values_in, precision=HIGH)
    attended = lax.map(per_block, (query_blocks, block_starts))
    return attended.reshape(LENGTH, H * HD)

def forward(features, gain_one, shift_one, gain_two, shift_two, w_qkv, b_qkv, w_out, b_out, w_up, b_up, w_down, b_down):
    normed_first = low(normed(features, gain_one, shift_one))
    normed_second = low(normed(features, gain_two, shift_two))
    merged_proj = low_back(product(normed_first, w_qkv) + b_qkv)
    cosine, sine_table = angles(jnp.arange(LENGTH, dtype=jnp.int32))
    queries = low(rotate(merged_proj[:, :D].reshape(LENGTH, H, HD), cosine, sine_table))
    keys_rot = low(rotate(merged_proj[:, D:2 * D].reshape(LENGTH, H, HD), cosine, sine_table))
    values_in = low(merged_proj[:, 2 * D:].reshape(LENGTH, H, HD))
    mixed_rows = low_back(low(attention(queries, keys_rot, values_in)))
    attn_out = product(mixed_rows, w_out) + b_out
    hidden = low_back(product(normed_second, w_up) + b_up)
    activated = low(jax.nn.gelu(hidden, approximate=False))
    return features + attn_out + product(activated, w_down) + b_down

def reference(tokens, cotangent, ln1_gain, ln1_bias, ln2_gain, ln2_bias, qkv_weight, qkv_bias, out_weight, out_bias, up_weight, up_bias, down_weight, down_bias):
    params = tuple((item.astype(jnp.float32) for item in (ln1_gain, ln1_bias, ln2_gain, ln2_bias, qkv_weight, qkv_bias, out_weight, out_bias, up_weight, up_bias, down_weight, down_bias)))

    def per_sequence(running_sum, pair_in):
        sequence_in, cotangent_row = pair_in
        layer_out, pullback = jax.vjp(forward, sequence_in.astype(jnp.float32), *params)
        gradients = pullback(cotangent_row.astype(jnp.float32))
        running_sum = tuple((left + right for left, right in zip(running_sum, gradients[1:])))
        return (running_sum, (layer_out.astype(jnp.bfloat16), gradients[0].astype(jnp.bfloat16)))
    zero_sums = tuple((jnp.zeros_like(item) for item in params))
    totals, (outputs, input_grads) = lax.scan(per_sequence, zero_sums, (tokens, cotangent))
    return (outputs, input_grads, totals[0], totals[1], totals[2], totals[3], totals[4], totals[5], totals[6], totals[7], totals[8], totals[9], totals[10], totals[11])
```

```python
import functools
import math

import jax
import jax.numpy as jnp
import numpy as np
from jax import lax
from jax.experimental import pallas as pl
from jax.experimental.pallas import tpu as pltpu
from jax.sharding import PartitionSpec as P

H = 16
HD = 64
ROT = 16
EPS = 1e-05
BF = jnp.bfloat16
F32 = jnp.float32
MESH = pl.DeviceIdType.MESH
QT = 256
NSMALL = 13


def nn(a, b):
    return lax.dot_general(a, b, (((1,), (0,)), ((), ())), preferred_element_type=F32)


def nt(a, b):
    return lax.dot_general(a, b, (((1,), (1,)), ((), ())), preferred_element_type=F32)


def tn(a, b):
    return lax.dot_general(a, b, (((0,), (0,)), ((), ())), preferred_element_type=F32)


def flat(v):
    return v.reshape(-1, v.shape[-1])


def rcopy(src, dst, ss, rs, dev):
    return pltpu.make_async_remote_copy(
        src_ref=src, dst_ref=dst, send_sem=ss, recv_sem=rs, device_id=dev, device_id_type=MESH
    )


def lcopy(src, dst, sem):
    return pltpu.make_async_copy(src, dst, sem)


def mult(v, m):
    return pl.multiple_of(v, m)


def stats(xf):
    mean = jnp.mean(xf, axis=-1, keepdims=True)
    cen = xf - mean
    var = jnp.mean(cen * cen, axis=-1, keepdims=True)
    return cen, lax.rsqrt(var + EPS)


def gelu_parts(h):
    a = jnp.abs(h)
    t = 1.0 / (1.0 + (0.3275911 * 0.5**0.5) * a)
    e = jnp.exp(-0.5 * h * h)
    poly = t * (
        0.127414796
        + t * (-0.142248368 + t * (0.7107068705 + t * (-0.7265760135 + t * 0.5307027145)))
    )
    tail = poly * e
    cum = jnp.where(h >= 0, 1.0 - tail, tail)
    return h * cum, cum + h * e * ((2.0 * math.pi) ** -0.5)


class Plan:
    def __init__(self, mesh, tokens, wqkv, wup, wdown):
        self.dp, self.ctx, self.n = mesh.shape["dp"], mesh.shape["ctx"], mesh.shape["fsdp"]
        self.D = tokens.shape[2]
        self.R = tokens.shape[1]
        self.L = self.R * self.ctx
        self.u = wqkv.shape[0]
        self.FF = wup.shape[1]
        self.ffs = wdown.shape[0]
        self.hq = self.D // self.dp
        self.fq = self.FF // self.dp
        self.g = max(128, self.ffs // self.dp)
        self.nl = self.fq // self.g
        self.no = self.hq // self.u
        self.heads = self.hq // HD
        self.spc = self.dp // self.ctx
        self.nb = self.spc * self.ctx
        self.T = self.nb * self.R


def make_kernel(pn):
    dp, n, D, R, u, ffs, hq, fq = pn.dp, pn.n, pn.D, pn.R, pn.u, pn.ffs, pn.hq, pn.fq
    G_, nl, no, heads, spc, nb, T, L = pn.g, pn.nl, pn.no, pn.heads, pn.spc, pn.nb, pn.T, pn.L
    uh, gh = u // 2, G_ // 2
    nqt = L // QT
    kq = QT // u
    RC = 128
    scale = HD**-0.5

    def kernel(
        x_h, dy_h, sm_h, wq_h, wo_h, wu_h, wd_h, cos_r, sin_r,
        yo_h, dxo_h, gq_h, go_h, gu_h, gd_h, gs_h,
        X, DY, A1, A2, WQ, WU, WD, WO, QKV, O, DO, PS0, PS1, PS2, GA, SL, YS, YR,
        GQ, GU, GD, GO, RU, RD, ZD, FU, FD,
        SM, SB, VEC, SG, RSG, ZSG, FSG, PSG, LNA, UBA, QBA, DYA, DKA, DVA,
        xss, xrs, dss, drs, smss, smrs,
        wqs, wqr, wus, wur, wds, wdr, wos, wor, fws, fwr,
        yss, yrs, zss, zrs,
        gds, gdr, zqs, zqr, zus, zur, zds, zdr, zos, zor,
        pqs, pqr, pus, pur, pds, pdr, pos, por, pfs, pfr,
        sgs, sgr, zsgs, zsgr, psgs, psgr, loc, zfree, yfree,
    ):
        p = lax.axis_index("dp")
        c = lax.axis_index("ctx")
        z = lax.axis_index("fsdp")
        sib = (p, 1 - c, z)
        home = p // spc
        oblk = lax.rem(p, spc) * 2 + c
        PSS = (PS0, PS1, PS2)
        RQ, RO = GA.at[0:n, :, 0 : 3 * hq], GA.at[n : n + no]
        ZU, ZQ = A2.at[0 : n - 1], A2.at[n - 1 : 2 * n - 2, :, 0 : 3 * hq]
        ZO = A2.at[2 * n - 2 : 3 * n - 3]
        FQ, FO = GA.at[n + no, :, 0 : 3 * hq], GA.at[n + no + 1]

        def ga(b):
            return pl.ds(b * (R // uh), R // uh)

        def rot(v, k):
            return lax.rem(v, k)

        bar = pltpu.get_barrier_semaphore()
        partners = [sib]
        for i in range(1, dp):
            partners += [(rot(p + i, dp), 0, z), (rot(p + i, dp), 1, z)]
        for i in range(1, n):
            partners.append((p, c, rot(z + i, n)))
        for d in partners:
            pl.semaphore_signal(bar, inc=1, device_id=d, device_id_type=MESH)
        pl.semaphore_wait(bar, len(partners))

        def spread(src, buf, ss, rs, op):
            for i in range(1, dp):
                d = rcopy(src, buf.at[oblk], ss.at[i], rs.at[oblk], (rot(p + i, dp), home, z))
                getattr(d, op)()

            @pl.when(home == c)
            def _():
                if op == "start":
                    lcopy(src, buf.at[oblk], rs.at[oblk]).start()

            @pl.when(home != c)
            def _():
                getattr(rcopy(src, buf.at[oblk], ss.at[0], rs.at[oblk], sib), op)()

        def got(buf, rs, b):
            rcopy(buf.at[b], buf.at[b], xss.at[0], rs.at[b], sib).wait_recv()

        def small(op):
            for i in range(1, n):
                d = rcopy(sm_h, SB.at[z], smss.at[i], smrs.at[z], (p, c, rot(z + i, n)))
                getattr(d, op)()

        qcols = [(mult(j * D + p * hq, 128), j * hq, hq) for j in range(3)]
        ucols = [(mult((k * dp + p) * G_, 128), k * G_, G_) for k in range(nl)]

        def d_owner(k):
            return ((k * dp + p) * G_) // ffs

        def d_row(k):
            return rot((k * dp + p) * G_, ffs)

        def o_owner(k):
            return p * no + k

        def o_row(k):
            return 0

        def send_a(src, W, cols, ss, rs, op):
            for k, (sc, dc, w) in enumerate(cols):
                s = src.at[pl.ds(mult(c * uh, uh), uh), pl.ds(sc, w)]
                t = W.at[z, c, :, pl.ds(dc, w)]
                for i in range(1, n):
                    getattr(rcopy(s, t, ss.at[i, k], rs.at[z, k], (p, c, rot(z + i, n))), op)()
                if op == "start":
                    lcopy(s, t, rs.at[z, k]).start()

        def send_b(src, W, pieces, owner, row, half, ss, rs, op):
            for k in range(pieces):

                @pl.when(owner(k) == z)
                def _():
                    s = src.at[pl.ds(mult(row(k) + c * half, half), half)]
                    for i in range(1, n):
                        d = rcopy(s, W.at[k, c], ss.at[i], rs.at[k], (p, c, rot(z + i, n)))
                        getattr(d, op)()
                    if op == "start":
                        lcopy(s, W.at[k, c], rs.at[k]).start()

        def recv_a(W, cols, rs):
            for k in range(n):
                for j, (_, dc, w) in enumerate(cols):
                    t = W.at[k, c, :, pl.ds(dc, w)]
                    rcopy(t, t, xss.at[0], rs.at[k, j], sib).wait_recv()

        def recv_b(W, pieces, rs):
            for k in range(pieces):
                rcopy(W.at[k, c], W.at[k, c], xss.at[0], rs.at[k], sib).wait_recv()

        def pass_on(W, k, op):
            side = c if op != "wait_recv" else 1 - c
            getattr(rcopy(W.at[:, side], W.at[:, side], fws.at[k], fwr.at[k], sib), op)()

        lcopy(sm_h, SB.at[z], smrs.at[z]).start()
        spread(x_h, X, xss, xrs, "start")
        small("start")
        send_a(wq_h, WQ, qcols, wqs, wqr, "start")

        for r in (LNA, UBA, QBA, DYA, SG):
            r[...] = jnp.zeros(r.shape, F32)

        for k in range(n):
            rcopy(SB.at[k], SB.at[k], xss.at[0], smrs.at[k], sib).wait_recv()
        for row, r in ((0, 0), (1, 1), (2, 2), (3, 3)):
            VEC[row] = jnp.concatenate([SB[k, r] for k in range(n)], axis=1)
        VEC[4] = jnp.concatenate([SB[k, 7] + SB[k, 12] for k in range(n)], axis=1)
        units = []
        for k in range(nl):
            for i in range(G_ // u if G_ >= u else 1):
                unit = ((k * dp + p) * G_) // u + i
                units.append(SB[unit // (ffs // u), 8 + rot(unit, ffs // u)])
        VEC[5] = jnp.concatenate(units, axis=1)
        for j in range(3):
            units = []
            for i in range(no):
                unit = (j * D + p * hq) // u + i
                units.append(SB[unit // 3, 4 + rot(unit, 3)])
            VEC[6, :, j * hq : (j + 1) * hq] = jnp.concatenate(units, axis=1)

        def blk(i):
            return rot(p + i // 2, spc) * 2 + rot(c + i, 2)

        def norm_step(i, _):
            b = blk(i)
            got(X, xrs, b)

            def part(k, _):
                rc = pl.ds(mult(k * RC, RC), RC)
                cen, rstd = stats(X[b, rc, :].astype(F32))
                xh = cen * rstd
                A1[b, rc, :] = (xh * VEC[0] + VEC[1]).astype(BF)
                A2[pl.ds((b * R + k * RC) // uh, RC // uh)] = (
                    (xh * VEC[2] + VEC[3]).astype(BF).reshape(RC // uh, uh, D)
                )
                return 0

            lax.fori_loop(0, R // RC, part, 0)
            return 0

        lax.fori_loop(0, 2, norm_step, 0)
        send_a(wu_h, WU, ucols, wus, wur, "start")
        lax.fori_loop(2, nb, norm_step, 0)
        spread(x_h, X, xss, xrs, "wait_send")
        spread(dy_h, DY, dss, drs, "start")

        recv_a(WQ, qcols, wqr)
        pass_on(WQ, 0, "start")
        send_b(wd_h, WD, nl, d_owner, d_row, gh, wds, wdr, "start")
        send_b(wo_h, WO, no, o_owner, o_row, uh, wos, wor, "start")
        pass_on(WQ, 0, "wait_recv")

        def turn(v, r0, sign):
            out = []
            ct, st = cos_r[pl.ds(r0, v.shape[0]), :], sin_r[pl.ds(r0, v.shape[0]), :]
            first = lax.broadcasted_iota(jnp.int32, ct.shape, 1) % HD < ROT // 2
            for j in range(hq // 128):
                w = v[:, j * 128 : (j + 1) * 128]
                back = st * jnp.where(
                    first, pltpu.roll(w, 128 - ROT // 2, 1), pltpu.roll(w, ROT // 2, 1)
                )
                out.append(w * ct + (back if sign > 0 else -back))
            return jnp.concatenate(out, axis=1)

        def rows(b):
            return pl.ds(mult(b * R, R), R)

        def qkv_step(b, _):
            a = A1[b]
            r0 = mult(rot(b, 2) * R, R)
            for j in range(3):
                w = flat(WQ[:, :, :, j * hq : (j + 1) * hq])
                f = nn(a, w) + VEC[6, :, j * hq : (j + 1) * hq]
                if j < 2:
                    f = turn(f, r0, 1)
                if j == 0:
                    f = f * scale
                QKV[rows(b), j * hq : (j + 1) * hq] = f.astype(BF)
            return 0

        lax.fori_loop(0, nb, qkv_step, 0)

        def head_mask(h):
            lane = lax.broadcasted_iota(jnp.int32, (1, hq), 1)
            return ((lane // HD) == h).astype(F32).astype(BF)

        def attn_step(s, _):
            base = mult(s * L, L)
            for t in range(nqt):
                ext = (t + 1) * QT
                q = QKV[pl.ds(base + t * QT, QT), 0:hq]
                keys = QKV[pl.ds(base, ext), hq : 2 * hq]
                vals = QKV[pl.ds(base, ext), 2 * hq : 3 * hq]
                out = jnp.zeros((QT, hq), F32)
                below = lax.broadcasted_iota(jnp.int32, (QT, ext), 1) <= (
                    lax.broadcasted_iota(jnp.int32, (QT, ext), 0) + t * QT
                )
                for h in range(heads):
                    m = head_mask(h)
                    sc = jnp.where(below, nt(q * m, keys), -1e9)
                    e = jnp.exp(sc - jnp.max(sc, axis=-1, keepdims=True))
                    pr = (e * (1.0 / jnp.sum(e, axis=-1, keepdims=True))).astype(BF)
                    PSS[t][s, h * QT : (h + 1) * QT, :] = pr
                    out = out + nn(pr, vals * m)
                O[pl.ds(base + t * QT, QT), :] = out.astype(BF)
            return 0

        lax.fori_loop(0, spc, attn_step, 0)

        recv_a(WU, ucols, wur)
        pass_on(WU, 1, "start")
        pass_on(WU, 1, "wait_recv")

        def up_step(b, _):
            a = flat(A2[ga(b)])
            for j in range(fq // 256):
                cs = slice(j * 256, (j + 1) * 256)
                h = nn(a, flat(WU[:, :, :, cs])) + VEC[5, :, cs]
                g, sl = gelu_parts(h)
                GA[ga(b), :, cs] = g.astype(BF).reshape(R // uh, uh, 256)
                SL[b, :, cs] = sl.astype(BF)
            return 0

        lax.fori_loop(0, nb, up_step, 0)

        recv_b(WD, nl, wdr)
        pass_on(WD, 2, "start")
        recv_b(WO, no, wor)
        pass_on(WO, 3, "start")
        pass_on(WD, 2, "wait_recv")
        pass_on(WO, 3, "wait_recv")

        def hand(src, buf, ss, rs, i, op):
            b = blk(i)
            s, h = c * spc + b // 2, rot(b, 2)
            mine = jnp.logical_and(s == p, h == c)

            @pl.when(mine)
            def _():
                if op == "start":
                    lcopy(src.at[b], buf.at[p], rs.at[p]).start()

            @pl.when(jnp.logical_not(mine))
            def _():
                getattr(rcopy(src.at[b], buf.at[p], ss.at[b], rs.at[p], (s, h, z)), op)()

        def y_step(i, _):
            b = blk(i)
            for j in range(D // 256):
                cs = slice(j * 256, (j + 1) * 256)
                y = nn(flat(GA[ga(b)]), flat(WD[:, :, :, cs])) + nn(O[rows(b), :], flat(WO[:, :, :, cs]))
                YS[b, :, cs] = y.astype(BF)
            hand(YS, YR, yss, yrs, i, "start")
            return 0

        lax.fori_loop(0, nb, y_step, 0)

        def dh_step(i, _):
            b = blk(i)
            got(DY, drs, b)
            dy = DY[b]
            for j in range(fq // 256):
                cs = slice(j * 256, (j + 1) * 256)
                k = 256 // G_
                dg = nt(dy, flat(WD[j * k : (j + 1) * k]))
                dh = (dg * SL[b, :, cs].astype(F32)).astype(BF)
                SL[b, :, cs] = dh
                UBA[:, cs] += jnp.sum(dh.astype(F32), axis=0, keepdims=True)
            DO[rows(b), :] = nt(dy, flat(WO[...])).astype(BF)
            part = DY[b, :, pl.ds(mult(p * hq, 128), hq)]
            DYA[...] += jnp.sum(part.astype(F32), axis=0, keepdims=True)
            return 0

        lax.fori_loop(0, nb, dh_step, 0)

        def grad(left, right, dst, rows_, cols_, tm, tc, half):
            for a in range(rows_ // tm):
                for b in range(cols_ // tc):
                    v = tn(left(a * tm, tm), right(b * tc, tc)).astype(BF)
                    k = tm // (2 * half)
                    dst[a * k : (a + 1) * k, :, :, b * tc : (b + 1) * tc] = v.reshape(
                        k, 2, half, tc
                    )

        grad(lambda o, w: flat(GA[:, :, o : o + w]), lambda o, w: flat(DY[:, :, o : o + w]),
             GD, fq, D, 512, 512, gh)

        def swap(src, dst, k, op):
            getattr(rcopy(src.at[:, 1 - c], dst, gds.at[k], gdr.at[k], sib), op)()

        swap(GD, RD, 0, "start")
        grad(lambda o, w: flat(A2[:, :, o : o + w]), lambda o, w: flat(SL[:, :, o : o + w]),
             GU, D, fq, 512, 512, uh)
        swap(GU, RU, 1, "start")
        for i in range(1, n):
            pl.semaphore_signal(
                zfree, inc=1, device_id=(p, c, rot(z + i, n)), device_id_type=MESH
            )

        def attn_back(s, _):
            base = mult(s * L, L)
            DKA[...] = jnp.zeros(DKA.shape, F32)
            DVA[...] = jnp.zeros(DVA.shape, F32)
            for t in range(nqt):
                ext = (t + 1) * QT
                qr = pl.ds(base + t * QT, QT)
                q = QKV[qr, 0:hq]
                keys = QKV[pl.ds(base, ext), hq : 2 * hq]
                vals = QKV[pl.ds(base, ext), 2 * hq : 3 * hq]
                do = DO[qr, :]
                dq = jnp.zeros((QT, hq), F32)
                for h in range(heads):
                    m = head_mask(h)
                    hs = slice(h * QT, (h + 1) * QT)
                    pr = PSS[t][s, hs, :].astype(F32)
                    dpr = nt(do * m, vals)
                    ds = (pr * (dpr - jnp.sum(pr * dpr, axis=-1, keepdims=True))).astype(BF)
                    GQ[h * kq : (h + 1) * kq, :, :, 0:ext] = ds.reshape(kq, 2, uh, ext)
                    dq = dq + nn(ds, keys * m)
                qs = jnp.concatenate([q * head_mask(h) for h in range(heads)], axis=0)
                dos = jnp.concatenate([do * head_mask(h) for h in range(heads)], axis=0)
                for k in range(t + 1):
                    ks = slice(k * QT, (k + 1) * QT)
                    DKA[ks, :] += tn(flat(GQ[:, :, :, ks]), qs)
                    DVA[ks, :] += tn(PSS[t][s, :, ks], dos)
                dqr = turn(dq * scale, t * QT, -1).astype(BF)
                QKV[qr, 0:hq] = dqr
                QBA[:, 0:hq] += jnp.sum(dqr.astype(F32), axis=0, keepdims=True)
            for t in range(nqt):
                kr = pl.ds(base + t * QT, QT)
                ts = slice(t * QT, (t + 1) * QT)
                dk = turn(DKA[ts, :], t * QT, -1).astype(BF)
                dv = DVA[ts, :].astype(BF)
                QKV[kr, hq : 2 * hq] = dk
                QKV[kr, 2 * hq : 3 * hq] = dv
                QBA[:, hq : 2 * hq] += jnp.sum(dk.astype(F32), axis=0, keepdims=True)
                QBA[:, 2 * hq : 3 * hq] += jnp.sum(dv.astype(F32), axis=0, keepdims=True)
            return 0

        def add_half(dst, src, k, pieces):
            rcopy(src, src, gds.at[k], gdr.at[k], sib).wait_recv()

            def one(i, _):
                dst[i, c] = (dst[i, c].astype(F32) + src[i].astype(F32)).astype(BF)
                return 0

            lax.fori_loop(0, pieces, one, 0)

        def line_a(src, Z, ss, rs, op):
            for i in range(1, n):
                to = rot(z + i, n)
                d = rcopy(src.at[to, c], Z.at[n - 1 - i], ss.at[i], rs.at[n - 1 - i], (p, c, to))
                getattr(d, op)()

        def line_b(src, Z, pieces, owner, ss, rs, op):
            for k in range(pieces):

                @pl.when(owner(k) != z)
                def _():
                    slot = rot(z - owner(k) - 1 + n, n)
                    d = rcopy(src.at[k, c], Z.at[slot], ss.at[k], rs.at[slot], (p, c, owner(k)))
                    getattr(d, op)()

        def line_sum(own, Z, F, rs):
            for i in range(n - 1):
                rcopy(Z.at[i], Z.at[i], xss.at[0], rs.at[i], sib).wait_recv()
            F[...] = (own().astype(F32) + sum_of(Z)).astype(BF)

        def sum_of(Z):
            acc = Z[0].astype(F32)
            for i in range(1, n - 1):
                acc = acc + Z[i].astype(F32)
            return acc

        def line_sum_b(src, Z, F, pieces, owner, rs, then):
            for k in range(pieces):

                @pl.when(owner(k) == z)
                def _():
                    line_sum(lambda: src[k, c], Z, F, rs)
                    then(k, "start")

        def plane(F, dst_of, parts, ss, rs, base, op):
            for k, w in enumerate(parts):
                s = F if w is None else F.at[:, pl.ds(w[0], w[1])]
                for i in range(1, dp):
                    d = rcopy(s, dst_of(k), ss.at[i, k], rs.at[dp - 1 - i, k], (rot(p + i, dp), c, z))
                    getattr(d, op)()
                ld = lcopy(s, dst_of(k), loc.at[base + k])
                if op == "start":
                    ld.start()
                else:
                    ld.wait()

        half_rows = pl.ds(mult(c * uh, uh), uh)

        def plane_q(op):
            plane(FQ, lambda k: gq_h.at[half_rows, pl.ds(qcols[k][0], hq)],
                  [(j * hq, hq) for j in range(3)], pqs, pqr, 1, op)

        def plane_u(op):
            plane(FU, lambda k: gu_h.at[half_rows, pl.ds(ucols[k][0], G_)],
                  [(j * G_, G_) for j in range(nl)], pus, pur, 4, op)

        def plane_d(k, op):
            plane(FD, lambda _: gd_h.at[pl.ds(mult(d_row(k) + c * gh, gh), gh)], [None], pds, pdr, 4 + nl, op)

        def plane_o(k, op):
            plane(FO, lambda _: go_h.at[half_rows], [None], pos, por, 5 + nl, op)

        per = ffs // G_

        def d_who(i):
            return rot(z * per + i, dp)

        o_who = (z * u) // hq

        def plane_recv_cols(dst, width_of, starts, rs):
            for i in range(1, dp):
                src_p = rot(p + i, dp)
                for k in range(len(starts)):
                    t = dst.at[half_rows, pl.ds(mult(starts[k](src_p), 128), width_of)]
                    rcopy(t, t, xss.at[0], rs.at[i - 1, k], sib).wait_recv()

        def shard_on(dst, k, op):
            r = half_rows if op != "wait_recv" else pl.ds(mult((1 - c) * uh, uh), uh)
            getattr(rcopy(dst.at[r], dst.at[r], pfs.at[k], pfr.at[k], sib), op)()

        def d_recv():
            for i in range(per):
                t = gd_h.at[pl.ds(mult(i * G_ + c * gh, gh), gh)]

                @pl.when(d_who(i) != p)
                def _():
                    slot = rot(d_who(i) - p - 1 + dp, dp)
                    rcopy(t, t, xss.at[0], pdr.at[slot, 0], sib).wait_recv()

        def d_on(op):
            for i in range(per):
                side = c if op != "wait_recv" else 1 - c
                t = gd_h.at[pl.ds(mult(i * G_ + side * gh, gh), gh)]
                getattr(rcopy(t, t, pfs.at[3 + i], pfr.at[3 + i], sib), op)()

        def o_recv():
            @pl.when(o_who != p)
            def _():
                slot = rot(o_who - p - 1 + dp, dp)
                t = go_h.at[half_rows]
                rcopy(t, t, xss.at[0], por.at[slot, 0], sib).wait_recv()

        lax.fori_loop(0, 1, attn_back, 0)
        add_half(GD, RD, 0, nl)
        pl.semaphore_wait(zfree, n - 1)
        line_b(GD, ZD, nl, d_owner, zds, zdr, "start")
        add_half(GU, RU, 1, n)
        line_a(GU, ZU, zus, zur, "start")
        lax.fori_loop(1, spc, attn_back, 0)

        tfl = slice(None)
        grad(lambda o, w: O[tfl, o : o + w], lambda o, w: flat(DY[:, :, o : o + w]),
             GO, hq, D, 256, 512, uh)
        swap(GO, RO, 2, "start")
        grad(lambda o, w: flat(A1[:, :, o : o + w]), lambda o, w: QKV[tfl, o : o + w],
             GQ, D, 3 * hq, 512, 256, uh)
        swap(GQ, RQ, 3, "start")

        lcopy(x_h, A1.at[0], loc.at[0]).start()
        lcopy(dy_h, A1.at[1], loc.at[6 + nl]).start()
        for q in range(dp):
            rcopy(YR.at[q], YR.at[q], xss.at[0], yrs.at[q], sib).wait_recv()
        lcopy(x_h, A1.at[0], loc.at[0]).wait()
        lcopy(dy_h, A1.at[1], loc.at[6 + nl]).wait()
        for j in range(D // 256):
            cs = slice(j * 256, (j + 1) * 256)
            acc = A1[0, :, cs].astype(F32) + VEC[4, :, cs]
            for q in range(dp):
                acc = acc + YR[q, :, cs].astype(F32)
            A1[2, :, cs] = acc.astype(BF)
        lcopy(A1.at[2], yo_h, loc.at[7 + nl]).start()
        for i in range(dp):
            q = rot(p + i, dp)
            if i == 0:

                @pl.when(home == c)
                def _():
                    pl.semaphore_signal(yfree, inc=1)

                @pl.when(home != c)
                def _():
                    pl.semaphore_signal(yfree, inc=1, device_id=sib, device_id_type=MESH)
            else:
                pl.semaphore_signal(yfree, inc=1, device_id=(q, home, z), device_id_type=MESH)

        add_half(GO, RO, 2, no)
        line_b(GO, ZO, no, o_owner, zos, zor, "start")
        add_half(GQ, RQ, 3, n)
        line_a(GQ, ZQ, zqs, zqr, "start")

        def ysent(i, _):
            hand(YS, YR, yss, yrs, i, "wait_send")
            return 0

        lax.fori_loop(0, nb, ysent, 0)

        def dz_step(i, _):
            b = blk(i)

            def part(q, _):
                rc = pl.ds(mult(q * RC, RC), RC)
                cen, rstd = stats(X[b, rc, :].astype(F32))
                X[b, rc, :] = (cen * rstd).astype(BF)
                return 0

            lax.fori_loop(0, R // RC, part, 0)
            k = 256 // u if u <= 256 else 1
            for j in range(D // 256):
                cs = slice(j * 256, (j + 1) * 256)
                xh = X[b, :, cs].astype(F32)
                d1 = nt(QKV[rows(b), :], flat(WQ[j * k : (j + 1) * k]))
                d2 = nt(SL[b], flat(WU[j * k : (j + 1) * k]))
                LNA[0, :, cs] += jnp.sum(d1 * xh, axis=0, keepdims=True)
                LNA[1, :, cs] += jnp.sum(d1, axis=0, keepdims=True)
                LNA[2, :, cs] += jnp.sum(d2 * xh, axis=0, keepdims=True)
                LNA[3, :, cs] += jnp.sum(d2, axis=0, keepdims=True)
                YS[b, :, cs] = (d1 * VEC[0, :, cs] + d2 * VEC[2, :, cs]).astype(BF)
            hand(YS, YR, zss, zrs, i, "start")
            return 0

        pl.semaphore_wait(yfree, nb)
        lax.fori_loop(0, 2, dz_step, 0)
        line_sum_b(GD, ZD, FD, nl, d_owner, zdr, plane_d)
        line_sum(lambda: GU[z, c], ZU, FU, zur)
        plane_u("start")
        lax.fori_loop(2, nb, dz_step, 0)

        for r in range(4):
            v = LNA[r]
            for k in range(n):
                SG[k, r] = v[:, k * u : (k + 1) * u]
        v = QBA[...]
        for j in range(3):
            for i in range(no):
                unit = (j * D + p * hq) // u + i
                SG[unit // 3, 4 + rot(unit, 3)] = v[:, j * hq + i * u : j * hq + (i + 1) * u]
        v = DYA[...]
        for i in range(no):
            SG[p * no + i, 7] = v[:, i * u : (i + 1) * u]
            SG[p * no + i, 12] = v[:, i * u : (i + 1) * u]
        v = UBA[...]
        for k in range(nl):
            for i in range(G_ // u):
                unit = ((k * dp + p) * G_) // u + i
                o = k * G_ + i * u
                SG[unit // (ffs // u), 8 + rot(unit, ffs // u)] = v[:, o : o + u]
        rcopy(SG, RSG, sgs, sgr, sib).start()

        line_sum_b(GO, ZO, FO, no, o_owner, zor, plane_o)
        line_sum(lambda: GQ[z, c], ZQ, FQ, zqr)
        plane_q("start")

        rcopy(SG, RSG, sgs, sgr, sib).wait()
        SG[...] = SG[...] + RSG[...]

        def line_s(op):
            for i in range(1, n):
                to = rot(z + i, n)
                d = rcopy(SG.at[to], ZSG.at[n - 1 - i], zsgs.at[i], zsgr.at[n - 1 - i], (p, c, to))
                getattr(d, op)()

        line_s("start")

        d_recv()
        for k in range(nl):

            @pl.when(d_owner(k) == z)
            def _():
                plane_d(k, "wait_send")

        d_on("start")
        plane_recv_cols(gu_h, G_, [lambda q, k=k: (k * dp + q) * G_ for k in range(nl)], pur)
        plane_u("wait_send")
        shard_on(gu_h, 1, "start")

        for i in range(n - 1):
            rcopy(ZSG.at[i], ZSG.at[i], xss.at[0], zsgr.at[i], sib).wait_recv()
        FSG[...] = SG[z] + sum_of(ZSG)

        def plane_s(op):
            for i in range(1, dp):
                to = (rot(p + i, dp), c, z)
                getattr(rcopy(FSG, PSG.at[dp - 1 - i], psgs.at[i], psgr.at[dp - 1 - i], to), op)()

        plane_s("start")

        for q in range(dp):
            rcopy(YR.at[q], YR.at[q], xss.at[0], zrs.at[q], sib).wait_recv()

        def token_grad(k, _):
            rc = pl.ds(mult(k * RC, RC), RC)
            cen, rstd = stats(A1[0, rc, :].astype(F32))
            xh = cen * rstd
            tot = YR[0, rc, :].astype(F32)
            for q in range(1, dp):
                tot = tot + YR[q, rc, :].astype(F32)
            m1 = jnp.mean(tot, axis=-1, keepdims=True)
            m2 = jnp.mean(tot * xh, axis=-1, keepdims=True)
            A1[3, rc, :] = (A1[1, rc, :].astype(F32) + rstd * (tot - m1 - xh * m2)).astype(BF)
            return 0

        lax.fori_loop(0, R // RC, token_grad, 0)
        lcopy(A1.at[3], dxo_h, loc.at[0]).start()

        for i in range(dp - 1):
            rcopy(PSG.at[i], PSG.at[i], xss.at[0], psgr.at[i], sib).wait_recv()
        acc = FSG[...]
        for i in range(dp - 1):
            acc = acc + PSG[i]
        SM[...] = acc
        lcopy(SM, gs_h, loc.at[6 + nl]).start()

        o_recv()
        for k in range(no):

            @pl.when(o_owner(k) == z)
            def _():
                plane_o(k, "wait_send")

        shard_on(go_h, 2, "start")
        plane_recv_cols(gq_h, hq, [lambda q, j=j: j * D + q * hq for j in range(3)], pqr)
        plane_q("wait_send")
        shard_on(gq_h, 0, "start")

        for k in range(3):
            shard_on((gq_h, gu_h, go_h)[k], k, "wait_recv")
            shard_on((gq_h, gu_h, go_h)[k], k, "wait_send")
        d_on("wait_recv")
        d_on("wait_send")
        small("wait_send")
        send_a(wq_h, WQ, qcols, wqs, wqr, "wait_send")
        send_a(wu_h, WU, ucols, wus, wur, "wait_send")
        send_b(wd_h, WD, nl, d_owner, d_row, gh, wds, wdr, "wait_send")
        send_b(wo_h, WO, no, o_owner, o_row, uh, wos, wor, "wait_send")
        for k, W in enumerate((WQ, WU, WD, WO)):
            pass_on(W, k, "wait_send")
        spread(dy_h, DY, dss, drs, "wait_send")
        for k, (s, d) in enumerate(((GD, RD), (GU, RU), (GO, RO), (GQ, RQ))):
            swap(s, d, k, "wait_send")
        line_b(GD, ZD, nl, d_owner, zds, zdr, "wait_send")
        line_a(GU, ZU, zus, zur, "wait_send")
        line_b(GO, ZO, no, o_owner, zos, zor, "wait_send")
        line_a(GQ, ZQ, zqs, zqr, "wait_send")
        line_s("wait_send")
        plane_s("wait_send")

        def zsent(i, _):
            hand(YS, YR, zss, zrs, i, "wait_send")
            return 0

        lax.fori_loop(0, nb, zsent, 0)
        lcopy(A1.at[2], yo_h, loc.at[7 + nl]).wait()
        lcopy(A1.at[3], dxo_h, loc.at[0]).wait()
        lcopy(SM, gs_h, loc.at[6 + nl]).wait()

    return kernel


def tables(length):
    freq = (np.float32(10000.0) ** (-(np.arange(ROT // 2) * 2).astype(np.float32) / ROT)).astype(
        np.float32
    )
    ang = np.arange(length, dtype=np.float32)[:, None] * freq[None, :]
    co, si = np.cos(ang).astype(np.float32), np.sin(ang).astype(np.float32)
    half = ROT // 2
    ct = np.ones((length, HD), np.float32)
    st = np.zeros((length, HD), np.float32)
    ct[:, :half], ct[:, half:ROT] = co, co
    st[:, :half], st[:, half:ROT] = -si, si
    return tuple(np.concatenate([t, t], axis=1) for t in (ct, st))


def body(mesh, tokens, cotangent, ln1_gain, ln1_bias, ln2_gain, ln2_bias, qkv_weight, qkv_bias,
         out_weight, out_bias, up_weight, up_bias, down_weight, down_bias):
    pn = Plan(mesh, tokens, qkv_weight, up_weight, down_weight)
    n, D, R, u, ffs, hq, fq, dp = pn.n, pn.D, pn.R, pn.u, pn.ffs, pn.hq, pn.fq, pn.dp
    G_, nl, no, nb, T, L, spc = pn.g, pn.nl, pn.no, pn.nb, pn.T, pn.L, pn.spc
    uh, gh = u // 2, G_ // 2
    small = jnp.concatenate(
        [ln1_gain, ln1_bias, ln2_gain, ln2_bias, qkv_bias, out_bias, up_bias, down_bias]
    ).astype(F32).reshape(NSMALL, 1, u)
    ct, st = tables(L)
    vm = lambda *s, t=BF: pltpu.VMEM(s, t)
    dma = lambda *s: pltpu.SemaphoreType.DMA(s)
    scratch = [
        vm(nb, R, D), vm(nb, R, D), vm(nb, R, D), vm(T // uh, uh, D),
        vm(n, 2, uh, 3 * hq), vm(n, 2, uh, fq), vm(nl, 2, gh, D), vm(no, 2, uh, D),
        vm(T, 3 * hq), vm(T, hq), vm(T, hq),
        vm(spc, pn.heads * QT, QT), vm(spc, pn.heads * QT, 2 * QT), vm(spc, pn.heads * QT, 3 * QT),
        vm(T // uh, uh, fq), vm(nb, R, fq), vm(nb, R, D), vm(dp, R, D),
        vm(n, 2, uh, 3 * hq), vm(n, 2, uh, fq), vm(nl, 2, gh, D), vm(no, 2, uh, D),
        vm(n, uh, fq), vm(nl, gh, D),
        vm(n - 1, gh, D),
        vm(uh, fq), vm(gh, D),
        vm(NSMALL, 1, u, t=F32), vm(n, NSMALL, 1, u, t=F32), vm(7, 1, max(D, fq), t=F32),
        vm(n, NSMALL, 1, u, t=F32), vm(n, NSMALL, 1, u, t=F32), vm(n - 1, NSMALL, 1, u, t=F32),
        vm(NSMALL, 1, u, t=F32), vm(dp - 1, NSMALL, 1, u, t=F32),
        vm(4, 1, D, t=F32), vm(1, fq, t=F32), vm(1, 3 * hq, t=F32), vm(1, hq, t=F32),
        vm(L, hq, t=F32), vm(L, hq, t=F32),
        dma(dp), dma(nb), dma(dp), dma(nb), dma(n), dma(n),
        dma(n, 3), dma(n, 3), dma(n, nl), dma(n, nl), dma(n), dma(nl), dma(n), dma(no), dma(4), dma(4),
        dma(nb), dma(dp), dma(nb), dma(dp),
        dma(4), dma(4), dma(n), dma(n), dma(n), dma(n), dma(nl), dma(n), dma(no), dma(n),
        dma(dp, 3), dma(dp, 3), dma(dp, nl), dma(dp, nl), dma(dp, 1), dma(dp, 1), dma(dp, 1), dma(dp, 1),
        dma(3 + ffs // G_), dma(3 + ffs // G_),
        pltpu.SemaphoreType.DMA, pltpu.SemaphoreType.DMA, dma(n), dma(n), dma(dp), dma(dp), dma(8 + nl),
        pltpu.SemaphoreType.REGULAR, pltpu.SemaphoreType.REGULAR,
    ]
    hbm = pl.BlockSpec(memory_space=pl.ANY)
    vmem = pl.BlockSpec(memory_space=pltpu.VMEM)
    sds = jax.ShapeDtypeStruct
    y, dx, gq, go, gu, gd, gs = pl.pallas_call(
        make_kernel(pn),
        out_shape=(
            sds((R, D), BF), sds((R, D), BF), sds((u, 3 * D), BF), sds((u, D), BF),
            sds((u, pn.FF), BF), sds((ffs, D), BF), sds((NSMALL, 1, u), F32),
        ),
        in_specs=[hbm] * 7 + [vmem] * 2,
        out_specs=[hbm] * 7,
        scratch_shapes=scratch,
        compiler_params=pltpu.CompilerParams(
            collective_id=0, has_side_effects=True, vmem_limit_bytes=63 * 2**20
        ),
    )(tokens[0], cotangent[0], small, qkv_weight, out_weight, up_weight, down_weight,
      jnp.asarray(ct), jnp.asarray(st))
    sv = gs.reshape(NSMALL * u)
    return (
        y[None], dx[None], sv[0:u], sv[u : 2 * u], sv[2 * u : 3 * u], sv[3 * u : 4 * u],
        gq.astype(F32), sv[4 * u : 7 * u], go.astype(F32), sv[7 * u : 8 * u],
        gu.astype(F32), sv[8 * u : 12 * u], gd.astype(F32), sv[12 * u : 13 * u],
    )


def solution(mesh):
    row = P(("dp", "fsdp"), "ctx", None)
    vec, mat = P("fsdp"), P("fsdp", None)
    in_specs = (row, row, vec, vec, vec, vec, mat, vec, mat, vec, mat, vec, mat, vec)
    out_specs = (row, row, vec, vec, vec, vec, mat, vec, mat, vec, mat, vec, mat, vec)
    return jax.shard_map(
        functools.partial(body, mesh), mesh=mesh, in_specs=in_specs, out_specs=out_specs, check_vma=False
    )
```

```python
import functools
import math

import jax
import jax.numpy as jnp
import numpy as np
from jax import lax
from jax.experimental import pallas as pl
from jax.experimental.pallas import tpu as pltpu
from jax.sharding import PartitionSpec as P

H = 16
HD = 64
ROT = 16
EPS = 1e-05
BF = jnp.bfloat16
F32 = jnp.float32
MESH = pl.DeviceIdType.MESH
QT = 256
NSMALL = 13


def nn(a, b):
    return lax.dot_general(a, b, (((1,), (0,)), ((), ())), preferred_element_type=F32)


def nt(a, b):
    return lax.dot_general(a, b, (((1,), (1,)), ((), ())), preferred_element_type=F32)


def tn(a, b):
    return lax.dot_general(a, b, (((0,), (0,)), ((), ())), preferred_element_type=F32)


def flat(v):
    return v.reshape(-1, v.shape[-1])


def rcopy(src, dst, ss, rs, dev):
    return pltpu.make_async_remote_copy(
        src_ref=src, dst_ref=dst, send_sem=ss, recv_sem=rs, device_id=dev, device_id_type=MESH
    )


def lcopy(src, dst, sem):
    return pltpu.make_async_copy(src, dst, sem)


def mult(v, m):
    return pl.multiple_of(v, m)


def stats(xf):
    mean = jnp.mean(xf, axis=-1, keepdims=True)
    cen = xf - mean
    var = jnp.mean(cen * cen, axis=-1, keepdims=True)
    return cen, lax.rsqrt(var + EPS)


def gelu_parts(h):
    a = jnp.abs(h)
    t = 1.0 / (1.0 + (0.3275911 * 0.5**0.5) * a)
    e = jnp.exp(-0.5 * h * h)
    poly = t * (
        0.127414796
        + t * (-0.142248368 + t * (0.7107068705 + t * (-0.7265760135 + t * 0.5307027145)))
    )
    tail = poly * e
    cum = jnp.where(h >= 0, 1.0 - tail, tail)
    return h * cum, cum + h * e * ((2.0 * math.pi) ** -0.5)


class Plan:
    def __init__(self, mesh, tokens, wqkv, wup, wdown):
        self.dp, self.ctx, self.n = mesh.shape["dp"], mesh.shape["ctx"], mesh.shape["fsdp"]
        self.D = tokens.shape[2]
        self.R = tokens.shape[1]
        self.L = self.R * self.ctx
        self.u = wqkv.shape[0]
        self.FF = wup.shape[1]
        self.ffs = wdown.shape[0]
        self.hq = self.D // self.dp
        self.fq = self.FF // self.dp
        self.g = max(128, self.ffs // self.dp)
        self.nl = self.fq // self.g
        self.no = self.hq // self.u
        self.heads = self.hq // HD
        self.spc = self.dp // self.ctx
        self.nb = self.spc * self.ctx
        self.T = self.nb * self.R


def make_kernel(pn):
    dp, n, D, R, u, ffs, hq, fq = pn.dp, pn.n, pn.D, pn.R, pn.u, pn.ffs, pn.hq, pn.fq
    G_, nl, no, heads, spc, nb, T, L = pn.g, pn.nl, pn.no, pn.heads, pn.spc, pn.nb, pn.T, pn.L
    uh, gh = u // 2, G_ // 2
    nqt = L // QT
    kq = QT // u
    RC = 128
    scale = HD**-0.5

    def kernel(
        x_h, dy_h, sm_h, wq_h, wo_h, wu_h, wd_h, cos_r, sin_r,
        yo_h, dxo_h, gq_h, go_h, gu_h, gd_h, gs_h,
        X, DY, A1, A2, WQ, WU, WD, WO, QKV, O, DO, PS0, PS1, PS2, GA, SL, YS, YR, RL, XO, YO,
        GQ, GU, GD, GO, RU, RD, ZD, FU, FD,
        SM, SB, VEC, SG, RSG, ZSG, FSG, PSG, LNA, UBA, QBA, DYA, DKA, DVA,
        xss, xrs, dss, drs, smss, smrs,
        wqs, wqr, wus, wur, wds, wdr, wos, wor, fws, fwr,
        yss, yrs, zss, zrs,
        gds, gdr, zqs, zqr, zus, zur, zds, zdr, zos, zor,
        pqs, pqr, pus, pur, pds, pdr, pos, por, pfs, pfr,
        sgs, sgr, zsgs, zsgr, psgs, psgr, loc, zfree, yfree, rus, rds, rlr,
    ):
        p = lax.axis_index("dp")
        c = lax.axis_index("ctx")
        z = lax.axis_index("fsdp")
        sib = (p, 1 - c, z)
        home = p // spc
        oblk = lax.rem(p, spc) * 2 + c
        e = lax.rem(p, 2)
        p1, p2, p3 = p + 1 - 2 * e, lax.rem(p + 2, 4), 3 - p
        away = home + c - 2 * home * c
        via, to_ = p1 + away * (p2 - p1), p2 + away * (p1 - p2)
        fblk = lax.rem(via, spc) * 2 + away
        PSS = (PS0, PS1, PS2)
        RQ, RO = GA.at[0:n, :, 0 : 3 * hq], GA.at[n : n + no]
        ZU, ZQ = A2.at[0 : n - 1], A2.at[n - 1 : 2 * n - 2, :, 0 : 3 * hq]
        ZO = A2.at[2 * n - 2 : 3 * n - 3]
        FQ, FO = GA.at[n + no, :, 0 : 3 * hq], GA.at[n + no + 1]

        def ga(b):
            return pl.ds(b * (R // uh), R // uh)

        def rot(v, k):
            return lax.rem(v, k)

        bar = pltpu.get_barrier_semaphore()
        partners = [sib]
        for i in range(1, dp):
            partners += [(rot(p + i, dp), 0, z), (rot(p + i, dp), 1, z)]
        for i in range(1, n):
            partners.append((p, c, rot(z + i, n)))
        for d in partners:
            pl.semaphore_signal(bar, inc=1, device_id=d, device_id_type=MESH)
        pl.semaphore_wait(bar, len(partners))

        def spread(src, buf, ss, rs, op):
            for i, q in ((1, p1), (2, p2)):
                getattr(rcopy(src, buf.at[oblk], ss.at[i], rs.at[oblk], (q, home, z)), op)()

            @pl.when(home == c)
            def _():
                if op == "start":
                    lcopy(src, buf.at[oblk], rs.at[oblk]).start()

            @pl.when(home != c)
            def _():
                getattr(rcopy(src, buf.at[oblk], ss.at[0], rs.at[oblk], sib), op)()

        def got(buf, rs, b):
            rcopy(buf.at[b], buf.at[b], xss.at[0], rs.at[b], sib).wait_recv()

        def hand_on(buf, ss, rs, op):
            if op == "start":
                got(buf, rs, fblk)
            d = rcopy(buf.at[fblk], buf.at[fblk], ss.at[3], rs.at[fblk], (to_, c, z))
            getattr(d, op)()

        def got_other(buf, rs, b):
            @pl.when(b != fblk)
            def _():
                got(buf, rs, b)

        def small(op):
            for i in range(1, n):
                d = rcopy(sm_h, SB.at[z], smss.at[i], smrs.at[z], (p, c, rot(z + i, n)))
                getattr(d, op)()

        qcols = [(mult(j * D + p * hq, 128), j * hq, hq) for j in range(3)]
        ucols = [(mult((k * dp + p) * G_, 128), k * G_, G_) for k in range(nl)]

        def d_owner(k):
            return ((k * dp + p) * G_) // ffs

        def d_row(k):
            return rot((k * dp + p) * G_, ffs)

        def o_owner(k):
            return p * no + k

        def o_row(k):
            return 0

        far = n >= 4

        def peers(send):
            for i in range(1, n):
                if far and i == 1:
                    pl.when(z != n - 1)(functools.partial(send, i))
                elif far and i == n - 1:
                    pl.when(z != 0)(functools.partial(send, i))
                else:
                    send(i)

        def direct(send):
            for i in range(1, n):
                send(i)

        def send_a(src, W, cols, ss, rs, each, op):
            for k, (sc, dc, w) in enumerate(cols):
                s = src.at[pl.ds(mult(c * uh, uh), uh), pl.ds(sc, w)]
                t = W.at[z, c, :, pl.ds(dc, w)]
                each(
                    lambda i: getattr(
                        rcopy(s, t, ss.at[i, k], rs.at[z, k], (p, c, rot(z + i, n))), op
                    )()
                )
                if op == "start":
                    lcopy(s, t, rs.at[z, k]).start()

        def send_b(src, W, pieces, owner, row, half, ss, rs, each, op):
            for k in range(pieces):

                @pl.when(owner(k) == z)
                def _():
                    s = src.at[pl.ds(mult(row(k) + c * half, half), half)]
                    each(
                        lambda i: getattr(
                            rcopy(s, W.at[k, c], ss.at[i], rs.at[k], (p, c, rot(z + i, n))), op
                        )()
                    )
                    if op == "start":
                        lcopy(s, W.at[k, c], rs.at[k]).start()

        def part_wait(W, k, dc, w, sem):
            t = W.at[k, c, :, pl.ds(dc, w)]
            rcopy(t, t, xss.at[0], sem, sib).wait_recv()

        def recv_a(W, cols, rs, each):
            for k in range(n):

                def one():
                    for j, (_, dc, w) in enumerate(cols):
                        part_wait(W, k, dc, w, rs.at[k, j])

                if far and each is peers and k == 0:
                    pl.when(z != n - 2)(one)
                elif far and each is peers and k == n - 1:
                    pl.when(z != 1)(one)
                else:
                    one()

        def relay_a(W, cols, ss, rs, op):
            if far:
                for at, k, to in ((1, n - 1, 0), (n - 2, 0, n - 1)):

                    @pl.when(z == at)
                    def _():
                        for j, (_, dc, w) in enumerate(cols):
                            if op == "start":
                                part_wait(W, k, dc, w, rs.at[k, j])
                            t = W.at[k, c, :, pl.ds(dc, w)]
                            getattr(rcopy(t, t, ss.at[j], rs.at[k, j], (p, c, to)), op)()

        def recv_b(W, pieces, owner, rs, each):
            for k in range(pieces):

                def one():
                    rcopy(W.at[k, c], W.at[k, c], xss.at[0], rs.at[k], sib).wait_recv()

                if far and each is peers:
                    first = jnp.logical_and(owner(k) == n - 1, z == 1)
                    last = jnp.logical_and(owner(k) == 0, z == n - 2)
                    pl.when(jnp.logical_not(jnp.logical_or(first, last)))(one)
                else:
                    one()

        def relay_b(W, pieces, owner, ss, rs, op):
            if far:
                for k in range(pieces):
                    for at, o, to in ((1, n - 1, 0), (n - 2, 0, n - 1)):

                        @pl.when(jnp.logical_and(owner(k) == o, z == at))
                        def _():
                            t = W.at[k, c]
                            d = rcopy(t, t, ss.at[k], rs.at[k], (p, c, to))
                            if op == "start":
                                d.wait_recv()
                            getattr(d, op)()

        def pass_on(W, k, op):
            side = c if op != "wait_recv" else 1 - c
            getattr(rcopy(W.at[:, side], W.at[:, side], fws.at[k], fwr.at[k], sib), op)()

        lcopy(sm_h, SB.at[z], smrs.at[z]).start()
        spread(x_h, X, xss, xrs, "start")
        small("start")
        send_a(wq_h, WQ, qcols, wqs, wqr, direct, "start")
        send_a(wu_h, WU, ucols, wus, wur, peers, "start")

        for r in (LNA, UBA, QBA, DYA, SG):
            r[...] = jnp.zeros(r.shape, F32)

        for k in range(n):
            rcopy(SB.at[k], SB.at[k], xss.at[0], smrs.at[k], sib).wait_recv()
        for row, r in ((0, 0), (1, 1), (2, 2), (3, 3)):
            VEC[row] = jnp.concatenate([SB[k, r] for k in range(n)], axis=1)
        VEC[4] = jnp.concatenate([SB[k, 7] + SB[k, 12] for k in range(n)], axis=1)
        units = []
        for k in range(nl):
            for i in range(G_ // u if G_ >= u else 1):
                unit = ((k * dp + p) * G_) // u + i
                units.append(SB[unit // (ffs // u), 8 + rot(unit, ffs // u)])
        VEC[5] = jnp.concatenate(units, axis=1)
        for j in range(3):
            units = []
            for i in range(no):
                unit = (j * D + p * hq) // u + i
                units.append(SB[unit // 3, 4 + rot(unit, 3)])
            VEC[6, :, j * hq : (j + 1) * hq] = jnp.concatenate(units, axis=1)

        def blk(i):
            return rot(p + i // 2, spc) * 2 + rot(c + i, 2)

        def norm_step(i, _):
            b = blk(i)
            got_other(X, xrs, b)

            def part(k, _):
                rc = pl.ds(mult(k * RC, RC), RC)
                cen, rstd = stats(X[b, rc, :].astype(F32))
                xh = cen * rstd
                A1[b, rc, :] = (xh * VEC[0] + VEC[1]).astype(BF)
                A2[pl.ds((b * R + k * RC) // uh, RC // uh)] = (
                    (xh * VEC[2] + VEC[3]).astype(BF).reshape(RC // uh, uh, D)
                )
                return 0

            lax.fori_loop(0, R // RC, part, 0)
            return 0

        @pl.when(away == 1)
        def _():
            hand_on(X, xss, xrs, "start")

        lax.fori_loop(0, 2, norm_step, 0)

        @pl.when(away == 0)
        def _():
            hand_on(X, xss, xrs, "start")

        spread(x_h, X, xss, xrs, "wait_send")
        spread(dy_h, DY, dss, drs, "start")
        lax.fori_loop(2, nb, norm_step, 0)

        recv_a(WQ, qcols, wqr, direct)
        pass_on(WQ, 0, "start")
        relay_a(WU, ucols, rus, wur, "start")
        send_b(wd_h, WD, nl, d_owner, d_row, gh, wds, wdr, peers, "start")
        send_b(wo_h, WO, no, o_owner, o_row, uh, wos, wor, direct, "start")
        pass_on(WQ, 0, "wait_recv")

        def turn(v, r0, sign):
            out = []
            ct, st = cos_r[pl.ds(r0, v.shape[0]), :], sin_r[pl.ds(r0, v.shape[0]), :]
            first = lax.broadcasted_iota(jnp.int32, ct.shape, 1) % HD < ROT // 2
            for j in range(hq // 128):
                w = v[:, j * 128 : (j + 1) * 128]
                back = st * jnp.where(
                    first, pltpu.roll(w, 128 - ROT // 2, 1), pltpu.roll(w, ROT // 2, 1)
                )
                out.append(w * ct + (back if sign > 0 else -back))
            return jnp.concatenate(out, axis=1)

        def rows(b):
            return pl.ds(mult(b * R, R), R)

        def qkv_step(b, _):
            a = A1[b]
            r0 = mult(rot(b, 2) * R, R)
            for j in range(3):
                w = flat(WQ[:, :, :, j * hq : (j + 1) * hq])
                f = nn(a, w) + VEC[6, :, j * hq : (j + 1) * hq]
                if j < 2:
                    f = turn(f, r0, 1)
                if j == 0:
                    f = f * scale
                QKV[rows(b), j * hq : (j + 1) * hq] = f.astype(BF)
            return 0

        lax.fori_loop(0, nb, qkv_step, 0)

        def head_mask(h):
            lane = lax.broadcasted_iota(jnp.int32, (1, hq), 1)
            return ((lane // HD) == h).astype(F32).astype(BF)

        def attn_step(s, _):
            base = mult(s * L, L)
            for t in range(nqt):
                ext = (t + 1) * QT
                q = QKV[pl.ds(base + t * QT, QT), 0:hq]
                keys = QKV[pl.ds(base, ext), hq : 2 * hq]
                vals = QKV[pl.ds(base, ext), 2 * hq : 3 * hq]
                out = jnp.zeros((QT, hq), F32)
                below = lax.broadcasted_iota(jnp.int32, (QT, ext), 1) <= (
                    lax.broadcasted_iota(jnp.int32, (QT, ext), 0) + t * QT
                )
                for h in range(heads):
                    m = head_mask(h)
                    sc = jnp.where(below, nt(q * m, keys), -1e9)
                    e = jnp.exp(sc - jnp.max(sc, axis=-1, keepdims=True))
                    pr = (e * (1.0 / jnp.sum(e, axis=-1, keepdims=True))).astype(BF)
                    PSS[t][s, h * QT : (h + 1) * QT, :] = pr
                    out = out + nn(pr, vals * m)
                O[pl.ds(base + t * QT, QT), :] = out.astype(BF)
            return 0

        recv_a(WU, ucols, wur, peers)
        pass_on(WU, 1, "start")
        lax.fori_loop(0, 1, attn_step, 0)
        hand_on(DY, dss, drs, "start")
        lax.fori_loop(1, spc, attn_step, 0)

        pass_on(WU, 1, "wait_recv")
        relay_b(WD, nl, d_owner, rds, wdr, "start")

        def up_step(b, _):
            a = flat(A2[ga(b)])
            for j in range(fq // 256):
                cs = slice(j * 256, (j + 1) * 256)
                h = nn(a, flat(WU[:, :, :, cs])) + VEC[5, :, cs]
                g, sl = gelu_parts(h)
                GA[ga(b), :, cs] = g.astype(BF).reshape(R // uh, uh, 256)
                SL[b, :, cs] = sl.astype(BF)
            return 0

        lax.fori_loop(0, nb, up_step, 0)

        recv_b(WD, nl, d_owner, wdr, peers)
        pass_on(WD, 2, "start")
        recv_b(WO, no, o_owner, wor, direct)
        pass_on(WO, 3, "start")
        pass_on(WD, 2, "wait_recv")
        pass_on(WO, 3, "wait_recv")

        def yb(i):
            j = i + 1 - away
            return rot(e + 1 - rot(j // 2, 2), 2) * 2 + rot(j, 2)

        def give(k, lane, ss, rs, rlr, op):
            b = yb(k)
            src = YS.at[b]

            @pl.when(away == 0)
            def _():
                if k in (0, 3):
                    d = rcopy(src, YR.at[1], ss.at[k], rs.at[1], (p1, z * 0 + (1 if k == 0 else 0), z))
                    getattr(d, op)()
                else:

                    @pl.when(c == k - 1)
                    def _():
                        if op == "start":
                            lcopy(src, YR.at[0], rs.at[0]).start()

                    @pl.when(c != k - 1)
                    def _():
                        getattr(rcopy(src, YR.at[0], ss.at[k], rs.at[0], sib), op)()

            @pl.when(away == 1)
            def _():
                if k < 2:
                    d = rcopy(src, RL.at[lane], ss.at[k], rlr.at[lane], ((p2, p1)[k], c, z))
                else:
                    d = rcopy(src, YR.at[2], ss.at[k], rs.at[2], (p2, z * 0 + k - 2, z))
                getattr(d, op)()

        def add_on(lane, ss, rs, rlr):
            rcopy(RL.at[lane], RL.at[lane], xss.at[0], rlr.at[lane], sib).wait_recv()
            b = yb(3)

            def part(k, _):
                rc = pl.ds(mult(k * RC, RC), RC)
                YS[b, rc, :] = (YS[b, rc, :].astype(F32) + RL[lane, rc, :].astype(F32)).astype(BF)
                return 0

            lax.fori_loop(0, R // RC, part, 0)
            give(3, lane, ss, rs, rlr, "start")

        def y_step(i, _):
            b = yb(i)
            for j in range(D // 256):
                cs = slice(j * 256, (j + 1) * 256)
                y = nn(flat(GA[ga(b)]), flat(WD[:, :, :, cs])) + nn(
                    O[rows(b), :], flat(WO[:, :, :, cs])
                )
                YS[b, :, cs] = y.astype(BF)
            for k in range(3):

                @pl.when(i == k)
                def _():
                    give(k, 0, yss, yrs, rlr, "start")

            return 0

        lax.fori_loop(0, nb, y_step, 0)

        def dh_step(i, _):
            b = blk(i)
            got_other(DY, drs, b)
            dy = DY[b]
            for j in range(fq // 256):
                cs = slice(j * 256, (j + 1) * 256)
                k = 256 // G_
                dg = nt(dy, flat(WD[j * k : (j + 1) * k]))
                dh = (dg * SL[b, :, cs].astype(F32)).astype(BF)
                SL[b, :, cs] = dh
                UBA[:, cs] += jnp.sum(dh.astype(F32), axis=0, keepdims=True)
            DO[rows(b), :] = nt(dy, flat(WO[...])).astype(BF)
            part = DY[b, :, pl.ds(mult(p * hq, 128), hq)]
            DYA[...] += jnp.sum(part.astype(F32), axis=0, keepdims=True)
            return 0

        lax.fori_loop(0, nb, dh_step, 0)

        def grad(left, right, dst, rows_, cols_, tm, tc, half):
            for a in range(rows_ // tm):
                for b in range(cols_ // tc):
                    v = tn(left(a * tm, tm), right(b * tc, tc)).astype(BF)
                    k = tm // (2 * half)
                    dst[a * k : (a + 1) * k, :, :, b * tc : (b + 1) * tc] = v.reshape(
                        k, 2, half, tc
                    )

        grad(lambda o, w: flat(GA[:, :, o : o + w]), lambda o, w: flat(DY[:, :, o : o + w]),
             GD, fq, D, 512, 512, gh)

        def swap(src, dst, k, op):
            getattr(rcopy(src.at[:, 1 - c], dst, gds.at[k], gdr.at[k], sib), op)()

        swap(GD, RD, 0, "start")
        grad(lambda o, w: flat(A2[:, :, o : o + w]), lambda o, w: flat(SL[:, :, o : o + w]),
             GU, D, fq, 512, 512, uh)
        swap(GU, RU, 1, "start")
        for i in range(1, n):
            pl.semaphore_signal(
                zfree, inc=1, device_id=(p, c, rot(z + i, n)), device_id_type=MESH
            )

        def attn_back(s, _):
            base = mult(s * L, L)
            DKA[...] = jnp.zeros(DKA.shape, F32)
            DVA[...] = jnp.zeros(DVA.shape, F32)
            for t in range(nqt):
                ext = (t + 1) * QT
                qr = pl.ds(base + t * QT, QT)
                q = QKV[qr, 0:hq]
                keys = QKV[pl.ds(base, ext), hq : 2 * hq]
                vals = QKV[pl.ds(base, ext), 2 * hq : 3 * hq]
                do = DO[qr, :]
                dq = jnp.zeros((QT, hq), F32)
                for h in range(heads):
                    m = head_mask(h)
                    hs = slice(h * QT, (h + 1) * QT)
                    pr = PSS[t][s, hs, :].astype(F32)
                    dpr = nt(do * m, vals)
                    ds = (pr * (dpr - jnp.sum(pr * dpr, axis=-1, keepdims=True))).astype(BF)
                    GQ[h * kq : (h + 1) * kq, :, :, 0:ext] = ds.reshape(kq, 2, uh, ext)
                    dq = dq + nn(ds, keys * m)
                qs = jnp.concatenate([q * head_mask(h) for h in range(heads)], axis=0)
                dos = jnp.concatenate([do * head_mask(h) for h in range(heads)], axis=0)
                for k in range(t + 1):
                    ks = slice(k * QT, (k + 1) * QT)
                    DKA[ks, :] += tn(flat(GQ[:, :, :, ks]), qs)
                    DVA[ks, :] += tn(PSS[t][s, :, ks], dos)
                dqr = turn(dq * scale, t * QT, -1).astype(BF)
                QKV[qr, 0:hq] = dqr
                QBA[:, 0:hq] += jnp.sum(dqr.astype(F32), axis=0, keepdims=True)
            for t in range(nqt):
                kr = pl.ds(base + t * QT, QT)
                ts = slice(t * QT, (t + 1) * QT)
                dk = turn(DKA[ts, :], t * QT, -1).astype(BF)
                dv = DVA[ts, :].astype(BF)
                QKV[kr, hq : 2 * hq] = dk
                QKV[kr, 2 * hq : 3 * hq] = dv
                QBA[:, hq : 2 * hq] += jnp.sum(dk.astype(F32), axis=0, keepdims=True)
                QBA[:, 2 * hq : 3 * hq] += jnp.sum(dv.astype(F32), axis=0, keepdims=True)
            return 0

        def add_half(dst, src, k, pieces):
            rcopy(src, src, gds.at[k], gdr.at[k], sib).wait_recv()

            def one(i, _):
                dst[i, c] = (dst[i, c].astype(F32) + src[i].astype(F32)).astype(BF)
                return 0

            lax.fori_loop(0, pieces, one, 0)

        def line_a(src, Z, ss, rs, op):
            for i in range(1, n):
                to = rot(z + i, n)
                d = rcopy(src.at[to, c], Z.at[n - 1 - i], ss.at[i], rs.at[n - 1 - i], (p, c, to))
                getattr(d, op)()

        def line_b(src, Z, pieces, owner, ss, rs, op):
            for k in range(pieces):

                @pl.when(owner(k) != z)
                def _():
                    slot = rot(z - owner(k) - 1 + n, n)
                    d = rcopy(src.at[k, c], Z.at[slot], ss.at[k], rs.at[slot], (p, c, owner(k)))
                    getattr(d, op)()

        def line_sum(own, Z, F, rs):
            for i in range(n - 1):
                rcopy(Z.at[i], Z.at[i], xss.at[0], rs.at[i], sib).wait_recv()
            F[...] = (own().astype(F32) + sum_of(Z)).astype(BF)

        def sum_of(Z):
            acc = Z[0].astype(F32)
            for i in range(1, n - 1):
                acc = acc + Z[i].astype(F32)
            return acc

        def line_sum_b(src, Z, F, pieces, owner, rs, then):
            for k in range(pieces):

                @pl.when(owner(k) == z)
                def _():
                    line_sum(lambda: src[k, c], Z, F, rs)

            then("start")

        half_rows = pl.ds(mult(c * uh, uh), uh)
        per = ffs // G_
        o_who = (z * u) // hq
        dcols = [(0, D // 2), (D // 2, D // 2)]

        class Share:
            def __init__(self, F, place, parts, ss, rs, base, has):
                self.F, self.place, self.parts, self.ss, self.rs = F, place, parts, ss, rs
                self.base, self.has = base, has

            def when(self, w, f):
                if self.has is None:
                    f()
                else:
                    pl.when(self.has(w))(f)

            def own(self, op):
                def f():
                    for k, (o, w) in enumerate(self.parts):
                        s, t = self.F.at[:, pl.ds(o, w)], self.place(p, k)
                        for i, q in enumerate((p1, p2)):
                            d = rcopy(s, t, self.ss.at[i, k], self.rs.at[i, k], (q, c, z))
                            getattr(d, op)()
                        ld = lcopy(s, t, loc.at[self.base + k])
                        if op == "start":
                            ld.start()
                        else:
                            ld.wait()

                self.when(p, f)

            def relay(self, op):
                for i, (q, to) in enumerate(((p1, p2), (p2, p1))):

                    def f():
                        for k in range(len(self.parts)):
                            t = self.place(q, k)
                            if op == "start":
                                rcopy(t, t, xss.at[0], self.rs.at[i, k], sib).wait_recv()
                            if k % 2 == i:
                                d = rcopy(t, t, self.ss.at[2, k], self.rs.at[2, k], (to, c, z))
                                getattr(d, op)()

                    self.when(q, f)

            def last(self):
                def f():
                    for k in range(len(self.parts)):
                        t = self.place(p3, k)
                        rcopy(t, t, xss.at[0], self.rs.at[2, k], sib).wait_recv()

                self.when(p3, f)

        def slot_of(w):
            return rot(w + dp * n * per - z * per, dp)

        sq = Share(
            FQ,
            lambda w, k: gq_h.at[half_rows, pl.ds(mult(k * D + w * hq, 128), hq)],
            [(j * hq, hq) for j in range(3)], pqs, pqr, 1, None,
        )
        su = Share(
            FU,
            lambda w, k: gu_h.at[half_rows, pl.ds(mult((k * dp + w) * G_, 128), G_)],
            [(j * G_, G_) for j in range(nl)], pus, pur, 4, None,
        )
        sd = Share(
            FD,
            lambda w, k: gd_h.at[
                pl.ds(mult(slot_of(w) * G_ + c * gh, gh), gh), pl.ds(dcols[k][0], dcols[k][1])
            ],
            dcols, pds, pdr, 4 + nl, None if per >= dp else (lambda w: slot_of(w) < per),
        )
        so = Share(
            FO, lambda w, k: go_h.at[half_rows, pl.ds(dcols[k][0], dcols[k][1])],
            dcols, pos, por, 6 + nl, lambda w: o_who == w,
        )

        def shard_on(dst, k, op):
            r = half_rows if op != "wait_recv" else pl.ds(mult((1 - c) * uh, uh), uh)
            getattr(rcopy(dst.at[r], dst.at[r], pfs.at[k], pfr.at[k], sib), op)()

        def d_on(op):
            for i in range(per):
                side = c if op != "wait_recv" else 1 - c
                t = gd_h.at[pl.ds(mult(i * G_ + side * gh, gh), gh)]
                getattr(rcopy(t, t, pfs.at[3 + i], pfr.at[3 + i], sib), op)()

        def done(sh, on):
            sh.last()
            sh.own("wait_send")
            sh.relay("wait_send")
            on()

        add_half(GD, RD, 0, nl)
        pl.semaphore_wait(zfree, n - 1)
        line_b(GD, ZD, nl, d_owner, zds, zdr, "start")
        add_on(0, yss, yrs, rlr)
        add_half(GU, RU, 1, n)
        line_a(GU, ZU, zus, zur, "start")
        lax.fori_loop(0, 1, attn_back, 0)

        lcopy(x_h, XO, loc.at[0]).start()
        for q in range(3):
            rcopy(YR.at[q], YR.at[q], xss.at[0], yrs.at[q], sib).wait_recv()
        lcopy(x_h, XO, loc.at[0]).wait()

        def out_part(k, _):
            rc = pl.ds(mult(k * RC, RC), RC)
            acc = XO[rc, :].astype(F32) + VEC[4]
            for q in range(3):
                acc = acc + YR[q, rc, :].astype(F32)
            YO[rc, :] = acc.astype(BF)
            return 0

        lax.fori_loop(0, R // RC, out_part, 0)
        lcopy(YO, yo_h, loc.at[9 + nl]).start()

        @pl.when(home == c)
        def _():
            pl.semaphore_signal(yfree, inc=1)

        @pl.when(home != c)
        def _():
            pl.semaphore_signal(yfree, inc=1, device_id=sib, device_id_type=MESH)

        for q in (p1, p2):
            pl.semaphore_signal(yfree, inc=1, device_id=(q, home, z), device_id_type=MESH)

        lax.fori_loop(1, spc, attn_back, 0)
        for k in range(nb):
            give(k, 0, yss, yrs, rlr, "wait_send")
        hand_on(X, xss, xrs, "wait_send")
        line_sum_b(GD, ZD, FD, nl, d_owner, zdr, sd.own)

        def dz_step(i, _):
            b = yb(i)

            def part(q, _):
                rc = pl.ds(mult(q * RC, RC), RC)
                cen, rstd = stats(X[b, rc, :].astype(F32))
                X[b, rc, :] = (cen * rstd).astype(BF)
                return 0

            lax.fori_loop(0, R // RC, part, 0)
            k = 256 // u if u <= 256 else 1
            for j in range(D // 256):
                cs = slice(j * 256, (j + 1) * 256)
                xh = X[b, :, cs].astype(F32)
                d1 = nt(QKV[rows(b), :], flat(WQ[j * k : (j + 1) * k]))
                d2 = nt(SL[b], flat(WU[j * k : (j + 1) * k]))
                LNA[0, :, cs] += jnp.sum(d1 * xh, axis=0, keepdims=True)
                LNA[1, :, cs] += jnp.sum(d1, axis=0, keepdims=True)
                LNA[2, :, cs] += jnp.sum(d2 * xh, axis=0, keepdims=True)
                LNA[3, :, cs] += jnp.sum(d2, axis=0, keepdims=True)
                YS[b, :, cs] = (d1 * VEC[0, :, cs] + d2 * VEC[2, :, cs]).astype(BF)
            for k in range(3):

                @pl.when(i == k)
                def _():
                    give(k, 1, zss, zrs, rlr, "start")

            return 0

        pl.semaphore_wait(yfree, nb - 2 * away)
        lax.fori_loop(0, 2, dz_step, 0)
        sd.relay("start")
        line_sum(lambda: GU[z, c], ZU, FU, zur)
        su.own("start")
        lax.fori_loop(2, nb, dz_step, 0)

        tfl = slice(None)
        grad(lambda o, w: O[tfl, o : o + w], lambda o, w: flat(DY[:, :, o : o + w]),
             GO, hq, D, 256, 512, uh)
        swap(GO, RO, 2, "start")
        grad(lambda o, w: flat(A1[:, :, o : o + w]), lambda o, w: QKV[tfl, o : o + w],
             GQ, D, 3 * hq, 512, 256, uh)
        swap(GQ, RQ, 3, "start")
        add_on(1, zss, zrs, rlr)
        add_half(GO, RO, 2, no)
        line_b(GO, ZO, no, o_owner, zos, zor, "start")
        add_half(GQ, RQ, 3, n)
        line_a(GQ, ZQ, zqs, zqr, "start")

        for r in range(4):
            v = LNA[r]
            for k in range(n):
                SG[k, r] = v[:, k * u : (k + 1) * u]
        v = QBA[...]
        for j in range(3):
            for i in range(no):
                unit = (j * D + p * hq) // u + i
                SG[unit // 3, 4 + rot(unit, 3)] = v[:, j * hq + i * u : j * hq + (i + 1) * u]
        v = DYA[...]
        for i in range(no):
            SG[p * no + i, 7] = v[:, i * u : (i + 1) * u]
            SG[p * no + i, 12] = v[:, i * u : (i + 1) * u]
        v = UBA[...]
        for k in range(nl):
            for i in range(G_ // u):
                unit = ((k * dp + p) * G_) // u + i
                o = k * G_ + i * u
                SG[unit // (ffs // u), 8 + rot(unit, ffs // u)] = v[:, o : o + u]
        rcopy(SG, RSG, sgs, sgr, sib).start()

        lcopy(dy_h, A1.at[1], loc.at[8 + nl]).start()
        done(sd, lambda: d_on("start"))
        su.relay("start")

        rcopy(SG, RSG, sgs, sgr, sib).wait()
        SG[...] = SG[...] + RSG[...]

        def line_s(op):
            for i in range(1, n):
                to = rot(z + i, n)
                d = rcopy(SG.at[to], ZSG.at[n - 1 - i], zsgs.at[i], zsgr.at[n - 1 - i], (p, c, to))
                getattr(d, op)()

        line_s("start")
        done(su, lambda: shard_on(gu_h, 1, "start"))

        line_sum_b(GO, ZO, FO, no, o_owner, zor, so.own)
        line_sum(lambda: GQ[z, c], ZQ, FQ, zqr)
        sq.own("start")

        for i in range(n - 1):
            rcopy(ZSG.at[i], ZSG.at[i], xss.at[0], zsgr.at[i], sib).wait_recv()
        FSG[...] = SG[z] + sum_of(ZSG)

        def plane_s(op):
            for i in range(1, dp):
                to = (rot(p + i, dp), c, z)
                getattr(rcopy(FSG, PSG.at[dp - 1 - i], psgs.at[i], psgr.at[dp - 1 - i], to), op)()

        plane_s("start")

        lcopy(dy_h, A1.at[1], loc.at[8 + nl]).wait()
        for q in range(3):
            rcopy(YR.at[q], YR.at[q], xss.at[0], zrs.at[q], sib).wait_recv()

        def token_grad(k, _):
            rc = pl.ds(mult(k * RC, RC), RC)
            cen, rstd = stats(XO[rc, :].astype(F32))
            xh = cen * rstd
            tot = YR[0, rc, :].astype(F32)
            for q in range(1, 3):
                tot = tot + YR[q, rc, :].astype(F32)
            m1 = jnp.mean(tot, axis=-1, keepdims=True)
            m2 = jnp.mean(tot * xh, axis=-1, keepdims=True)
            A1[3, rc, :] = (A1[1, rc, :].astype(F32) + rstd * (tot - m1 - xh * m2)).astype(BF)
            return 0

        lax.fori_loop(0, R // RC, token_grad, 0)
        lcopy(A1.at[3], dxo_h, loc.at[0]).start()

        so.relay("start")
        sq.relay("start")
        for i in range(dp - 1):
            rcopy(PSG.at[i], PSG.at[i], xss.at[0], psgr.at[i], sib).wait_recv()
        acc = FSG[...]
        for i in range(dp - 1):
            acc = acc + PSG[i]
        SM[...] = acc
        lcopy(SM, gs_h, loc.at[8 + nl]).start()
        done(so, lambda: shard_on(go_h, 2, "start"))
        done(sq, lambda: shard_on(gq_h, 0, "start"))

        for k in range(3):
            shard_on((gq_h, gu_h, go_h)[k], k, "wait_recv")
            shard_on((gq_h, gu_h, go_h)[k], k, "wait_send")
        d_on("wait_recv")
        d_on("wait_send")
        small("wait_send")
        send_a(wq_h, WQ, qcols, wqs, wqr, direct, "wait_send")
        send_a(wu_h, WU, ucols, wus, wur, peers, "wait_send")
        relay_a(WU, ucols, rus, wur, "wait_send")
        send_b(wd_h, WD, nl, d_owner, d_row, gh, wds, wdr, peers, "wait_send")
        relay_b(WD, nl, d_owner, rds, wdr, "wait_send")
        send_b(wo_h, WO, no, o_owner, o_row, uh, wos, wor, direct, "wait_send")
        for k, W in enumerate((WQ, WU, WD, WO)):
            pass_on(W, k, "wait_send")
        spread(dy_h, DY, dss, drs, "wait_send")
        hand_on(DY, dss, drs, "wait_send")
        for k, (s, d) in enumerate(((GD, RD), (GU, RU), (GO, RO), (GQ, RQ))):
            swap(s, d, k, "wait_send")
        line_b(GD, ZD, nl, d_owner, zds, zdr, "wait_send")
        line_a(GU, ZU, zus, zur, "wait_send")
        line_b(GO, ZO, no, o_owner, zos, zor, "wait_send")
        line_a(GQ, ZQ, zqs, zqr, "wait_send")
        line_s("wait_send")
        plane_s("wait_send")

        for k in range(nb):
            give(k, 1, zss, zrs, rlr, "wait_send")
        lcopy(YO, yo_h, loc.at[9 + nl]).wait()
        lcopy(A1.at[3], dxo_h, loc.at[0]).wait()
        lcopy(SM, gs_h, loc.at[8 + nl]).wait()

    return kernel


def tables(length):
    freq = (np.float32(10000.0) ** (-(np.arange(ROT // 2) * 2).astype(np.float32) / ROT)).astype(
        np.float32
    )
    ang = np.arange(length, dtype=np.float32)[:, None] * freq[None, :]
    co, si = np.cos(ang).astype(np.float32), np.sin(ang).astype(np.float32)
    half = ROT // 2
    ct = np.ones((length, HD), np.float32)
    st = np.zeros((length, HD), np.float32)
    ct[:, :half], ct[:, half:ROT] = co, co
    st[:, :half], st[:, half:ROT] = -si, si
    return tuple(np.concatenate([t, t], axis=1) for t in (ct, st))


def body(mesh, tokens, cotangent, ln1_gain, ln1_bias, ln2_gain, ln2_bias, qkv_weight, qkv_bias,
         out_weight, out_bias, up_weight, up_bias, down_weight, down_bias):
    pn = Plan(mesh, tokens, qkv_weight, up_weight, down_weight)
    n, D, R, u, ffs, hq, fq, dp = pn.n, pn.D, pn.R, pn.u, pn.ffs, pn.hq, pn.fq, pn.dp
    G_, nl, no, nb, T, L, spc = pn.g, pn.nl, pn.no, pn.nb, pn.T, pn.L, pn.spc
    uh, gh = u // 2, G_ // 2
    small, at = None, 0
    for v in (ln1_gain, ln1_bias, ln2_gain, ln2_bias, qkv_bias, out_bias, up_bias, down_bias):
        w = jnp.pad(v, (at, NSMALL * u - at - v.shape[0])).astype(F32)
        small, at = w if small is None else small + w, at + v.shape[0]
    small = small.reshape(NSMALL, 1, u)
    ct, st = tables(L)
    vm = lambda *s, t=BF: pltpu.VMEM(s, t)
    dma = lambda *s: pltpu.SemaphoreType.DMA(s)
    scratch = [
        vm(nb, R, D), vm(nb, R, D), vm(nb, R, D), vm(T // uh, uh, D),
        vm(n, 2, uh, 3 * hq), vm(n, 2, uh, fq), vm(nl, 2, gh, D), vm(no, 2, uh, D),
        vm(T, 3 * hq), vm(T, hq), vm(T, hq),
        vm(spc, pn.heads * QT, QT), vm(spc, pn.heads * QT, 2 * QT), vm(spc, pn.heads * QT, 3 * QT),
        vm(T // uh, uh, fq), vm(nb, R, fq), vm(nb, R, D), vm(3, R, D), vm(2, R, D), vm(R, D), vm(R, D),
        vm(n, 2, uh, 3 * hq), vm(n, 2, uh, fq), vm(nl, 2, gh, D), vm(no, 2, uh, D),
        vm(n, uh, fq), vm(nl, gh, D),
        vm(n - 1, gh, D),
        vm(uh, fq), vm(gh, D),
        vm(NSMALL, 1, u, t=F32), vm(n, NSMALL, 1, u, t=F32), vm(7, 1, max(D, fq), t=F32),
        vm(n, NSMALL, 1, u, t=F32), vm(n, NSMALL, 1, u, t=F32), vm(n - 1, NSMALL, 1, u, t=F32),
        vm(NSMALL, 1, u, t=F32), vm(dp - 1, NSMALL, 1, u, t=F32),
        vm(4, 1, D, t=F32), vm(1, fq, t=F32), vm(1, 3 * hq, t=F32), vm(1, hq, t=F32),
        vm(L, hq, t=F32), vm(L, hq, t=F32),
        dma(dp), dma(nb), dma(dp), dma(nb), dma(n), dma(n),
        dma(n, 3), dma(n, 3), dma(n, nl), dma(n, nl), dma(n), dma(nl), dma(n), dma(no), dma(4), dma(4),
        dma(nb), dma(3), dma(nb), dma(3),
        dma(4), dma(4), dma(n), dma(n), dma(n), dma(n), dma(nl), dma(n), dma(no), dma(n),
        dma(3, 3), dma(3, 3), dma(3, nl), dma(3, nl), dma(3, 2), dma(3, 2), dma(3, 2), dma(3, 2),
        dma(3 + ffs // G_), dma(3 + ffs // G_),
        pltpu.SemaphoreType.DMA, pltpu.SemaphoreType.DMA, dma(n), dma(n), dma(dp), dma(dp), dma(10 + nl),
        pltpu.SemaphoreType.REGULAR, pltpu.SemaphoreType.REGULAR, dma(nl), dma(nl), dma(2),
    ]
    hbm = pl.BlockSpec(memory_space=pl.ANY)
    vmem = pl.BlockSpec(memory_space=pltpu.VMEM)
    sds = jax.ShapeDtypeStruct
    y, dx, gq, go, gu, gd, gs = pl.pallas_call(
        make_kernel(pn),
        out_shape=(
            sds((R, D), BF), sds((R, D), BF), sds((u, 3 * D), BF), sds((u, D), BF),
            sds((u, pn.FF), BF), sds((ffs, D), BF), sds((NSMALL, 1, u), F32),
        ),
        in_specs=[hbm] * 7 + [vmem] * 2,
        out_specs=[hbm] * 7,
        scratch_shapes=scratch,
        compiler_params=pltpu.CompilerParams(
            collective_id=0, has_side_effects=True, vmem_limit_bytes=63 * 2**20
        ),
    )(tokens[0], cotangent[0], small, qkv_weight, out_weight, up_weight, down_weight,
      jnp.asarray(ct), jnp.asarray(st))
    sv = gs.reshape(NSMALL * u)
    return (
        y[None], dx[None], sv[0:u], sv[u : 2 * u], sv[2 * u : 3 * u], sv[3 * u : 4 * u],
        gq.astype(F32), sv[4 * u : 7 * u], go.astype(F32), sv[7 * u : 8 * u],
        gu.astype(F32), sv[8 * u : 12 * u], gd.astype(F32), sv[12 * u : 13 * u],
    )


def solution(mesh):
    row = P(("dp", "fsdp"), "ctx", None)
    vec, mat = P("fsdp"), P("fsdp", None)
    in_specs = (row, row, vec, vec, vec, vec, mat, vec, mat, vec, mat, vec, mat, vec)
    out_specs = (row, row, vec, vec, vec, vec, mat, vec, mat, vec, mat, vec, mat, vec)
    return jax.shard_map(
        functools.partial(body, mesh), mesh=mesh, in_specs=in_specs, out_specs=out_specs, check_vma=False
    )
```

```python
import functools
import math

import jax
import jax.numpy as jnp
import numpy as np
from jax import lax
from jax.experimental import pallas as pl
from jax.experimental.pallas import tpu as pltpu
from jax.sharding import PartitionSpec as P

H = 16
HD = 64
ROT = 16
EPS = 1e-05
BF = jnp.bfloat16
F32 = jnp.float32
MESH = pl.DeviceIdType.MESH
QT = 256
NSMALL = 13


def nn(a, b):
    return lax.dot_general(a, b, (((1,), (0,)), ((), ())), preferred_element_type=F32)


def nt(a, b):
    return lax.dot_general(a, b, (((1,), (1,)), ((), ())), preferred_element_type=F32)


def tn(a, b):
    return lax.dot_general(a, b, (((0,), (0,)), ((), ())), preferred_element_type=F32)


def flat(v):
    return v.reshape(-1, v.shape[-1])


def rcopy(src, dst, ss, rs, dev):
    return pltpu.make_async_remote_copy(
        src_ref=src, dst_ref=dst, send_sem=ss, recv_sem=rs, device_id=dev, device_id_type=MESH
    )


def lcopy(src, dst, sem):
    return pltpu.make_async_copy(src, dst, sem)


def mult(v, m):
    return pl.multiple_of(v, m)


def stats(xf):
    mean = jnp.mean(xf, axis=-1, keepdims=True)
    cen = xf - mean
    var = jnp.mean(cen * cen, axis=-1, keepdims=True)
    return cen, lax.rsqrt(var + EPS)


def gelu_parts(h):
    a = jnp.abs(h)
    t = 1.0 / (1.0 + (0.3275911 * 0.5**0.5) * a)
    e = jnp.exp(-0.5 * h * h)
    poly = t * (
        0.127414796
        + t * (-0.142248368 + t * (0.7107068705 + t * (-0.7265760135 + t * 0.5307027145)))
    )
    tail = poly * e
    cum = jnp.where(h >= 0, 1.0 - tail, tail)
    return h * cum, cum + h * e * ((2.0 * math.pi) ** -0.5)


class Plan:
    def __init__(self, mesh, tokens, wqkv, wup, wdown):
        self.dp, self.ctx, self.n = mesh.shape["dp"], mesh.shape["ctx"], mesh.shape["fsdp"]
        self.D = tokens.shape[2]
        self.R = tokens.shape[1]
        self.L = self.R * self.ctx
        self.u = wqkv.shape[0]
        self.FF = wup.shape[1]
        self.ffs = wdown.shape[0]
        self.hq = self.D // self.dp
        self.fq = self.FF // self.dp
        self.g = max(128, self.ffs // self.dp)
        self.nl = self.fq // self.g
        self.no = self.hq // self.u
        self.heads = self.hq // HD
        self.spc = self.dp // self.ctx
        self.nb = self.spc * self.ctx
        self.T = self.nb * self.R


def make_kernel(pn):
    dp, n, D, R, u, ffs, hq, fq = pn.dp, pn.n, pn.D, pn.R, pn.u, pn.ffs, pn.hq, pn.fq
    G_, nl, no, heads, spc, nb, T, L = pn.g, pn.nl, pn.no, pn.heads, pn.spc, pn.nb, pn.T, pn.L
    uh, gh = u // 2, G_ // 2
    nqt = L // QT
    kq = QT // u
    RC = 128
    scale = HD**-0.5

    def kernel(
        x_h, dy_h, sm_h, wq_h, wo_h, wu_h, wd_h, cos_r, sin_r,
        yo_h, dxo_h, gq_h, go_h, gu_h, gd_h, gs_h,
        X, DY, A1, A2, WQ, WU, WD, WO, QKV, O, DO, PS0, PS1, PS2, GA, SL, YS, YR, RL, XO, YO,
        GQ, GU, GD, GO, RU, RD, ZD, FU, FD,
        SM, SB, VEC, SG, RSG, ZSG, FSG, PSG, LNA, UBA, QBA, DYA, DKA, DVA,
        xss, xrs, dss, drs, smss, smrs,
        wqs, wqr, wus, wur, wds, wdr, wos, wor, fws, fwr,
        yss, yrs, zss, zrs,
        gds, gdr, zqs, zqr, zus, zur, zds, zdr, zos, zor,
        pqs, pqr, pus, pur, pds, pdr, pos, por, pfs, pfr,
        sgs, sgr, zsgs, zsgr, psgs, psgr, loc, zfree, yfree, rus, rds, rlr, MD, mls, mlr,
    ):
        p = lax.axis_index("dp")
        c = lax.axis_index("ctx")
        z = lax.axis_index("fsdp")
        sib = (p, 1 - c, z)
        home = p // spc
        oblk = lax.rem(p, spc) * 2 + c
        e = lax.rem(p, 2)
        p1, p2, p3 = p + 1 - 2 * e, lax.rem(p + 2, 4), 3 - p
        away = home + c - 2 * home * c
        via, to_ = p1 + away * (p2 - p1), p2 + away * (p1 - p2)
        fblk = lax.rem(via, spc) * 2 + away
        PSS = (PS0, PS1, PS2)
        RQ, RO = GA.at[0:n, :, 0 : 3 * hq], GA.at[n : n + no]
        ZU, ZQ = A2.at[0 : n - 1], A2.at[n - 1 : 2 * n - 2, :, 0 : 3 * hq]
        ZO = A2.at[2 * n - 2 : 3 * n - 3]
        MU, MQ = A2.at[3 * n - 3], A2.at[3 * n - 2, :, 0 : 3 * hq]
        FQ, FO = GA.at[n + no, :, 0 : 3 * hq], GA.at[n + no + 1]

        def ga(b):
            return pl.ds(b * (R // uh), R // uh)

        def rot(v, k):
            return lax.rem(v, k)

        bar = pltpu.get_barrier_semaphore()
        partners = [sib]
        for i in range(1, dp):
            partners += [(rot(p + i, dp), 0, z), (rot(p + i, dp), 1, z)]
        for i in range(1, n):
            partners.append((p, c, rot(z + i, n)))
        for d in partners:
            pl.semaphore_signal(bar, inc=1, device_id=d, device_id_type=MESH)
        pl.semaphore_wait(bar, len(partners))

        def spread(src, buf, ss, rs, op):
            for i, q in ((1, p1), (2, p2)):
                getattr(rcopy(src, buf.at[oblk], ss.at[i], rs.at[oblk], (q, home, z)), op)()

            @pl.when(home == c)
            def _():
                if op == "start":
                    lcopy(src, buf.at[oblk], rs.at[oblk]).start()

            @pl.when(home != c)
            def _():
                getattr(rcopy(src, buf.at[oblk], ss.at[0], rs.at[oblk], sib), op)()

        def got(buf, rs, b):
            rcopy(buf.at[b], buf.at[b], xss.at[0], rs.at[b], sib).wait_recv()

        def hand_on(buf, ss, rs, op):
            if op == "start":
                got(buf, rs, fblk)
            d = rcopy(buf.at[fblk], buf.at[fblk], ss.at[3], rs.at[fblk], (to_, c, z))
            getattr(d, op)()

        def got_other(buf, rs, b):
            @pl.when(b != fblk)
            def _():
                got(buf, rs, b)

        def small(op):
            for i in range(1, n):
                d = rcopy(sm_h, SB.at[z], smss.at[i], smrs.at[z], (p, c, rot(z + i, n)))
                getattr(d, op)()

        qcols = [(mult(j * D + p * hq, 128), j * hq, hq) for j in range(3)]
        ucols = [(mult((k * dp + p) * G_, 128), k * G_, G_) for k in range(nl)]

        def d_owner(k):
            return ((k * dp + p) * G_) // ffs

        def d_row(k):
            return rot((k * dp + p) * G_, ffs)

        def o_owner(k):
            return p * no + k

        def o_row(k):
            return 0

        far = n >= 4

        def peers(send):
            for i in range(1, n):
                if far and i == 1:
                    pl.when(z != n - 1)(functools.partial(send, i))
                elif far and i == n - 1:
                    pl.when(z != 0)(functools.partial(send, i))
                else:
                    send(i)

        def direct(send):
            for i in range(1, n):
                send(i)

        def send_a(src, W, cols, ss, rs, each, op):
            for k, (sc, dc, w) in enumerate(cols):
                s = src.at[pl.ds(mult(c * uh, uh), uh), pl.ds(sc, w)]
                t = W.at[z, c, :, pl.ds(dc, w)]
                each(
                    lambda i: getattr(
                        rcopy(s, t, ss.at[i, k], rs.at[z, k], (p, c, rot(z + i, n))), op
                    )()
                )
                if op == "start":
                    lcopy(s, t, rs.at[z, k]).start()

        def send_b(src, W, pieces, owner, row, half, ss, rs, each, op):
            for k in range(pieces):

                @pl.when(owner(k) == z)
                def _():
                    s = src.at[pl.ds(mult(row(k) + c * half, half), half)]
                    each(
                        lambda i: getattr(
                            rcopy(s, W.at[k, c], ss.at[i], rs.at[k], (p, c, rot(z + i, n))), op
                        )()
                    )
                    if op == "start":
                        lcopy(s, W.at[k, c], rs.at[k]).start()

        def part_wait(W, k, dc, w, sem):
            t = W.at[k, c, :, pl.ds(dc, w)]
            rcopy(t, t, xss.at[0], sem, sib).wait_recv()

        def recv_a(W, cols, rs, each):
            for k in range(n):

                def one():
                    for j, (_, dc, w) in enumerate(cols):
                        part_wait(W, k, dc, w, rs.at[k, j])

                if far and each is peers and k == 0:
                    pl.when(z != n - 2)(one)
                elif far and each is peers and k == n - 1:
                    pl.when(z != 1)(one)
                else:
                    one()

        def relay_a(W, cols, ss, rs, op):
            if far:
                for at, k, to in ((1, n - 1, 0), (n - 2, 0, n - 1)):

                    @pl.when(z == at)
                    def _():
                        for j, (_, dc, w) in enumerate(cols):
                            if op == "start":
                                part_wait(W, k, dc, w, rs.at[k, j])
                            t = W.at[k, c, :, pl.ds(dc, w)]
                            getattr(rcopy(t, t, ss.at[j], rs.at[k, j], (p, c, to)), op)()

        def recv_b(W, pieces, owner, rs, each):
            for k in range(pieces):

                def one():
                    rcopy(W.at[k, c], W.at[k, c], xss.at[0], rs.at[k], sib).wait_recv()

                if far and each is peers:
                    first = jnp.logical_and(owner(k) == n - 1, z == 1)
                    last = jnp.logical_and(owner(k) == 0, z == n - 2)
                    pl.when(jnp.logical_not(jnp.logical_or(first, last)))(one)
                else:
                    one()

        def relay_b(W, pieces, owner, ss, rs, op):
            if far:
                for k in range(pieces):
                    for at, o, to in ((1, n - 1, 0), (n - 2, 0, n - 1)):

                        @pl.when(jnp.logical_and(owner(k) == o, z == at))
                        def _():
                            t = W.at[k, c]
                            d = rcopy(t, t, ss.at[k], rs.at[k], (p, c, to))
                            if op == "start":
                                d.wait_recv()
                            getattr(d, op)()

        def pass_on(W, k, op):
            side = c if op != "wait_recv" else 1 - c
            getattr(rcopy(W.at[:, side], W.at[:, side], fws.at[k], fwr.at[k], sib), op)()

        lcopy(sm_h, SB.at[z], smrs.at[z]).start()
        spread(x_h, X, xss, xrs, "start")
        small("start")
        send_a(wq_h, WQ, qcols, wqs, wqr, direct, "start")

        for r in (LNA, UBA, QBA, DYA, SG):
            r[...] = jnp.zeros(r.shape, F32)

        for k in range(n):
            rcopy(SB.at[k], SB.at[k], xss.at[0], smrs.at[k], sib).wait_recv()
        for row, r in ((0, 0), (1, 1), (2, 2), (3, 3)):
            VEC[row] = jnp.concatenate([SB[k, r] for k in range(n)], axis=1)
        VEC[4] = jnp.concatenate([SB[k, 7] + SB[k, 12] for k in range(n)], axis=1)
        units = []
        for k in range(nl):
            for i in range(G_ // u if G_ >= u else 1):
                unit = ((k * dp + p) * G_) // u + i
                units.append(SB[unit // (ffs // u), 8 + rot(unit, ffs // u)])
        VEC[5] = jnp.concatenate(units, axis=1)
        for j in range(3):
            units = []
            for i in range(no):
                unit = (j * D + p * hq) // u + i
                units.append(SB[unit // 3, 4 + rot(unit, 3)])
            VEC[6, :, j * hq : (j + 1) * hq] = jnp.concatenate(units, axis=1)

        def blk(i):
            return rot(p + i // 2, spc) * 2 + rot(c + i, 2)

        def norm_step(i, _):
            b = blk(i)
            got_other(X, xrs, b)

            def part(k, _):
                rc = pl.ds(mult(k * RC, RC), RC)
                cen, rstd = stats(X[b, rc, :].astype(F32))
                xh = cen * rstd
                A1[b, rc, :] = (xh * VEC[0] + VEC[1]).astype(BF)
                A2[pl.ds((b * R + k * RC) // uh, RC // uh)] = (
                    (xh * VEC[2] + VEC[3]).astype(BF).reshape(RC // uh, uh, D)
                )
                return 0

            lax.fori_loop(0, R // RC, part, 0)
            return 0

        @pl.when(away == 1)
        def _():
            hand_on(X, xss, xrs, "start")

        lax.fori_loop(0, 2, norm_step, 0)
        recv_a(WQ, qcols, wqr, direct)
        pass_on(WQ, 0, "start")
        send_a(wu_h, WU, ucols, wus, wur, peers, "start")
        pass_on(WQ, 0, "wait_recv")

        def turn(v, r0, sign):
            out = []
            ct, st = cos_r[pl.ds(r0, v.shape[0]), :], sin_r[pl.ds(r0, v.shape[0]), :]
            first = lax.broadcasted_iota(jnp.int32, ct.shape, 1) % HD < ROT // 2
            for j in range(hq // 128):
                w = v[:, j * 128 : (j + 1) * 128]
                back = st * jnp.where(
                    first, pltpu.roll(w, 128 - ROT // 2, 1), pltpu.roll(w, ROT // 2, 1)
                )
                out.append(w * ct + (back if sign > 0 else -back))
            return jnp.concatenate(out, axis=1)

        def rows(b):
            return pl.ds(mult(b * R, R), R)

        def qkv_step(i, _):
            b = blk(i)
            a = A1[b]
            r0 = mult(rot(b, 2) * R, R)
            for j in range(3):
                w = flat(WQ[:, :, :, j * hq : (j + 1) * hq])
                f = nn(a, w) + VEC[6, :, j * hq : (j + 1) * hq]
                if j < 2:
                    f = turn(f, r0, 1)
                if j == 0:
                    f = f * scale
                QKV[rows(b), j * hq : (j + 1) * hq] = f.astype(BF)
            return 0

        lax.fori_loop(0, 2, qkv_step, 0)

        @pl.when(away == 0)
        def _():
            hand_on(X, xss, xrs, "start")

        def head_mask(h):
            lane = lax.broadcasted_iota(jnp.int32, (1, hq), 1)
            return ((lane // HD) == h).astype(F32).astype(BF)

        def attn_step(i, _):
            s = rot(e + i, spc)
            base = mult(s * L, L)
            for t in range(nqt):
                ext = (t + 1) * QT
                q = QKV[pl.ds(base + t * QT, QT), 0:hq]
                keys = QKV[pl.ds(base, ext), hq : 2 * hq]
                vals = QKV[pl.ds(base, ext), 2 * hq : 3 * hq]
                out = jnp.zeros((QT, hq), F32)
                below = lax.broadcasted_iota(jnp.int32, (QT, ext), 1) <= (
                    lax.broadcasted_iota(jnp.int32, (QT, ext), 0) + t * QT
                )
                for h in range(heads):
                    m = head_mask(h)
                    sc = jnp.where(below, nt(q * m, keys), -1e9)
                    ex = jnp.exp(sc - jnp.max(sc, axis=-1, keepdims=True))
                    pr = (ex * (1.0 / jnp.sum(ex, axis=-1, keepdims=True))).astype(BF)
                    PSS[t][s, h * QT : (h + 1) * QT, :] = pr
                    out = out + nn(pr, vals * m)
                O[pl.ds(base + t * QT, QT), :] = out.astype(BF)
            return 0

        lax.fori_loop(0, 1, attn_step, 0)
        spread(x_h, X, xss, xrs, "wait_send")
        hand_on(X, xss, xrs, "wait_send")
        spread(dy_h, DY, dss, drs, "start")
        relay_a(WU, ucols, rus, wur, "start")
        send_b(wd_h, WD, nl, d_owner, d_row, gh, wds, wdr, peers, "start")
        send_b(wo_h, WO, no, o_owner, o_row, uh, wos, wor, direct, "start")
        lax.fori_loop(2, nb, norm_step, 0)
        lax.fori_loop(2, nb, qkv_step, 0)
        recv_a(WU, ucols, wur, peers)
        pass_on(WU, 1, "start")
        lax.fori_loop(1, spc, attn_step, 0)

        pass_on(WU, 1, "wait_recv")
        relay_b(WD, nl, d_owner, rds, wdr, "start")

        def up_step(b, _):
            a = flat(A2[ga(b)])
            for j in range(fq // 256):
                cs = slice(j * 256, (j + 1) * 256)
                h = nn(a, flat(WU[:, :, :, cs])) + VEC[5, :, cs]
                g, sl = gelu_parts(h)
                GA[ga(b), :, cs] = g.astype(BF).reshape(R // uh, uh, 256)
                SL[b, :, cs] = sl.astype(BF)
            return 0

        lax.fori_loop(0, nb, up_step, 0)
        hand_on(DY, dss, drs, "start")

        recv_b(WD, nl, d_owner, wdr, peers)
        pass_on(WD, 2, "start")
        recv_b(WO, no, o_owner, wor, direct)
        pass_on(WO, 3, "start")
        pass_on(WD, 2, "wait_recv")
        pass_on(WO, 3, "wait_recv")

        def yb(i):
            s = e + away * (1 - i // 2) + (1 - away) * (i // 2)
            h = i + (1 - away) * (i // 2) + away * (1 - i // 2)
            return rot(s, 2) * 2 + rot(h, 2)

        def give(k, lane, ss, rs, rlr, op):
            b = yb(k)
            src = YS.at[b]

            @pl.when(away == 0)
            def _():
                if k >= 2:
                    d = rcopy(src, YR.at[1], ss.at[k], rs.at[1], (p1, z * 0 + 3 - k, z))
                    getattr(d, op)()
                else:

                    @pl.when(c == k)
                    def _():
                        if op == "start":
                            lcopy(src, YR.at[0], rs.at[0]).start()

                    @pl.when(c != k)
                    def _():
                        getattr(rcopy(src, YR.at[0], ss.at[k], rs.at[0], sib), op)()

            @pl.when(away == 1)
            def _():
                if k < 2:
                    d = rcopy(src, RL.at[lane], ss.at[k], rlr.at[lane], ((p1, p2)[k], c, z))
                else:
                    d = rcopy(src, YR.at[2], ss.at[k], rs.at[2], (p2, z * 0 + k - 2, z))
                getattr(d, op)()

        def add_on(lane, ss, rs, rlr):
            rcopy(RL.at[lane], RL.at[lane], xss.at[0], rlr.at[lane], sib).wait_recv()
            b = yb(3)

            def part(k, _):
                rc = pl.ds(mult(k * RC, RC), RC)
                YS[b, rc, :] = (YS[b, rc, :].astype(F32) + RL[lane, rc, :].astype(F32)).astype(BF)
                return 0

            lax.fori_loop(0, R // RC, part, 0)
            give(3, lane, ss, rs, rlr, "start")

        def y_step(i, _):
            b = yb(i)
            for j in range(D // 256):
                cs = slice(j * 256, (j + 1) * 256)
                y = nn(flat(GA[ga(b)]), flat(WD[:, :, :, cs])) + nn(
                    O[rows(b), :], flat(WO[:, :, :, cs])
                )
                YS[b, :, cs] = y.astype(BF)
            for k in range(3):

                @pl.when(i == k)
                def _():
                    give(k, 0, yss, yrs, rlr, "start")

            return 0

        lax.fori_loop(0, nb, y_step, 0)

        def dh_step(i, _):
            b = blk(i)
            got_other(DY, drs, b)
            dy = DY[b]
            for j in range(fq // 256):
                cs = slice(j * 256, (j + 1) * 256)
                k = 256 // G_
                dg = nt(dy, flat(WD[j * k : (j + 1) * k]))
                dh = (dg * SL[b, :, cs].astype(F32)).astype(BF)
                SL[b, :, cs] = dh
                UBA[:, cs] += jnp.sum(dh.astype(F32), axis=0, keepdims=True)
            DO[rows(b), :] = nt(dy, flat(WO[...])).astype(BF)
            part = DY[b, :, pl.ds(mult(p * hq, 128), hq)]
            DYA[...] += jnp.sum(part.astype(F32), axis=0, keepdims=True)
            return 0

        lax.fori_loop(0, nb, dh_step, 0)

        def grad(left, right, dst, rows_, cols_, tm, tc, half):
            for a in range(rows_ // tm):
                for b in range(cols_ // tc):
                    v = tn(left(a * tm, tm), right(b * tc, tc)).astype(BF)
                    k = tm // (2 * half)
                    dst[a * k : (a + 1) * k, :, :, b * tc : (b + 1) * tc] = v.reshape(
                        k, 2, half, tc
                    )

        grad(lambda o, w: flat(GA[:, :, o : o + w]), lambda o, w: flat(DY[:, :, o : o + w]),
             GD, fq, D, 512, 512, gh)

        def swap(src, dst, k, op):
            getattr(rcopy(src.at[:, 1 - c], dst, gds.at[k], gdr.at[k], sib), op)()

        swap(GD, RD, 0, "start")
        grad(lambda o, w: flat(A2[:, :, o : o + w]), lambda o, w: flat(SL[:, :, o : o + w]),
             GU, D, fq, 512, 512, uh)
        swap(GU, RU, 1, "start")
        for i in range(1, n):
            pl.semaphore_signal(
                zfree, inc=1, device_id=(p, c, rot(z + i, n)), device_id_type=MESH
            )

        def attn_back(s, _):
            base = mult(s * L, L)
            DKA[...] = jnp.zeros(DKA.shape, F32)
            DVA[...] = jnp.zeros(DVA.shape, F32)
            for t in range(nqt):
                ext = (t + 1) * QT
                qr = pl.ds(base + t * QT, QT)
                q = QKV[qr, 0:hq]
                keys = QKV[pl.ds(base, ext), hq : 2 * hq]
                vals = QKV[pl.ds(base, ext), 2 * hq : 3 * hq]
                do = DO[qr, :]
                dq = jnp.zeros((QT, hq), F32)
                for h in range(heads):
                    m = head_mask(h)
                    hs = slice(h * QT, (h + 1) * QT)
                    pr = PSS[t][s, hs, :].astype(F32)
                    dpr = nt(do * m, vals)
                    ds = (pr * (dpr - jnp.sum(pr * dpr, axis=-1, keepdims=True))).astype(BF)
                    GQ[h * kq : (h + 1) * kq, :, :, 0:ext] = ds.reshape(kq, 2, uh, ext)
                    dq = dq + nn(ds, keys * m)
                qs = jnp.concatenate([q * head_mask(h) for h in range(heads)], axis=0)
                dos = jnp.concatenate([do * head_mask(h) for h in range(heads)], axis=0)
                for k in range(t + 1):
                    ks = slice(k * QT, (k + 1) * QT)
                    DKA[ks, :] += tn(flat(GQ[:, :, :, ks]), qs)
                    DVA[ks, :] += tn(PSS[t][s, :, ks], dos)
                dqr = turn(dq * scale, t * QT, -1).astype(BF)
                QKV[qr, 0:hq] = dqr
                QBA[:, 0:hq] += jnp.sum(dqr.astype(F32), axis=0, keepdims=True)
            for t in range(nqt):
                kr = pl.ds(base + t * QT, QT)
                ts = slice(t * QT, (t + 1) * QT)
                dk = turn(DKA[ts, :], t * QT, -1).astype(BF)
                dv = DVA[ts, :].astype(BF)
                QKV[kr, hq : 2 * hq] = dk
                QKV[kr, 2 * hq : 3 * hq] = dv
                QBA[:, hq : 2 * hq] += jnp.sum(dk.astype(F32), axis=0, keepdims=True)
                QBA[:, 2 * hq : 3 * hq] += jnp.sum(dv.astype(F32), axis=0, keepdims=True)
            return 0

        def add_half(dst, src, k, pieces):
            rcopy(src, src, gds.at[k], gdr.at[k], sib).wait_recv()

            def one(i, _):
                dst[i, c] = (dst[i, c].astype(F32) + src[i].astype(F32)).astype(BF)
                return 0

            lax.fori_loop(0, pieces, one, 0)

        def line_a(src, Z, M, ss, rs, ms, mr, op):
            def send(to, dst, sem, got_sem, dev):
                getattr(rcopy(src.at[to, c], dst, sem, got_sem, (p, c, dev)), op)()

            if far:
                for at, end, by in ((0, n - 1, 1), (n - 1, 0, n - 2)):

                    @pl.when(z == at)
                    def _():
                        send(end, M, ms, mr, by)

            for i in range(1, n):
                to = rot(z + i, n)

                def one():
                    send(to, Z.at[n - 1 - i], ss.at[i], rs.at[n - 1 - i], to)

                pl.when(jnp.logical_not(later(to)))(one) if far else one()

        def later(to):
            up = jnp.logical_and(to == n - 1, z < 2)
            return jnp.logical_or(up, jnp.logical_and(to == 0, z >= n - 2))

        def line_a_on(src, Z, M, ss, rs, ms, mr, op):
            if far:
                for at, end, i in ((1, n - 1, n - 2), (n - 2, 0, 2)):

                    @pl.when(z == at)
                    def _():
                        if op == "start":
                            rcopy(M, M, ms, mr, sib).wait_recv()
                            src[end, c] = (src[end, c].astype(F32) + M[...].astype(F32)).astype(BF)
                        d = rcopy(
                            src.at[end, c], Z.at[n - 1 - i], ss.at[i], rs.at[n - 1 - i], (p, c, end)
                        )
                        getattr(d, op)()

        def line_b(src, Z, M, pieces, owner, ss, rs, ms, mr, op):
            for k in range(pieces):
                o = owner(k)
                slot = rot(z - o - 1 + n, n)

                def one():
                    d = rcopy(src.at[k, c], Z.at[slot], ss.at[k], rs.at[slot], (p, c, o))
                    getattr(d, op)()

                pl.when(jnp.logical_not(jnp.logical_or(o == z, later(o) if M is not None else o < 0)))(one)
                if M is not None:
                    for at, end, by in ((0, n - 1, 1), (n - 1, 0, n - 2)):

                        @pl.when(jnp.logical_and(z == at, o == end))
                        def _():
                            getattr(rcopy(src.at[k, c], M, ms, mr, (p, c, by)), op)()

        def line_b_on(src, Z, M, pieces, owner, ss, rs, ms, mr, op):
            for k in range(pieces):
                o = owner(k)
                slot = rot(z - o - 1 + n, n)
                for at, end in ((1, n - 1), (n - 2, 0)):

                    @pl.when(jnp.logical_and(z == at, o == end))
                    def _():
                        if op == "start":
                            rcopy(M, M, ms, mr, sib).wait_recv()
                            src[k, c] = (src[k, c].astype(F32) + M[...].astype(F32)).astype(BF)
                        d = rcopy(src.at[k, c], Z.at[slot], ss.at[k], rs.at[slot], (p, c, o))
                        getattr(d, op)()

        def line_sum(own, Z, F, rs, thin=True):
            for i in range(n - 1):

                def one():
                    rcopy(Z.at[i], Z.at[i], xss.at[0], rs.at[i], sib).wait_recv()

                def none():
                    Z[i] = jnp.zeros(Z.shape[1:], BF)

                end = {0: n - 1, n - 2: 0}.get(i)
                if far and thin and end is not None:
                    pl.when(z != end)(one)
                    pl.when(z == end)(none)
                else:
                    one()
            F[...] = (own().astype(F32) + sum_of(Z)).astype(BF)

        def sum_of(Z):
            acc = Z[0].astype(F32)
            for i in range(1, n - 1):
                acc = acc + Z[i].astype(F32)
            return acc

        def line_sum_b(src, Z, F, pieces, owner, rs, then, thin):
            for k in range(pieces):

                @pl.when(owner(k) == z)
                def _():
                    line_sum(lambda: src[k, c], Z, F, rs, thin)

            then("start")

        half_rows = pl.ds(mult(c * uh, uh), uh)
        per = ffs // G_
        o_who = (z * u) // hq
        dcols = [(0, D // 2), (D // 2, D // 2)]

        class Share:
            def __init__(self, F, place, parts, ss, rs, base, has):
                self.F, self.place, self.parts, self.ss, self.rs = F, place, parts, ss, rs
                self.base, self.has = base, has

            def when(self, w, f):
                if self.has is None:
                    f()
                else:
                    pl.when(self.has(w))(f)

            def own(self, op):
                def f():
                    for k, (o, w) in enumerate(self.parts):
                        s, t = self.F.at[:, pl.ds(o, w)], self.place(p, k)
                        for i, q in enumerate((p1, p2)):
                            d = rcopy(s, t, self.ss.at[i, k], self.rs.at[i, k], (q, c, z))
                            getattr(d, op)()
                        ld = lcopy(s, t, loc.at[self.base + k])
                        if op == "start":
                            ld.start()
                        else:
                            ld.wait()

                self.when(p, f)

            def relay(self, op):
                for i, (q, to) in enumerate(((p1, p2), (p2, p1))):

                    def f():
                        for k in range(len(self.parts)):
                            t = self.place(q, k)
                            if op == "start":
                                rcopy(t, t, xss.at[0], self.rs.at[i, k], sib).wait_recv()
                            if k % 2 == i:
                                d = rcopy(t, t, self.ss.at[2, k], self.rs.at[2, k], (to, c, z))
                                getattr(d, op)()

                    self.when(q, f)

            def last(self):
                def f():
                    for k in range(len(self.parts)):
                        t = self.place(p3, k)
                        rcopy(t, t, xss.at[0], self.rs.at[2, k], sib).wait_recv()

                self.when(p3, f)

        def slot_of(w):
            return rot(w + dp * n * per - z * per, dp)

        sq = Share(
            FQ,
            lambda w, k: gq_h.at[half_rows, pl.ds(mult(k * D + w * hq, 128), hq)],
            [(j * hq, hq) for j in range(3)], pqs, pqr, 1, None,
        )
        su = Share(
            FU,
            lambda w, k: gu_h.at[half_rows, pl.ds(mult((k * dp + w) * G_, 128), G_)],
            [(j * G_, G_) for j in range(nl)], pus, pur, 4, None,
        )
        sd = Share(
            FD,
            lambda w, k: gd_h.at[
                pl.ds(mult(slot_of(w) * G_ + c * gh, gh), gh), pl.ds(dcols[k][0], dcols[k][1])
            ],
            dcols, pds, pdr, 4 + nl, None if per >= dp else (lambda w: slot_of(w) < per),
        )
        so = Share(
            FO, lambda w, k: go_h.at[half_rows, pl.ds(dcols[k][0], dcols[k][1])],
            dcols, pos, por, 6 + nl, lambda w: o_who == w,
        )

        def shard_on(dst, k, op):
            r = half_rows if op != "wait_recv" else pl.ds(mult((1 - c) * uh, uh), uh)
            getattr(rcopy(dst.at[r], dst.at[r], pfs.at[k], pfr.at[k], sib), op)()

        def d_on(op):
            for i in range(per):
                side = c if op != "wait_recv" else 1 - c
                t = gd_h.at[pl.ds(mult(i * G_ + side * gh, gh), gh)]
                getattr(rcopy(t, t, pfs.at[3 + i], pfr.at[3 + i], sib), op)()

        def done(sh, on):
            sh.last()
            sh.own("wait_send")
            sh.relay("wait_send")
            on()

        add_on(0, yss, yrs, rlr)
        add_half(GD, RD, 0, nl)
        pl.semaphore_wait(zfree, n - 1)
        gd_line = (GD, ZD, MD if far else None, nl, d_owner, zds, zdr, mls.at[0], mlr.at[0])
        gu_line = (GU, ZU, MU, zus, zur, mls.at[1], mlr.at[1])
        gq_line = (GQ, ZQ, MQ, zqs, zqr, mls.at[2], mlr.at[2])
        go_line = (GO, ZO, None, no, o_owner, zos, zor, None, None)
        line_b(*gd_line, "start")
        add_half(GU, RU, 1, n)
        line_a(*gu_line, "start")
        lax.fori_loop(0, 1, attn_back, 0)
        if far:
            line_b_on(*gd_line, "start")

        lcopy(x_h, XO, loc.at[0]).start()
        for q in range(3):
            rcopy(YR.at[q], YR.at[q], xss.at[0], yrs.at[q], sib).wait_recv()
        lcopy(x_h, XO, loc.at[0]).wait()

        def out_part(k, _):
            rc = pl.ds(mult(k * RC, RC), RC)
            acc = XO[rc, :].astype(F32) + VEC[4]
            for q in range(3):
                acc = acc + YR[q, rc, :].astype(F32)
            YO[rc, :] = acc.astype(BF)
            return 0

        lax.fori_loop(0, R // RC, out_part, 0)
        lcopy(YO, yo_h, loc.at[9 + nl]).start()

        @pl.when(home == c)
        def _():
            pl.semaphore_signal(yfree, inc=1)

        @pl.when(home != c)
        def _():
            pl.semaphore_signal(yfree, inc=1, device_id=sib, device_id_type=MESH)

        for q in (p1, p2):
            pl.semaphore_signal(yfree, inc=1, device_id=(q, home, z), device_id_type=MESH)

        lax.fori_loop(1, spc, attn_back, 0)
        line_a_on(*gu_line, "start")
        for k in range(nb):
            give(k, 0, yss, yrs, rlr, "wait_send")
        def dz_step(i, _):
            b = yb(i)

            def part(q, _):
                rc = pl.ds(mult(q * RC, RC), RC)
                cen, rstd = stats(X[b, rc, :].astype(F32))
                X[b, rc, :] = (cen * rstd).astype(BF)
                return 0

            lax.fori_loop(0, R // RC, part, 0)
            k = 256 // u if u <= 256 else 1
            for j in range(D // 256):
                cs = slice(j * 256, (j + 1) * 256)
                xh = X[b, :, cs].astype(F32)
                d1 = nt(QKV[rows(b), :], flat(WQ[j * k : (j + 1) * k]))
                d2 = nt(SL[b], flat(WU[j * k : (j + 1) * k]))
                LNA[0, :, cs] += jnp.sum(d1 * xh, axis=0, keepdims=True)
                LNA[1, :, cs] += jnp.sum(d1, axis=0, keepdims=True)
                LNA[2, :, cs] += jnp.sum(d2 * xh, axis=0, keepdims=True)
                LNA[3, :, cs] += jnp.sum(d2, axis=0, keepdims=True)
                YS[b, :, cs] = (d1 * VEC[0, :, cs] + d2 * VEC[2, :, cs]).astype(BF)
            for k in range(3):

                @pl.when(i == k)
                def _():
                    give(k, 1, zss, zrs, rlr, "start")

            return 0

        pl.semaphore_wait(yfree, nb - 2 * away)
        lax.fori_loop(0, 2, dz_step, 0)
        line_sum_b(GD, ZD, FD, nl, d_owner, zdr, sd.own, far)
        lax.fori_loop(2, nb, dz_step, 0)

        tfl = slice(None)
        grad(lambda o, w: O[tfl, o : o + w], lambda o, w: flat(DY[:, :, o : o + w]),
             GO, hq, D, 256, 512, uh)
        swap(GO, RO, 2, "start")
        grad(lambda o, w: flat(A1[:, :, o : o + w]), lambda o, w: QKV[tfl, o : o + w],
             GQ, D, 3 * hq, 512, 256, uh)
        swap(GQ, RQ, 3, "start")
        line_sum(lambda: GU[z, c], ZU, FU, zur)
        su.own("start")
        add_on(1, zss, zrs, rlr)
        add_half(GO, RO, 2, no)
        line_b(*go_line, "start")
        add_half(GQ, RQ, 3, n)
        line_a(*gq_line, "start")
        sd.relay("start")

        for r in range(4):
            v = LNA[r]
            for k in range(n):
                SG[k, r] = v[:, k * u : (k + 1) * u]
        v = QBA[...]
        for j in range(3):
            for i in range(no):
                unit = (j * D + p * hq) // u + i
                SG[unit // 3, 4 + rot(unit, 3)] = v[:, j * hq + i * u : j * hq + (i + 1) * u]
        v = DYA[...]
        for i in range(no):
            SG[p * no + i, 7] = v[:, i * u : (i + 1) * u]
            SG[p * no + i, 12] = v[:, i * u : (i + 1) * u]
        v = UBA[...]
        for k in range(nl):
            for i in range(G_ // u):
                unit = ((k * dp + p) * G_) // u + i
                o = k * G_ + i * u
                SG[unit // (ffs // u), 8 + rot(unit, ffs // u)] = v[:, o : o + u]
        rcopy(SG, RSG, sgs, sgr, sib).start()

        lcopy(dy_h, A1.at[1], loc.at[8 + nl]).start()
        line_a_on(*gq_line, "start")
        su.relay("start")

        rcopy(SG, RSG, sgs, sgr, sib).wait()
        SG[...] = SG[...] + RSG[...]

        def line_s(op):
            for i in range(1, n):
                to = rot(z + i, n)
                d = rcopy(SG.at[to], ZSG.at[n - 1 - i], zsgs.at[i], zsgr.at[n - 1 - i], (p, c, to))
                getattr(d, op)()

        line_s("start")
        line_sum_b(GO, ZO, FO, no, o_owner, zor, so.own, False)
        line_sum(lambda: GQ[z, c], ZQ, FQ, zqr)
        sq.own("start")
        done(sd, lambda: d_on("start"))
        done(su, lambda: shard_on(gu_h, 1, "start"))

        for i in range(n - 1):
            rcopy(ZSG.at[i], ZSG.at[i], xss.at[0], zsgr.at[i], sib).wait_recv()
        FSG[...] = SG[z] + sum_of(ZSG)

        def plane_s(op):
            for i in range(1, dp):
                to = (rot(p + i, dp), c, z)
                getattr(rcopy(FSG, PSG.at[dp - 1 - i], psgs.at[i], psgr.at[dp - 1 - i], to), op)()

        plane_s("start")

        lcopy(dy_h, A1.at[1], loc.at[8 + nl]).wait()
        for q in range(3):
            rcopy(YR.at[q], YR.at[q], xss.at[0], zrs.at[q], sib).wait_recv()

        def token_grad(k, _):
            rc = pl.ds(mult(k * RC, RC), RC)
            cen, rstd = stats(XO[rc, :].astype(F32))
            xh = cen * rstd
            tot = YR[0, rc, :].astype(F32)
            for q in range(1, 3):
                tot = tot + YR[q, rc, :].astype(F32)
            m1 = jnp.mean(tot, axis=-1, keepdims=True)
            m2 = jnp.mean(tot * xh, axis=-1, keepdims=True)
            A1[3, rc, :] = (A1[1, rc, :].astype(F32) + rstd * (tot - m1 - xh * m2)).astype(BF)
            return 0

        lax.fori_loop(0, R // RC, token_grad, 0)
        lcopy(A1.at[3], dxo_h, loc.at[0]).start()

        so.relay("start")
        sq.relay("start")
        for i in range(dp - 1):
            rcopy(PSG.at[i], PSG.at[i], xss.at[0], psgr.at[i], sib).wait_recv()
        acc = FSG[...]
        for i in range(dp - 1):
            acc = acc + PSG[i]
        SM[...] = acc
        lcopy(SM, gs_h, loc.at[8 + nl]).start()
        done(so, lambda: shard_on(go_h, 2, "start"))
        done(sq, lambda: shard_on(gq_h, 0, "start"))

        for k in range(3):
            shard_on((gq_h, gu_h, go_h)[k], k, "wait_recv")
            shard_on((gq_h, gu_h, go_h)[k], k, "wait_send")
        d_on("wait_recv")
        d_on("wait_send")
        small("wait_send")
        send_a(wq_h, WQ, qcols, wqs, wqr, direct, "wait_send")
        send_a(wu_h, WU, ucols, wus, wur, peers, "wait_send")
        relay_a(WU, ucols, rus, wur, "wait_send")
        send_b(wd_h, WD, nl, d_owner, d_row, gh, wds, wdr, peers, "wait_send")
        relay_b(WD, nl, d_owner, rds, wdr, "wait_send")
        send_b(wo_h, WO, no, o_owner, o_row, uh, wos, wor, direct, "wait_send")
        for k, W in enumerate((WQ, WU, WD, WO)):
            pass_on(W, k, "wait_send")
        spread(dy_h, DY, dss, drs, "wait_send")
        hand_on(DY, dss, drs, "wait_send")
        for k, (s, d) in enumerate(((GD, RD), (GU, RU), (GO, RO), (GQ, RQ))):
            swap(s, d, k, "wait_send")
        line_b(*gd_line, "wait_send")
        if far:
            line_b_on(*gd_line, "wait_send")
        for g in (gu_line, gq_line):
            line_a(*g, "wait_send")
            line_a_on(*g, "wait_send")
        line_b(*go_line, "wait_send")
        line_s("wait_send")
        plane_s("wait_send")

        for k in range(nb):
            give(k, 1, zss, zrs, rlr, "wait_send")
        lcopy(YO, yo_h, loc.at[9 + nl]).wait()
        lcopy(A1.at[3], dxo_h, loc.at[0]).wait()
        lcopy(SM, gs_h, loc.at[8 + nl]).wait()

    return kernel


PLACES = ((0, 1), (1, 1), (2, 1), (3, 1), (4, 3), (7, 1), (8, 4), (12, 1))


def widen(gq, go, gu, gd, y, dx, gs):
    u = gq.shape[0]
    steps = min(8, u // 16)

    def kernel(a, b, c, d, e, f, g, oa, ob, oc, od, oe, of, *outs):
        for i, o in ((a, oa), (b, ob), (c, oc), (d, od)):
            o[...] = i[...].astype(F32)
        oe[0] = e[...]
        of[0] = f[...]

        @pl.when(pl.program_id(0) == 0)
        def _():
            for o, (at, k) in zip(outs, PLACES):
                o[...] = jnp.concatenate([g[at + i] for i in range(k)], axis=1)[0]

    def block(v):
        return pl.BlockSpec((v.shape[0] // steps, v.shape[1]), lambda i: (i, 0))

    def lead(v):
        return pl.BlockSpec((1, v.shape[0] // steps, v.shape[1]), lambda i: (0, i, 0))

    mats = (gq, go, gu, gd)
    return pl.pallas_call(
        kernel,
        grid=(steps,),
        out_shape=tuple(jax.ShapeDtypeStruct(v.shape, F32) for v in mats)
        + tuple(jax.ShapeDtypeStruct((1,) + v.shape, BF) for v in (y, dx))
        + tuple(jax.ShapeDtypeStruct((k * u,), F32) for _, k in PLACES),
        in_specs=[block(v) for v in mats + (y, dx)]
        + [pl.BlockSpec(gs.shape, lambda i: (0, 0, 0))],
        out_specs=[block(v) for v in mats]
        + [lead(y), lead(dx)]
        + [pl.BlockSpec((k * u,), lambda i: (0,)) for _, k in PLACES],
        compiler_params=pltpu.CompilerParams(vmem_limit_bytes=63 * 2**20),
    )(gq, go, gu, gd, y, dx, gs)


def tables(length):
    freq = (np.float32(10000.0) ** (-(np.arange(ROT // 2) * 2).astype(np.float32) / ROT)).astype(
        np.float32
    )
    ang = np.arange(length, dtype=np.float32)[:, None] * freq[None, :]
    co, si = np.cos(ang).astype(np.float32), np.sin(ang).astype(np.float32)
    half = ROT // 2
    ct = np.ones((length, HD), np.float32)
    st = np.zeros((length, HD), np.float32)
    ct[:, :half], ct[:, half:ROT] = co, co
    st[:, :half], st[:, half:ROT] = -si, si
    return tuple(np.concatenate([t, t], axis=1) for t in (ct, st))


def body(mesh, tokens, cotangent, ln1_gain, ln1_bias, ln2_gain, ln2_bias, qkv_weight, qkv_bias,
         out_weight, out_bias, up_weight, up_bias, down_weight, down_bias):
    pn = Plan(mesh, tokens, qkv_weight, up_weight, down_weight)
    n, D, R, u, ffs, hq, fq, dp = pn.n, pn.D, pn.R, pn.u, pn.ffs, pn.hq, pn.fq, pn.dp
    G_, nl, no, nb, T, L, spc = pn.g, pn.nl, pn.no, pn.nb, pn.T, pn.L, pn.spc
    uh, gh = u // 2, G_ // 2
    small, at = None, 0
    for v in (ln1_gain, ln1_bias, ln2_gain, ln2_bias, qkv_bias, out_bias, up_bias, down_bias):
        w = jnp.pad(v, (at, NSMALL * u - at - v.shape[0])).astype(F32)
        small, at = w if small is None else small + w, at + v.shape[0]
    small = small.reshape(NSMALL, 1, u)
    ct, st = tables(L)
    vm = lambda *s, t=BF: pltpu.VMEM(s, t)
    dma = lambda *s: pltpu.SemaphoreType.DMA(s)
    scratch = [
        vm(nb, R, D), vm(nb, R, D), vm(nb, R, D), vm(T // uh, uh, D),
        vm(n, 2, uh, 3 * hq), vm(n, 2, uh, fq), vm(nl, 2, gh, D), vm(no, 2, uh, D),
        vm(T, 3 * hq), vm(T, hq), vm(T, hq),
        vm(spc, pn.heads * QT, QT), vm(spc, pn.heads * QT, 2 * QT), vm(spc, pn.heads * QT, 3 * QT),
        vm(T // uh, uh, fq), vm(nb, R, fq), vm(nb, R, D), vm(3, R, D), vm(2, R, D), vm(R, D), vm(R, D),
        vm(n, 2, uh, 3 * hq), vm(n, 2, uh, fq), vm(nl, 2, gh, D), vm(no, 2, uh, D),
        vm(n, uh, fq), vm(nl, gh, D),
        vm(n - 1, gh, D),
        vm(uh, fq), vm(gh, D),
        vm(NSMALL, 1, u, t=F32), vm(n, NSMALL, 1, u, t=F32), vm(7, 1, max(D, fq), t=F32),
        vm(n, NSMALL, 1, u, t=F32), vm(n, NSMALL, 1, u, t=F32), vm(n - 1, NSMALL, 1, u, t=F32),
        vm(NSMALL, 1, u, t=F32), vm(dp - 1, NSMALL, 1, u, t=F32),
        vm(4, 1, D, t=F32), vm(1, fq, t=F32), vm(1, 3 * hq, t=F32), vm(1, hq, t=F32),
        vm(L, hq, t=F32), vm(L, hq, t=F32),
        dma(dp), dma(nb), dma(dp), dma(nb), dma(n), dma(n),
        dma(n, 3), dma(n, 3), dma(n, nl), dma(n, nl), dma(n), dma(nl), dma(n), dma(no), dma(4), dma(4),
        dma(nb), dma(3), dma(nb), dma(3),
        dma(4), dma(4), dma(n), dma(n), dma(n), dma(n), dma(nl), dma(n), dma(no), dma(n),
        dma(3, 3), dma(3, 3), dma(3, nl), dma(3, nl), dma(3, 2), dma(3, 2), dma(3, 2), dma(3, 2),
        dma(3 + ffs // G_), dma(3 + ffs // G_),
        pltpu.SemaphoreType.DMA, pltpu.SemaphoreType.DMA, dma(n), dma(n), dma(dp), dma(dp), dma(10 + nl),
        pltpu.SemaphoreType.REGULAR, pltpu.SemaphoreType.REGULAR, dma(nl), dma(nl), dma(2), vm(gh, D), dma(3), dma(3),
    ]
    hbm = pl.BlockSpec(memory_space=pl.ANY)
    vmem = pl.BlockSpec(memory_space=pltpu.VMEM)
    sds = jax.ShapeDtypeStruct
    y, dx, gq, go, gu, gd, gs = pl.pallas_call(
        make_kernel(pn),
        out_shape=(
            sds((R, D), BF), sds((R, D), BF), sds((u, 3 * D), BF), sds((u, D), BF),
            sds((u, pn.FF), BF), sds((ffs, D), BF), sds((NSMALL, 1, u), F32),
        ),
        in_specs=[hbm] * 7 + [vmem] * 2,
        out_specs=[hbm] * 7,
        scratch_shapes=scratch,
        compiler_params=pltpu.CompilerParams(
            collective_id=0, has_side_effects=True, vmem_limit_bytes=63 * 2**20
        ),
    )(tokens[0], cotangent[0], small, qkv_weight, out_weight, up_weight, down_weight,
      jnp.asarray(ct), jnp.asarray(st))
    gq, go, gu, gd, y, dx, *sv = widen(gq, go, gu, gd, y, dx, gs)
    return (
        y, dx, sv[0], sv[1], sv[2], sv[3], gq, sv[4], go, sv[5], gu, sv[6], gd, sv[7],
    )


def solution(mesh):
    row = P(("dp", "fsdp"), "ctx", None)
    vec, mat = P("fsdp"), P("fsdp", None)
    in_specs = (row, row, vec, vec, vec, vec, mat, vec, mat, vec, mat, vec, mat, vec)
    out_specs = (row, row, vec, vec, vec, vec, mat, vec, mat, vec, mat, vec, mat, vec)
    return jax.shard_map(
        functools.partial(body, mesh), mesh=mesh, in_specs=in_specs, out_specs=out_specs, check_vma=False
    )
```

```python
import functools
import math

import jax
import jax.numpy as jnp
import numpy as np
from jax import lax
from jax.experimental import pallas as pl
from jax.experimental.pallas import tpu as pltpu
from jax.sharding import PartitionSpec as P

H = 16
HD = 64
ROT = 16
EPS = 1e-05
BF = jnp.bfloat16
F32 = jnp.float32
MESH = pl.DeviceIdType.MESH
QT = 256
NSMALL = 13


def nn(a, b):
    return lax.dot_general(a, b, (((1,), (0,)), ((), ())), preferred_element_type=F32)


def nt(a, b):
    return lax.dot_general(a, b, (((1,), (1,)), ((), ())), preferred_element_type=F32)


def tn(a, b):
    return lax.dot_general(a, b, (((0,), (0,)), ((), ())), preferred_element_type=F32)


def flat(v):
    return v.reshape(-1, v.shape[-1])


def rcopy(src, dst, ss, rs, dev):
    return pltpu.make_async_remote_copy(
        src_ref=src, dst_ref=dst, send_sem=ss, recv_sem=rs, device_id=dev, device_id_type=MESH
    )


def lcopy(src, dst, sem):
    return pltpu.make_async_copy(src, dst, sem)


def mult(v, m):
    return pl.multiple_of(v, m)


def stats(xf):
    mean = jnp.mean(xf, axis=-1, keepdims=True)
    cen = xf - mean
    var = jnp.mean(cen * cen, axis=-1, keepdims=True)
    return cen, lax.rsqrt(var + EPS)


def gelu_parts(h):
    a = jnp.abs(h)
    t = 1.0 / (1.0 + (0.3275911 * 0.5**0.5) * a)
    e = jnp.exp(-0.5 * h * h)
    poly = t * (
        0.127414796
        + t * (-0.142248368 + t * (0.7107068705 + t * (-0.7265760135 + t * 0.5307027145)))
    )
    tail = poly * e
    cum = jnp.where(h >= 0, 1.0 - tail, tail)
    return h * cum, cum + h * e * ((2.0 * math.pi) ** -0.5)


class Plan:
    def __init__(self, mesh, tokens, wqkv, wup, wdown):
        self.dp, self.ctx, self.n = mesh.shape["dp"], mesh.shape["ctx"], mesh.shape["fsdp"]
        self.D = tokens.shape[2]
        self.R = tokens.shape[1]
        self.L = self.R * self.ctx
        self.u = wqkv.shape[0]
        self.FF = wup.shape[1]
        self.ffs = wdown.shape[0]
        self.hq = self.D // self.dp
        self.fq = self.FF // self.dp
        self.g = max(128, self.ffs // self.dp)
        self.nl = self.fq // self.g
        self.no = self.hq // self.u
        self.heads = self.hq // HD
        self.spc = self.dp // self.ctx
        self.nb = self.spc * self.ctx
        self.T = self.nb * self.R


def make_kernel(pn):
    dp, n, D, R, u, ffs, hq, fq = pn.dp, pn.n, pn.D, pn.R, pn.u, pn.ffs, pn.hq, pn.fq
    G_, nl, no, heads, spc, nb, T, L = pn.g, pn.nl, pn.no, pn.heads, pn.spc, pn.nb, pn.T, pn.L
    uh, gh = u // 2, G_ // 2
    nqt = L // QT
    kq = QT // u
    RC = 128
    scale = HD**-0.5

    def kernel(
        x_h, dy_h, sm_h, wq_h, wo_h, wu_h, wd_h, cos_r, sin_r,
        yo_h, dxo_h, gq_h, go_h, gu_h, gd_h, gs_h,
        X, DY, A1, A2, WQ, WU, WD, WO, QKV, O, DO, PS0, PS1, PS2, GA, SL, YS, YR, ZR, RL,
        GQ, GU, GD, GO, RU, RD, ZD, FU, FD,
        SM, SB, VEC, SG, RSG, ZSG, FSG, PSG, LNA, UBA, QBA, DYA, DKA, DVA,
        xss, xrs, dss, drs, smss, smrs,
        wqs, wqr, wus, wur, wds, wdr, wos, wor, fws, fwr,
        yss, yrs, zss, zrs,
        gds, gdr, zqs, zqr, zus, zur, zds, zdr, zos, zor,
        pqs, pqr, pus, pur, pds, pdr, pos, por, pfs, pfr,
        sgs, sgr, zsgs, zsgr, psgs, psgr, loc, zfree, lws, rws, rlr, MD, mls, mlr,
    ):
        p = lax.axis_index("dp")
        c = lax.axis_index("ctx")
        z = lax.axis_index("fsdp")
        sib = (p, 1 - c, z)
        home = p // spc
        oblk = lax.rem(p, spc) * 2 + c
        e = lax.rem(p, 2)
        p1, p2, p3 = p + 1 - 2 * e, lax.rem(p + 2, 4), 3 - p
        away = home + c - 2 * home * c
        via, to_ = p1 + away * (p2 - p1), p2 + away * (p1 - p2)
        fblk = lax.rem(via, spc) * 2 + away
        PSS = (PS0, PS1, PS2)
        XO, DYO = YS.at[0], YS.at[1]
        RQ, RO = GA.at[0:n, :, 0 : 3 * hq], GA.at[n : n + no]
        ZU, ZQ = A2.at[0 : n - 1], A2.at[n - 1 : 2 * n - 2, :, 0 : 3 * hq]
        ZO = A2.at[2 * n - 2 : 3 * n - 3]
        MU, MQ = A2.at[3 * n - 3], A2.at[3 * n - 2, :, 0 : 3 * hq]
        FQ, FO = GA.at[n + no, :, 0 : 3 * hq], GA.at[n + no + 1]

        def ga(b):
            return pl.ds(b * (R // uh), R // uh)

        def rot(v, k):
            return lax.rem(v, k)

        lcopy(x_h, XO, loc.at[0]).start()

        def spread(src, buf, ss, rs, op):
            for i, q in ((1, p1), (2, p2)):
                getattr(rcopy(src, buf.at[oblk], ss.at[i], rs.at[oblk], (q, home, z)), op)()

            @pl.when(home == c)
            def _():
                if op == "start":
                    lcopy(src, buf.at[oblk], rs.at[oblk]).start()

            @pl.when(home != c)
            def _():
                getattr(rcopy(src, buf.at[oblk], ss.at[0], rs.at[oblk], sib), op)()

        def got(buf, rs, b):
            rcopy(buf.at[b], buf.at[b], xss.at[0], rs.at[b], sib).wait_recv()

        def hand_on(buf, ss, rs, op):
            if op == "start":
                got(buf, rs, fblk)
            d = rcopy(buf.at[fblk], buf.at[fblk], ss.at[3], rs.at[fblk], (to_, c, z))
            getattr(d, op)()

        def got_other(buf, rs, b, skip=lambda b: b == fblk):
            @pl.when(jnp.logical_not(skip(b)))
            def _():
                got(buf, rs, b)

        def small(op):
            for i in range(1, n):
                d = rcopy(sm_h, SB.at[z], smss.at[i], smrs.at[z], (p, c, rot(z + i, n)))
                getattr(d, op)()

        qcols = [(mult(j * D + p * hq, 128), j * hq, hq) for j in range(3)]
        ucols = [(mult((k * dp + p) * G_, 128), k * G_, G_) for k in range(nl)]

        def d_owner(k):
            return ((k * dp + p) * G_) // ffs

        def d_row(k):
            return rot((k * dp + p) * G_, ffs)

        def o_owner(k):
            return p * no + k

        def o_row(k):
            return 0

        far = n >= 4

        def peers(send):
            for i in range(1, n):
                if far and i == 1:
                    pl.when(z != n - 1)(functools.partial(send, i))
                elif far and i == n - 1:
                    pl.when(z != 0)(functools.partial(send, i))
                else:
                    send(i)

        def direct(send):
            for i in range(1, n):
                send(i)

        def own_w(op):
            half = pl.ds(mult(c * uh, uh), uh)
            for k, (sc, dc, w) in enumerate(qcols):
                s = wq_h.at[half, pl.ds(sc, w)]
                getattr(lcopy(s, WQ.at[z, c, :, pl.ds(dc, w)], lws.at[k]), op)()
            for k, (sc, dc, w) in enumerate(ucols):
                s = wu_h.at[half, pl.ds(sc, w)]
                getattr(lcopy(s, WU.at[z, c, :, pl.ds(dc, w)], lws.at[3 + k]), op)()
            for k in range(nl):

                @pl.when(d_owner(k) == z)
                def _():
                    s = wd_h.at[pl.ds(mult(d_row(k) + c * gh, gh), gh)]
                    getattr(lcopy(s, WD.at[k, c], lws.at[3 + nl]), op)()

            for k in range(no):

                @pl.when(o_owner(k) == z)
                def _():
                    getattr(lcopy(wo_h.at[half], WO.at[k, c], lws.at[4 + nl]), op)()

        def send_a(W, ss, rs, each, op):
            t = W.at[z, c]
            each(
                lambda i: getattr(rcopy(t, t, ss.at[i], rs.at[z], (p, c, rot(z + i, n))), op)()
            )

        def send_b(W, pieces, owner, ss, rs, each, op):
            for k in range(pieces):

                @pl.when(owner(k) == z)
                def _():
                    t = W.at[k, c]
                    each(
                        lambda i: getattr(
                            rcopy(t, t, ss.at[i], rs.at[k], (p, c, rot(z + i, n))), op
                        )()
                    )

        def piece_wait(W, k, rs):
            rcopy(W.at[k, c], W.at[k, c], xss.at[0], rs.at[k], sib).wait_recv()

        def mine_or_relayed(o, each):
            skip = o == z
            if far and each is peers:
                skip = jnp.logical_or(skip, jnp.logical_and(o == n - 1, z == 1))
                skip = jnp.logical_or(skip, jnp.logical_and(o == 0, z == n - 2))
            return skip

        def recv_w(W, pieces, owner, rs, each):
            for k in range(pieces):

                @pl.when(jnp.logical_not(mine_or_relayed(owner(k), each)))
                def _():
                    piece_wait(W, k, rs)

        def same(k):
            return k

        def relay_w(W, pieces, owner, ss, rs, op):
            if far:
                for k in range(pieces):
                    for at, o, to in ((1, n - 1, 0), (n - 2, 0, n - 1)):

                        @pl.when(jnp.logical_and(owner(k) == o, z == at))
                        def _():
                            t = W.at[k, c]
                            d = rcopy(t, t, ss, rs.at[k], (p, c, to))
                            if op == "start":
                                d.wait_recv()
                            getattr(d, op)()

        def pass_on(W, k, op):
            side = c if op != "wait_recv" else 1 - c
            getattr(rcopy(W.at[:, side], W.at[:, side], fws.at[k], fwr.at[k], sib), op)()

        own_w("start")
        lcopy(dy_h, DYO, loc.at[8 + nl]).start()
        lcopy(sm_h, SB.at[z], smrs.at[z]).start()

        bar = pltpu.get_barrier_semaphore()
        partners = [sib]
        for i in range(1, dp):
            partners += [(rot(p + i, dp), 0, z), (rot(p + i, dp), 1, z)]
        for i in range(1, n):
            partners.append((p, c, rot(z + i, n)))
        for d in partners:
            pl.semaphore_signal(bar, inc=1, device_id=d, device_id_type=MESH)
        pl.semaphore_wait(bar, len(partners))

        lcopy(x_h, XO, loc.at[0]).wait()
        spread(XO, X, xss, xrs, "start")
        small("start")
        own_w("wait")
        send_a(WU, wus, wur, peers, "start")
        send_a(WQ, wqs, wqr, peers, "start")

        for r in (LNA, UBA, QBA, DYA, SG):
            r[...] = jnp.zeros(r.shape, F32)

        for k in range(n):
            rcopy(SB.at[k], SB.at[k], xss.at[0], smrs.at[k], sib).wait_recv()
        for row, r in ((0, 0), (1, 1), (2, 2), (3, 3)):
            VEC[row] = jnp.concatenate([SB[k, r] for k in range(n)], axis=1)
        VEC[4] = jnp.concatenate([SB[k, 7] + SB[k, 12] for k in range(n)], axis=1)
        units = []
        for k in range(nl):
            for i in range(G_ // u if G_ >= u else 1):
                unit = ((k * dp + p) * G_) // u + i
                units.append(SB[unit // (ffs // u), 8 + rot(unit, ffs // u)])
        VEC[5] = jnp.concatenate(units, axis=1)
        for j in range(3):
            units = []
            for i in range(no):
                unit = (j * D + p * hq) // u + i
                units.append(SB[unit // 3, 4 + rot(unit, 3)])
            VEC[6, :, j * hq : (j + 1) * hq] = jnp.concatenate(units, axis=1)

        def blk(i):
            return rot(p + i // 2, spc) * 2 + rot(c + i, 2)

        def norm_step(i, _):
            b = blk(i)
            got_other(X, xrs, b, lambda b: (b - b % 2 * away == fblk - fblk % 2 * away))

            def part(k, _):
                rc = pl.ds(mult(k * RC, RC), RC)
                cen, rstd = stats(X[b, rc, :].astype(F32))
                xh = cen * rstd
                A1[b, rc, :] = (xh * VEC[0] + VEC[1]).astype(BF)
                A2[pl.ds((b * R + k * RC) // uh, RC // uh)] = (
                    (xh * VEC[2] + VEC[3]).astype(BF).reshape(RC // uh, uh, D)
                )
                return 0

            lax.fori_loop(0, R // RC, part, 0)
            return 0

        def turn(v, r0, sign):
            out = []
            ct, st = cos_r[pl.ds(r0, v.shape[0]), :], sin_r[pl.ds(r0, v.shape[0]), :]
            first = lax.broadcasted_iota(jnp.int32, ct.shape, 1) % HD < ROT // 2
            for j in range(hq // 128):
                w = v[:, j * 128 : (j + 1) * 128]
                back = st * jnp.where(
                    first, pltpu.roll(w, 128 - ROT // 2, 1), pltpu.roll(w, ROT // 2, 1)
                )
                out.append(w * ct + (back if sign > 0 else -back))
            return jnp.concatenate(out, axis=1)

        def rows(b):
            return pl.ds(mult(b * R, R), R)

        def qkv_step(i, _):
            b = blk(i)
            a = A1[b]
            r0 = mult(rot(b, 2) * R, R)
            for j in range(3):
                w = flat(WQ[:, :, :, j * hq : (j + 1) * hq])
                f = nn(a, w) + VEC[6, :, j * hq : (j + 1) * hq]
                if j < 2:
                    f = turn(f, r0, 1)
                if j == 0:
                    f = f * scale
                QKV[rows(b), j * hq : (j + 1) * hq] = f.astype(BF)
            return 0


        def head_mask(h):
            lane = lax.broadcasted_iota(jnp.int32, (1, hq), 1)
            return ((lane // HD) == h).astype(F32).astype(BF)

        def attn_step(i, _):
            s = rot(e + i, spc)
            base = mult(s * L, L)
            for t in range(nqt):
                ext = (t + 1) * QT
                q = QKV[pl.ds(base + t * QT, QT), 0:hq]
                keys = QKV[pl.ds(base, ext), hq : 2 * hq]
                vals = QKV[pl.ds(base, ext), 2 * hq : 3 * hq]
                out = jnp.zeros((QT, hq), F32)
                below = lax.broadcasted_iota(jnp.int32, (QT, ext), 1) <= (
                    lax.broadcasted_iota(jnp.int32, (QT, ext), 0) + t * QT
                )
                for h in range(heads):
                    m = head_mask(h)
                    sc = jnp.where(below, nt(q * m, keys), -1e9)
                    ex = jnp.exp(sc - jnp.max(sc, axis=-1, keepdims=True))
                    pr = (ex * (1.0 / jnp.sum(ex, axis=-1, keepdims=True))).astype(BF)
                    PSS[t][s, h * QT : (h + 1) * QT, :] = pr
                    out = out + nn(pr, vals * m)
                O[pl.ds(base + t * QT, QT), :] = out.astype(BF)
            return 0

        def up_step(i, _):
            b = blk(i)
            a = flat(A2[ga(b)])
            for j in range(fq // 256):
                cs = slice(j * 256, (j + 1) * 256)
                h = nn(a, flat(WU[:, :, :, cs])) + VEC[5, :, cs]
                g, sl = gelu_parts(h)
                GA[ga(b), :, cs] = g.astype(BF).reshape(R // uh, uh, 256)
                SL[b, :, cs] = sl.astype(BF)
            return 0

        def yb(i):
            s = e + away * (1 - i // 2) + (1 - away) * (i // 2)
            h = i + (1 - away) * (i // 2) + away * (1 - i // 2)
            return rot(s, 2) * 2 + rot(h, 2)

        def give(k, lane, ss, rs, rlr, op):
            IN = (YR, ZR)[lane]
            b = yb(k)
            src = YS.at[b]

            @pl.when(away == 0)
            def _():
                if k >= 2:
                    d = rcopy(src, IN.at[1], ss.at[k], rs.at[1], (p1, z * 0 + 3 - k, z))
                    getattr(d, op)()
                else:

                    @pl.when(c == k)
                    def _():
                        d = lcopy(src, IN.at[0], ss.at[k])
                        d.start() if op == "start" else d.wait()

                    @pl.when(c != k)
                    def _():
                        getattr(rcopy(src, IN.at[0], ss.at[k], rs.at[0], sib), op)()

            @pl.when(away == 1)
            def _():
                if k < 2:
                    d = rcopy(src, RL.at[lane], ss.at[k], rlr.at[lane], ((p1, p2)[k], c, z))
                else:
                    d = rcopy(src, IN.at[2], ss.at[k], rs.at[2], (p2, z * 0 + k - 2, z))
                getattr(d, op)()

        def all_in(IN, rs):
            @pl.when(home != c)
            def _():
                rcopy(IN.at[0], IN.at[0], xss.at[0], rs.at[0], sib).wait_recv()

            for q in (1, 2):
                rcopy(IN.at[q], IN.at[q], xss.at[0], rs.at[q], sib).wait_recv()

        def add_on(lane, ss, rs, rlr):
            rcopy(RL.at[lane], RL.at[lane], xss.at[0], rlr.at[lane], sib).wait_recv()
            b = yb(3)

            def part(k, _):
                rc = pl.ds(mult(k * RC, RC), RC)
                YS[b, rc, :] = (YS[b, rc, :].astype(F32) + RL[lane, rc, :].astype(F32)).astype(BF)
                return 0

            lax.fori_loop(0, R // RC, part, 0)
            give(3, lane, ss, rs, rlr, "start")

        def y_step(i, _):
            b = yb(i)
            for j in range(D // 256):
                cs = slice(j * 256, (j + 1) * 256)
                y = nn(flat(GA[ga(b)]), flat(WD[:, :, :, cs])) + nn(
                    O[rows(b), :], flat(WO[:, :, :, cs])
                )
                YS[b, :, cs] = y.astype(BF)
            for k in range(3):

                @pl.when(i == k)
                def _():
                    give(k, 0, yss, yrs, rlr, "start")

            return 0


        def dh_step(i, _):
            b = blk(i)
            got_other(DY, drs, b)
            dy = DY[b]
            for j in range(fq // 256):
                cs = slice(j * 256, (j + 1) * 256)
                k = 256 // G_
                dg = nt(dy, flat(WD[j * k : (j + 1) * k]))
                dh = (dg * SL[b, :, cs].astype(F32)).astype(BF)
                SL[b, :, cs] = dh
                UBA[:, cs] += jnp.sum(dh.astype(F32), axis=0, keepdims=True)
            DO[rows(b), :] = nt(dy, flat(WO[...])).astype(BF)
            part = DY[b, :, pl.ds(mult(p * hq, 128), hq)]
            DYA[...] += jnp.sum(part.astype(F32), axis=0, keepdims=True)
            return 0

        relay_w(WU, n, same, rws.at[3], wur, "start")

        @pl.when(away == 1)
        def _():
            got(X, xrs, fblk + 1 - 2 * rot(fblk, 2))
            hand_on(X, xss, xrs, "start")

        lax.fori_loop(0, 2, norm_step, 0)

        @pl.when(away == 0)
        def _():
            hand_on(X, xss, xrs, "start")

        recv_w(WU, n, same, wur, peers)
        pass_on(WU, 1, "start")
        send_b(WD, nl, d_owner, wds, wdr, peers, "start")
        send_b(WO, no, o_owner, wos, wor, peers, "start")
        pass_on(WU, 1, "wait_recv")
        spread(XO, X, xss, xrs, "wait_send")
        hand_on(X, xss, xrs, "wait_send")
        lcopy(dy_h, DYO, loc.at[8 + nl]).wait()
        spread(DYO, DY, dss, drs, "start")
        lax.fori_loop(0, 2, up_step, 0)
        relay_w(WQ, n, same, rws.at[0], wqr, "start")
        lax.fori_loop(2, nb, norm_step, 0)
        lax.fori_loop(2, nb, up_step, 0)
        recv_w(WQ, n, same, wqr, peers)
        pass_on(WQ, 0, "start")
        pass_on(WQ, 0, "wait_recv")
        lax.fori_loop(0, nb, qkv_step, 0)
        hand_on(DY, dss, drs, "start")
        relay_w(WD, nl, d_owner, rws.at[1], wdr, "start")
        relay_w(WO, no, o_owner, rws.at[2], wor, "start")
        lax.fori_loop(0, 1, attn_step, 0)
        lax.fori_loop(1, spc, attn_step, 0)
        recv_w(WD, nl, d_owner, wdr, peers)
        pass_on(WD, 2, "start")
        recv_w(WO, no, o_owner, wor, peers)
        pass_on(WO, 3, "start")
        pass_on(WD, 2, "wait_recv")
        pass_on(WO, 3, "wait_recv")
        lax.fori_loop(0, nb, dh_step, 0)

        def grad(left, right, dst, rows_, cols_, tm, tc, half):
            for a in range(rows_ // tm):
                for b in range(cols_ // tc):
                    v = tn(left(a * tm, tm), right(b * tc, tc)).astype(BF)
                    k = tm // (2 * half)
                    dst[a * k : (a + 1) * k, :, :, b * tc : (b + 1) * tc] = v.reshape(
                        k, 2, half, tc
                    )

        grad(lambda o, w: flat(GA[:, :, o : o + w]), lambda o, w: flat(DY[:, :, o : o + w]),
             GD, fq, D, 512, 512, gh)

        def swap(src, dst, k, op):
            getattr(rcopy(src.at[:, 1 - c], dst, gds.at[k], gdr.at[k], sib), op)()

        swap(GD, RD, 0, "start")
        def attn_back(s, _):
            base = mult(s * L, L)
            DKA[...] = jnp.zeros(DKA.shape, F32)
            DVA[...] = jnp.zeros(DVA.shape, F32)
            for t in range(nqt):
                ext = (t + 1) * QT
                qr = pl.ds(base + t * QT, QT)
                q = QKV[qr, 0:hq]
                keys = QKV[pl.ds(base, ext), hq : 2 * hq]
                vals = QKV[pl.ds(base, ext), 2 * hq : 3 * hq]
                do = DO[qr, :]
                dq = jnp.zeros((QT, hq), F32)
                for h in range(heads):
                    m = head_mask(h)
                    hs = slice(h * QT, (h + 1) * QT)
                    pr = PSS[t][s, hs, :].astype(F32)
                    dpr = nt(do * m, vals)
                    ds = (pr * (dpr - jnp.sum(pr * dpr, axis=-1, keepdims=True))).astype(BF)
                    GQ[h * kq : (h + 1) * kq, :, :, 0:ext] = ds.reshape(kq, 2, uh, ext)
                    dq = dq + nn(ds, keys * m)
                qs = jnp.concatenate([q * head_mask(h) for h in range(heads)], axis=0)
                dos = jnp.concatenate([do * head_mask(h) for h in range(heads)], axis=0)
                for k in range(t + 1):
                    ks = slice(k * QT, (k + 1) * QT)
                    DKA[ks, :] += tn(flat(GQ[:, :, :, ks]), qs)
                    DVA[ks, :] += tn(PSS[t][s, :, ks], dos)
                dqr = turn(dq * scale, t * QT, -1).astype(BF)
                QKV[qr, 0:hq] = dqr
                QBA[:, 0:hq] += jnp.sum(dqr.astype(F32), axis=0, keepdims=True)
            for t in range(nqt):
                kr = pl.ds(base + t * QT, QT)
                ts = slice(t * QT, (t + 1) * QT)
                dk = turn(DKA[ts, :], t * QT, -1).astype(BF)
                dv = DVA[ts, :].astype(BF)
                QKV[kr, hq : 2 * hq] = dk
                QKV[kr, 2 * hq : 3 * hq] = dv
                QBA[:, hq : 2 * hq] += jnp.sum(dk.astype(F32), axis=0, keepdims=True)
                QBA[:, 2 * hq : 3 * hq] += jnp.sum(dv.astype(F32), axis=0, keepdims=True)
            return 0

        def add_half(dst, src, k, pieces):
            rcopy(src, src, gds.at[k], gdr.at[k], sib).wait_recv()

            def one(i, _):
                dst[i, c] = (dst[i, c].astype(F32) + src[i].astype(F32)).astype(BF)
                return 0

            lax.fori_loop(0, pieces, one, 0)

        def line_a(src, Z, M, ss, rs, ms, mr, op):
            def send(to, dst, sem, got_sem, dev):
                getattr(rcopy(src.at[to, c], dst, sem, got_sem, (p, c, dev)), op)()

            if far:
                for at, end, by in ((0, n - 1, 1), (n - 1, 0, n - 2)):

                    @pl.when(z == at)
                    def _():
                        send(end, M, ms, mr, by)

            for i in range(1, n):
                to = rot(z + i, n)

                def one():
                    send(to, Z.at[n - 1 - i], ss.at[i], rs.at[n - 1 - i], to)

                pl.when(jnp.logical_not(later(to)))(one) if far else one()

        def later(to):
            up = jnp.logical_and(to == n - 1, z < 2)
            return jnp.logical_or(up, jnp.logical_and(to == 0, z >= n - 2))

        def line_a_on(src, Z, M, ss, rs, ms, mr, op):
            if far:
                for at, end, i in ((1, n - 1, n - 2), (n - 2, 0, 2)):

                    @pl.when(z == at)
                    def _():
                        if op == "start":
                            rcopy(M, M, ms, mr, sib).wait_recv()
                            src[end, c] = (src[end, c].astype(F32) + M[...].astype(F32)).astype(BF)
                        d = rcopy(
                            src.at[end, c], Z.at[n - 1 - i], ss.at[i], rs.at[n - 1 - i], (p, c, end)
                        )
                        getattr(d, op)()

        def line_b(src, Z, M, pieces, owner, ss, rs, ms, mr, op):
            if M is not None:
                for k in range(pieces):
                    for at, end, by in ((0, n - 1, 1), (n - 1, 0, n - 2)):

                        @pl.when(jnp.logical_and(z == at, owner(k) == end))
                        def _():
                            getattr(rcopy(src.at[k, c], M, ms, mr, (p, c, by)), op)()

            for k in range(pieces):
                o = owner(k)
                slot = rot(z - o - 1 + n, n)

                def one():
                    d = rcopy(src.at[k, c], Z.at[slot], ss.at[k], rs.at[slot], (p, c, o))
                    getattr(d, op)()

                pl.when(jnp.logical_not(jnp.logical_or(o == z, later(o) if M is not None else o < 0)))(one)

        def line_b_on(src, Z, M, pieces, owner, ss, rs, ms, mr, op):
            for k in range(pieces):
                o = owner(k)
                slot = rot(z - o - 1 + n, n)
                for at, end in ((1, n - 1), (n - 2, 0)):

                    @pl.when(jnp.logical_and(z == at, o == end))
                    def _():
                        if op == "start":
                            rcopy(M, M, ms, mr, sib).wait_recv()
                            src[k, c] = (src[k, c].astype(F32) + M[...].astype(F32)).astype(BF)
                        d = rcopy(src.at[k, c], Z.at[slot], ss.at[k], rs.at[slot], (p, c, o))
                        getattr(d, op)()

        def line_sum(own, Z, F, rs, thin=True):
            for i in range(n - 1):

                def one():
                    rcopy(Z.at[i], Z.at[i], xss.at[0], rs.at[i], sib).wait_recv()

                def none():
                    Z[i] = jnp.zeros(Z.shape[1:], BF)

                end = {0: n - 1, n - 2: 0}.get(i)
                if far and thin and end is not None:
                    pl.when(z != end)(one)
                    pl.when(z == end)(none)
                else:
                    one()
            F[...] = (own().astype(F32) + sum_of(Z)).astype(BF)

        def sum_of(Z):
            acc = Z[0].astype(F32)
            for i in range(1, n - 1):
                acc = acc + Z[i].astype(F32)
            return acc

        def line_sum_b(src, Z, F, pieces, owner, rs, then, thin):
            for k in range(pieces):

                @pl.when(owner(k) == z)
                def _():
                    line_sum(lambda: src[k, c], Z, F, rs, thin)

            then("start")

        half_rows = pl.ds(mult(c * uh, uh), uh)
        per = ffs // G_
        o_who = (z * u) // hq
        dcols = [(0, D // 2), (D // 2, D // 2)]

        class Share:
            def __init__(self, F, place, parts, ss, rs, base, has):
                self.F, self.place, self.parts, self.ss, self.rs = F, place, parts, ss, rs
                self.base, self.has = base, has

            def when(self, w, f):
                if self.has is None:
                    f()
                else:
                    pl.when(self.has(w))(f)

            def own(self, op):
                def f():
                    for k, (o, w) in enumerate(self.parts):
                        s, t = self.F.at[:, pl.ds(o, w)], self.place(p, k)
                        for i, q in enumerate((p1, p2)):
                            d = rcopy(s, t, self.ss.at[i, k], self.rs.at[i, k], (q, c, z))
                            getattr(d, op)()
                        ld = lcopy(s, t, loc.at[self.base + k])
                        if op == "start":
                            ld.start()
                        else:
                            ld.wait()

                self.when(p, f)

            def relay(self, op):
                for i, (q, to) in enumerate(((p1, p2), (p2, p1))):

                    def f():
                        for k in range(len(self.parts)):
                            t = self.place(q, k)
                            if op == "start":
                                rcopy(t, t, xss.at[0], self.rs.at[i, k], sib).wait_recv()
                            if k % 2 == i:
                                d = rcopy(t, t, self.ss.at[2, k], self.rs.at[2, k], (to, c, z))
                                getattr(d, op)()

                    self.when(q, f)

            def last(self):
                def f():
                    for k in range(len(self.parts)):
                        t = self.place(p3, k)
                        rcopy(t, t, xss.at[0], self.rs.at[2, k], sib).wait_recv()

                self.when(p3, f)

        def slot_of(w):
            return rot(w + dp * n * per - z * per, dp)

        sq = Share(
            FQ,
            lambda w, k: gq_h.at[half_rows, pl.ds(mult(k * D + w * hq, 128), hq)],
            [(j * hq, hq) for j in range(3)], pqs, pqr, 1, None,
        )
        su = Share(
            FU,
            lambda w, k: gu_h.at[half_rows, pl.ds(mult((k * dp + w) * G_, 128), G_)],
            [(j * G_, G_) for j in range(nl)], pus, pur, 4, None,
        )
        sd = Share(
            FD,
            lambda w, k: gd_h.at[
                pl.ds(mult(slot_of(w) * G_ + c * gh, gh), gh), pl.ds(dcols[k][0], dcols[k][1])
            ],
            dcols, pds, pdr, 4 + nl, None if per >= dp else (lambda w: slot_of(w) < per),
        )
        so = Share(
            FO, lambda w, k: go_h.at[half_rows, pl.ds(dcols[k][0], dcols[k][1])],
            dcols, pos, por, 6 + nl, lambda w: o_who == w,
        )

        def shard_on(dst, k, op):
            r = half_rows if op != "wait_recv" else pl.ds(mult((1 - c) * uh, uh), uh)
            getattr(rcopy(dst.at[r], dst.at[r], pfs.at[k], pfr.at[k], sib), op)()

        def d_on(op):
            for i in range(per):
                side = c if op != "wait_recv" else 1 - c
                t = gd_h.at[pl.ds(mult(i * G_ + side * gh, gh), gh)]
                getattr(rcopy(t, t, pfs.at[3 + i], pfr.at[3 + i], sib), op)()

        def done(sh, on):
            sh.last()
            sh.own("wait_send")
            sh.relay("wait_send")
            on()

        gd_line = (GD, ZD, MD if far else None, nl, d_owner, zds, zdr, mls.at[0], mlr.at[0])
        gu_line = (GU, ZU, MU, zus, zur, mls.at[1], mlr.at[1])
        gq_line = (GQ, ZQ, MQ, zqs, zqr, mls.at[2], mlr.at[2])
        go_line = (GO, ZO, None, no, o_owner, zos, zor, None, None)
        spread(DYO, DY, dss, drs, "wait_send")
        lax.fori_loop(0, nb, y_step, 0)
        add_half(GD, RD, 0, nl)
        line_b(*gd_line, "start")
        grad(lambda o, w: flat(A2[:, :, o : o + w]), lambda o, w: flat(SL[:, :, o : o + w]),
             GU, D, fq, 512, 512, uh)
        swap(GU, RU, 1, "start")
        for i in range(1, n):
            pl.semaphore_signal(
                zfree, inc=1, device_id=(p, c, rot(z + i, n)), device_id_type=MESH
            )

        pl.semaphore_wait(zfree, n - 1)
        add_half(GU, RU, 1, n)
        line_a(*gu_line, "start")
        lax.fori_loop(0, 1, attn_back, 0)
        if far:
            line_b_on(*gd_line, "start")
        add_on(0, yss, yrs, rlr)
        lax.fori_loop(1, spc, attn_back, 0)

        for k in range(3):
            give(k, 0, yss, yrs, rlr, "wait_send")

        tfl = slice(None)
        grad(lambda o, w: O[tfl, o : o + w], lambda o, w: flat(DY[:, :, o : o + w]),
             GO, hq, D, 256, 512, uh)
        swap(GO, RO, 2, "start")
        grad(lambda o, w: flat(A1[:, :, o : o + w]), lambda o, w: QKV[tfl, o : o + w],
             GQ, D, 3 * hq, 512, 256, uh)
        swap(GQ, RQ, 3, "start")
        line_a_on(*gu_line, "start")
        line_sum_b(GD, ZD, FD, nl, d_owner, zdr, sd.own, far)
        add_half(GO, RO, 2, no)
        line_b(*go_line, "start")
        add_half(GQ, RQ, 3, n)
        line_a(*gq_line, "start")

        def dz_step(i, _):
            b = yb(i)

            def part(q, _):
                rc = pl.ds(mult(q * RC, RC), RC)
                cen, rstd = stats(X[b, rc, :].astype(F32))
                X[b, rc, :] = (cen * rstd).astype(BF)
                return 0

            lax.fori_loop(0, R // RC, part, 0)
            k = 256 // u if u <= 256 else 1
            for j in range(D // 256):
                cs = slice(j * 256, (j + 1) * 256)
                xh = X[b, :, cs].astype(F32)
                d1 = nt(QKV[rows(b), :], flat(WQ[j * k : (j + 1) * k]))
                d2 = nt(SL[b], flat(WU[j * k : (j + 1) * k]))
                LNA[0, :, cs] += jnp.sum(d1 * xh, axis=0, keepdims=True)
                LNA[1, :, cs] += jnp.sum(d1, axis=0, keepdims=True)
                LNA[2, :, cs] += jnp.sum(d2 * xh, axis=0, keepdims=True)
                LNA[3, :, cs] += jnp.sum(d2, axis=0, keepdims=True)
                YS[b, :, cs] = (d1 * VEC[0, :, cs] + d2 * VEC[2, :, cs]).astype(BF)
            for k in range(3):

                @pl.when(i == k)
                def _():
                    give(k, 1, zss, zrs, rlr, "start")

            return 0

        lax.fori_loop(0, 2, dz_step, 0)
        sd.relay("start")
        line_sum(lambda: GU[z, c], ZU, FU, zur)
        su.own("start")
        give(3, 0, yss, yrs, rlr, "wait_send")
        lax.fori_loop(2, nb, dz_step, 0)
        line_a_on(*gq_line, "start")

        add_on(1, zss, zrs, rlr)
        lcopy(x_h, A1.at[0], loc.at[0]).start()
        lcopy(dy_h, A1.at[1], loc.at[8 + nl]).start()

        all_in(YR, yrs)

        lcopy(x_h, A1.at[0], loc.at[0]).wait()
        lcopy(dy_h, A1.at[1], loc.at[8 + nl]).wait()

        def out_part(k, _):
            rc = pl.ds(mult(k * RC, RC), RC)
            acc = A1[0, rc, :].astype(F32) + VEC[4]
            for q in range(3):
                acc = acc + YR[q, rc, :].astype(F32)
            A1[2, rc, :] = acc.astype(BF)
            return 0

        lax.fori_loop(0, R // RC, out_part, 0)
        lcopy(A1.at[2], yo_h, loc.at[9 + nl]).start()


        for r in range(4):
            v = LNA[r]
            for k in range(n):
                SG[k, r] = v[:, k * u : (k + 1) * u]
        v = QBA[...]
        for j in range(3):
            for i in range(no):
                unit = (j * D + p * hq) // u + i
                SG[unit // 3, 4 + rot(unit, 3)] = v[:, j * hq + i * u : j * hq + (i + 1) * u]
        v = DYA[...]
        for i in range(no):
            SG[p * no + i, 7] = v[:, i * u : (i + 1) * u]
            SG[p * no + i, 12] = v[:, i * u : (i + 1) * u]
        v = UBA[...]
        for k in range(nl):
            for i in range(G_ // u):
                unit = ((k * dp + p) * G_) // u + i
                o = k * G_ + i * u
                SG[unit // (ffs // u), 8 + rot(unit, ffs // u)] = v[:, o : o + u]
        rcopy(SG, RSG, sgs, sgr, sib).start()

        su.relay("start")

        rcopy(SG, RSG, sgs, sgr, sib).wait()
        SG[...] = SG[...] + RSG[...]

        def line_s(op):
            for i in range(1, n):
                to = rot(z + i, n)
                d = rcopy(SG.at[to], ZSG.at[n - 1 - i], zsgs.at[i], zsgr.at[n - 1 - i], (p, c, to))
                getattr(d, op)()

        line_s("start")
        line_sum_b(GO, ZO, FO, no, o_owner, zor, so.own, False)
        line_sum(lambda: GQ[z, c], ZQ, FQ, zqr)
        sq.own("start")
        done(sd, lambda: d_on("start"))
        done(su, lambda: shard_on(gu_h, 1, "start"))

        for i in range(n - 1):
            rcopy(ZSG.at[i], ZSG.at[i], xss.at[0], zsgr.at[i], sib).wait_recv()
        FSG[...] = SG[z] + sum_of(ZSG)

        def plane_s(op):
            for i in range(1, dp):
                to = (rot(p + i, dp), c, z)
                getattr(rcopy(FSG, PSG.at[dp - 1 - i], psgs.at[i], psgr.at[dp - 1 - i], to), op)()

        plane_s("start")

        give(0, 1, zss, zrs, rlr, "wait_send")
        give(1, 1, zss, zrs, rlr, "wait_send")
        all_in(ZR, zrs)

        def token_grad(k, _):
            rc = pl.ds(mult(k * RC, RC), RC)
            cen, rstd = stats(A1[0, rc, :].astype(F32))
            xh = cen * rstd
            tot = ZR[0, rc, :].astype(F32)
            for q in range(1, 3):
                tot = tot + ZR[q, rc, :].astype(F32)
            m1 = jnp.mean(tot, axis=-1, keepdims=True)
            m2 = jnp.mean(tot * xh, axis=-1, keepdims=True)
            A1[3, rc, :] = (A1[1, rc, :].astype(F32) + rstd * (tot - m1 - xh * m2)).astype(BF)
            return 0

        lax.fori_loop(0, R // RC, token_grad, 0)
        lcopy(A1.at[3], dxo_h, loc.at[0]).start()

        so.relay("start")
        sq.relay("start")
        for i in range(dp - 1):
            rcopy(PSG.at[i], PSG.at[i], xss.at[0], psgr.at[i], sib).wait_recv()
        acc = FSG[...]
        for i in range(dp - 1):
            acc = acc + PSG[i]
        SM[...] = acc
        lcopy(SM, gs_h, loc.at[8 + nl]).start()
        done(so, lambda: shard_on(go_h, 2, "start"))
        done(sq, lambda: shard_on(gq_h, 0, "start"))

        for k in range(3):
            shard_on((gq_h, gu_h, go_h)[k], k, "wait_recv")
            shard_on((gq_h, gu_h, go_h)[k], k, "wait_send")
        d_on("wait_recv")
        d_on("wait_send")
        small("wait_send")
        send_a(WU, wus, wur, peers, "wait_send")
        relay_w(WU, n, same, rws.at[3], wur, "wait_send")
        send_a(WQ, wqs, wqr, peers, "wait_send")
        relay_w(WQ, n, same, rws.at[0], wqr, "wait_send")
        send_b(WD, nl, d_owner, wds, wdr, peers, "wait_send")
        relay_w(WD, nl, d_owner, rws.at[1], wdr, "wait_send")
        send_b(WO, no, o_owner, wos, wor, peers, "wait_send")
        relay_w(WO, no, o_owner, rws.at[2], wor, "wait_send")
        for k, W in enumerate((WQ, WU, WD, WO)):
            pass_on(W, k, "wait_send")
        hand_on(DY, dss, drs, "wait_send")
        for k, (s, d) in enumerate(((GD, RD), (GU, RU), (GO, RO), (GQ, RQ))):
            swap(s, d, k, "wait_send")
        line_b(*gd_line, "wait_send")
        if far:
            line_b_on(*gd_line, "wait_send")
        for g in (gu_line, gq_line):
            line_a(*g, "wait_send")
            line_a_on(*g, "wait_send")
        line_b(*go_line, "wait_send")
        line_s("wait_send")
        plane_s("wait_send")

        for k in range(2, nb):
            give(k, 1, zss, zrs, rlr, "wait_send")
        lcopy(A1.at[2], yo_h, loc.at[9 + nl]).wait()
        lcopy(A1.at[3], dxo_h, loc.at[0]).wait()
        lcopy(SM, gs_h, loc.at[8 + nl]).wait()

    return kernel


PLACES = ((0, 1), (1, 1), (2, 1), (3, 1), (4, 3), (7, 1), (8, 4), (12, 1))


def widen(gq, go, gu, gd, y, dx, gs):
    u = gq.shape[0]
    mats, rows_ = (gq, go, gu, gd), (y, dx)
    order = (2, 3, 0, 1)
    cuts = max(1, min(4, u // 16))

    def kernel(a, b, c, d, e, f, g, oa, ob, oc, od, oe, of, *rest):
        outs, (ia, ib, ic, id_, wa, wb, wc, wd, ve, vf, si, so, sr) = rest[: len(PLACES)], rest[len(PLACES) :]
        src, dst = (a, b, c, d), (oa, ob, oc, od)
        inn, wide = (ia, ib, ic, id_), (wa, wb, wc, wd)

        def part(m, k):
            h = mats[m].shape[0] // cuts
            return pl.ds(k * h, h)

        def load(m, k):
            return lcopy(src[m].at[part(m, k)], inn[m].at[part(m, k)], si.at[m, k])

        def store(m, k):
            return lcopy(wide[m].at[part(m, k)], dst[m].at[part(m, k)], so.at[m, k])

        for m in order:
            for k in range(cuts):
                load(m, k).start()
        for i, (h, v) in enumerate(((e, ve), (f, vf))):
            lcopy(h, v, sr.at[i]).start()
        for o, (at, k) in zip(outs, PLACES):
            o[...] = jnp.concatenate([g[at + i] for i in range(k)], axis=1)[0]
        for m in order:
            for k in range(cuts):
                load(m, k).wait()
                wide[m][part(m, k), :] = inn[m][part(m, k), :].astype(F32)
                store(m, k).start()
        for i, (h, v, o) in enumerate(((e, ve, oe), (f, vf, of))):
            lcopy(h, v, sr.at[i]).wait()
            lcopy(v, o.at[0], sr.at[2 + i]).start()
        for m in order:
            for k in range(cuts):
                store(m, k).wait()
        for i, (v, o) in enumerate(((ve, oe), (vf, of))):
            lcopy(v, o.at[0], sr.at[2 + i]).wait()

    hbm = pl.BlockSpec(memory_space=pl.ANY)
    vmem = pl.BlockSpec(memory_space=pltpu.VMEM)
    return pl.pallas_call(
        kernel,
        out_shape=tuple(jax.ShapeDtypeStruct(v.shape, F32) for v in mats)
        + tuple(jax.ShapeDtypeStruct((1,) + v.shape, BF) for v in rows_)
        + tuple(jax.ShapeDtypeStruct((k * u,), F32) for _, k in PLACES),
        in_specs=[hbm] * 6 + [vmem],
        out_specs=[hbm] * 6 + [vmem] * len(PLACES),
        scratch_shapes=[pltpu.VMEM(v.shape, BF) for v in mats]
        + [pltpu.VMEM(v.shape, F32) for v in mats]
        + [pltpu.VMEM(v.shape, BF) for v in rows_]
        + [pltpu.SemaphoreType.DMA((4, cuts))] * 2 + [pltpu.SemaphoreType.DMA((4,))],
        compiler_params=pltpu.CompilerParams(vmem_limit_bytes=63 * 2**20),
    )(gq, go, gu, gd, y, dx, gs)


def tables(length):
    freq = (np.float32(10000.0) ** (-(np.arange(ROT // 2) * 2).astype(np.float32) / ROT)).astype(
        np.float32
    )
    ang = np.arange(length, dtype=np.float32)[:, None] * freq[None, :]
    co, si = np.cos(ang).astype(np.float32), np.sin(ang).astype(np.float32)
    half = ROT // 2
    ct = np.ones((length, HD), np.float32)
    st = np.zeros((length, HD), np.float32)
    ct[:, :half], ct[:, half:ROT] = co, co
    st[:, :half], st[:, half:ROT] = -si, si
    return tuple(np.concatenate([t, t], axis=1) for t in (ct, st))


def body(mesh, tokens, cotangent, ln1_gain, ln1_bias, ln2_gain, ln2_bias, qkv_weight, qkv_bias,
         out_weight, out_bias, up_weight, up_bias, down_weight, down_bias):
    pn = Plan(mesh, tokens, qkv_weight, up_weight, down_weight)
    n, D, R, u, ffs, hq, fq, dp = pn.n, pn.D, pn.R, pn.u, pn.ffs, pn.hq, pn.fq, pn.dp
    G_, nl, no, nb, T, L, spc = pn.g, pn.nl, pn.no, pn.nb, pn.T, pn.L, pn.spc
    uh, gh = u // 2, G_ // 2
    small, at = None, 0
    for v in (ln1_gain, ln1_bias, ln2_gain, ln2_bias, qkv_bias, out_bias, up_bias, down_bias):
        w = jnp.pad(v, (at, NSMALL * u - at - v.shape[0])).astype(F32)
        small, at = w if small is None else small + w, at + v.shape[0]
    small = small.reshape(NSMALL, 1, u)
    ct, st = tables(L)
    vm = lambda *s, t=BF: pltpu.VMEM(s, t)
    dma = lambda *s: pltpu.SemaphoreType.DMA(s)
    scratch = [
        vm(nb, R, D), vm(nb, R, D), vm(nb, R, D), vm(T // uh, uh, D),
        vm(n, 2, uh, 3 * hq), vm(n, 2, uh, fq), vm(nl, 2, gh, D), vm(no, 2, uh, D),
        vm(T, 3 * hq), vm(T, hq), vm(T, hq),
        vm(spc, pn.heads * QT, QT), vm(spc, pn.heads * QT, 2 * QT), vm(spc, pn.heads * QT, 3 * QT),
        vm(T // uh, uh, fq), vm(nb, R, fq), vm(nb, R, D), vm(3, R, D), vm(3, R, D), vm(2, R, D),
        vm(n, 2, uh, 3 * hq), vm(n, 2, uh, fq), vm(nl, 2, gh, D), vm(no, 2, uh, D),
        vm(n, uh, fq), vm(nl, gh, D),
        vm(n - 1, gh, D),
        vm(uh, fq), vm(gh, D),
        vm(NSMALL, 1, u, t=F32), vm(n, NSMALL, 1, u, t=F32), vm(7, 1, max(D, fq), t=F32),
        vm(n, NSMALL, 1, u, t=F32), vm(n, NSMALL, 1, u, t=F32), vm(n - 1, NSMALL, 1, u, t=F32),
        vm(NSMALL, 1, u, t=F32), vm(dp - 1, NSMALL, 1, u, t=F32),
        vm(4, 1, D, t=F32), vm(1, fq, t=F32), vm(1, 3 * hq, t=F32), vm(1, hq, t=F32),
        vm(L, hq, t=F32), vm(L, hq, t=F32),
        dma(dp), dma(nb), dma(dp), dma(nb), dma(n), dma(n),
        dma(n), dma(n), dma(n), dma(n), dma(n), dma(nl), dma(n), dma(no), dma(4), dma(4),
        dma(nb), dma(3), dma(nb), dma(3),
        dma(4), dma(4), dma(n), dma(n), dma(n), dma(n), dma(nl), dma(n), dma(no), dma(n),
        dma(3, 3), dma(3, 3), dma(3, nl), dma(3, nl), dma(3, 2), dma(3, 2), dma(3, 2), dma(3, 2),
        dma(3 + ffs // G_), dma(3 + ffs // G_),
        pltpu.SemaphoreType.DMA, pltpu.SemaphoreType.DMA, dma(n), dma(n), dma(dp), dma(dp), dma(10 + nl),
        pltpu.SemaphoreType.REGULAR, dma(5 + nl), dma(4), dma(2), vm(gh, D), dma(3), dma(3),
    ]
    hbm = pl.BlockSpec(memory_space=pl.ANY)
    vmem = pl.BlockSpec(memory_space=pltpu.VMEM)
    sds = jax.ShapeDtypeStruct
    y, dx, gq, go, gu, gd, gs = pl.pallas_call(
        make_kernel(pn),
        out_shape=(
            sds((R, D), BF), sds((R, D), BF), sds((u, 3 * D), BF), sds((u, D), BF),
            sds((u, pn.FF), BF), sds((ffs, D), BF), sds((NSMALL, 1, u), F32),
        ),
        in_specs=[hbm] * 7 + [vmem] * 2,
        out_specs=[hbm] * 7,
        scratch_shapes=scratch,
        compiler_params=pltpu.CompilerParams(
            collective_id=0, has_side_effects=True, vmem_limit_bytes=63 * 2**20
        ),
    )(tokens[0], cotangent[0], small, qkv_weight, out_weight, up_weight, down_weight,
      jnp.asarray(ct), jnp.asarray(st))
    gq, go, gu, gd, y, dx, *sv = widen(gq, go, gu, gd, y, dx, gs)
    return (
        y, dx, sv[0], sv[1], sv[2], sv[3], gq, sv[4], go, sv[5], gu, sv[6], gd, sv[7],
    )


def solution(mesh):
    row = P(("dp", "fsdp"), "ctx", None)
    vec, mat = P("fsdp"), P("fsdp", None)
    in_specs = (row, row, vec, vec, vec, vec, mat, vec, mat, vec, mat, vec, mat, vec)
    out_specs = (row, row, vec, vec, vec, vec, mat, vec, mat, vec, mat, vec, mat, vec)
    return jax.shard_map(
        functools.partial(body, mesh), mesh=mesh, in_specs=in_specs, out_specs=out_specs, check_vma=False
    )
```

```python
import functools
import math

import jax
import jax.numpy as jnp
import numpy as np
from jax import lax
from jax.experimental import pallas as pl
from jax.experimental.pallas import tpu as pltpu
from jax.sharding import PartitionSpec as P

H = 16
HD = 64
ROT = 16
EPS = 1e-05
BF = jnp.bfloat16
F32 = jnp.float32
MESH = pl.DeviceIdType.MESH
QT = 256
NSMALL = 13


def nn(a, b):
    return lax.dot_general(a, b, (((1,), (0,)), ((), ())), preferred_element_type=F32)


def nt(a, b):
    return lax.dot_general(a, b, (((1,), (1,)), ((), ())), preferred_element_type=F32)


def tn(a, b):
    return lax.dot_general(a, b, (((0,), (0,)), ((), ())), preferred_element_type=F32)


def flat(v):
    return v.reshape(-1, v.shape[-1])


def rcopy(src, dst, ss, rs, dev):
    return pltpu.make_async_remote_copy(
        src_ref=src, dst_ref=dst, send_sem=ss, recv_sem=rs, device_id=dev, device_id_type=MESH
    )


def lcopy(src, dst, sem):
    return pltpu.make_async_copy(src, dst, sem)


def mult(v, m):
    return pl.multiple_of(v, m)


def stats(xf):
    mean = jnp.mean(xf, axis=-1, keepdims=True)
    cen = xf - mean
    var = jnp.mean(cen * cen, axis=-1, keepdims=True)
    return cen, lax.rsqrt(var + EPS)


def gelu_parts(h):
    a = jnp.abs(h)
    t = 1.0 / (1.0 + (0.3275911 * 0.5**0.5) * a)
    e = jnp.exp(-0.5 * h * h)
    poly = t * (
        0.127414796
        + t * (-0.142248368 + t * (0.7107068705 + t * (-0.7265760135 + t * 0.5307027145)))
    )
    tail = poly * e
    cum = jnp.where(h >= 0, 1.0 - tail, tail)
    return h * cum, cum + h * e * ((2.0 * math.pi) ** -0.5)


class Plan:
    def __init__(self, mesh, tokens, wqkv, wup, wdown):
        self.dp, self.ctx, self.n = mesh.shape["dp"], mesh.shape["ctx"], mesh.shape["fsdp"]
        self.D = tokens.shape[2]
        self.R = tokens.shape[1]
        self.L = self.R * self.ctx
        self.u = wqkv.shape[0]
        self.FF = wup.shape[1]
        self.ffs = wdown.shape[0]
        self.hq = self.D // self.dp
        self.fq = self.FF // self.dp
        self.g = max(128, self.ffs // self.dp)
        self.nl = self.fq // self.g
        self.no = self.hq // self.u
        self.heads = self.hq // HD
        self.spc = self.dp // self.ctx
        self.nb = self.spc * self.ctx
        self.T = self.nb * self.R


def make_kernel(pn):
    dp, n, D, R, u, ffs, hq, fq = pn.dp, pn.n, pn.D, pn.R, pn.u, pn.ffs, pn.hq, pn.fq
    G_, nl, no, heads, spc, nb, T, L = pn.g, pn.nl, pn.no, pn.heads, pn.spc, pn.nb, pn.T, pn.L
    uh, gh = u // 2, G_ // 2
    nqt = L // QT
    kq = QT // u
    RC = 128
    scale = HD**-0.5

    def kernel(
        x_h, dy_h, sm_h, wq_h, wo_h, wu_h, wd_h, cos_r, sin_r,
        yo_h, dxo_h, gq_h, go_h, gu_h, gd_h, gs_h,
        X, DY, A1, A2, WQ, WU, WD, WO, QKV, O, DO, PS0, PS1, PS2, GA, SL, YS, YR, ZR, RL,
        GQ, GU, GD, GO, RU, RD, ZD, FU, FD,
        SM, SB, VEC, SG, RSG, ZSG, FSG, PSG, LNA, UBA, QBA, DYA, DKA, DVA,
        xss, xrs, dss, drs, smss, smrs,
        wqs, wqr, wus, wur, wds, wdr, wos, wor, fws, fwr,
        yss, yrs, zss, zrs,
        gds, gdr, zqs, zqr, zus, zur, zds, zdr, zos, zor,
        pqs, pqr, pus, pur, pds, pdr, pos, por, pfs, pfr,
        sgs, sgr, zsgs, zsgr, psgs, psgr, loc, zfree, lws, rws, rlr, MD, mls, mlr,
    ):
        p = lax.axis_index("dp")
        c = lax.axis_index("ctx")
        z = lax.axis_index("fsdp")
        sib = (p, 1 - c, z)
        home = p // spc
        oblk = lax.rem(p, spc) * 2 + c
        e = lax.rem(p, 2)
        p1, p2, p3 = p + 1 - 2 * e, lax.rem(p + 2, 4), 3 - p
        away = home + c - 2 * home * c
        via, to_ = p1 + away * (p2 - p1), p2 + away * (p1 - p2)
        fblk = lax.rem(via, spc) * 2 + away
        PSS = (PS0, PS1, PS2)
        XO, DYO = YS.at[0], YS.at[1]
        RQ, RO = GA.at[0:n, :, 0 : 3 * hq], GA.at[n : n + no]
        ZU, ZQ = A2.at[0 : n - 1], A2.at[n - 1 : 2 * n - 2, :, 0 : 3 * hq]
        ZO = A2.at[2 * n - 2 : 3 * n - 3]
        MU, MQ = A2.at[3 * n - 3], A2.at[3 * n - 2, :, 0 : 3 * hq]
        FQ, FO = GA.at[n + no, :, 0 : 3 * hq], GA.at[n + no + 1]

        def ga(b):
            return pl.ds(b * (R // uh), R // uh)

        def rot(v, k):
            return lax.rem(v, k)

        lcopy(x_h, XO, loc.at[0]).start()

        def spread(src, buf, ss, rs, op):
            for i, q in ((1, p1), (2, p2)):
                getattr(rcopy(src, buf.at[oblk], ss.at[i], rs.at[oblk], (q, home, z)), op)()

            @pl.when(home == c)
            def _():
                if op == "start":
                    lcopy(src, buf.at[oblk], rs.at[oblk]).start()

            @pl.when(home != c)
            def _():
                getattr(rcopy(src, buf.at[oblk], ss.at[0], rs.at[oblk], sib), op)()

        def got(buf, rs, b):
            rcopy(buf.at[b], buf.at[b], xss.at[0], rs.at[b], sib).wait_recv()

        def hand_on(buf, ss, rs, op):
            if op == "start":
                got(buf, rs, fblk)
            d = rcopy(buf.at[fblk], buf.at[fblk], ss.at[3], rs.at[fblk], (to_, c, z))
            getattr(d, op)()

        def got_other(buf, rs, b, skip=lambda b: b == fblk):
            @pl.when(jnp.logical_not(skip(b)))
            def _():
                got(buf, rs, b)

        def small(op):
            for i in range(1, n):
                d = rcopy(sm_h, SB.at[z], smss.at[i], smrs.at[z], (p, c, rot(z + i, n)))
                getattr(d, op)()

        qcols = [(mult(j * D + p * hq, 128), j * hq, hq) for j in range(3)]
        ucols = [(mult((k * dp + p) * G_, 128), k * G_, G_) for k in range(nl)]

        def d_owner(k):
            return ((k * dp + p) * G_) // ffs

        def d_row(k):
            return rot((k * dp + p) * G_, ffs)

        def o_owner(k):
            return p * no + k

        def o_row(k):
            return 0

        far = n >= 4

        def peers(send):
            for i in range(1, n):
                if far and i == 1:
                    pl.when(z != n - 1)(functools.partial(send, i))
                elif far and i == n - 1:
                    pl.when(z != 0)(functools.partial(send, i))
                else:
                    send(i)

        def direct(send):
            for i in range(1, n):
                send(i)

        def own_w(op):
            half = pl.ds(mult(c * uh, uh), uh)
            for k, (sc, dc, w) in enumerate(qcols):
                s = wq_h.at[half, pl.ds(sc, w)]
                getattr(lcopy(s, WQ.at[z, c, :, pl.ds(dc, w)], lws.at[k]), op)()
            for k, (sc, dc, w) in enumerate(ucols):
                s = wu_h.at[half, pl.ds(sc, w)]
                getattr(lcopy(s, WU.at[z, c, :, pl.ds(dc, w)], lws.at[3 + k]), op)()
            for k in range(nl):

                @pl.when(d_owner(k) == z)
                def _():
                    s = wd_h.at[pl.ds(mult(d_row(k) + c * gh, gh), gh)]
                    getattr(lcopy(s, WD.at[k, c], lws.at[3 + nl]), op)()

            for k in range(no):

                @pl.when(o_owner(k) == z)
                def _():
                    getattr(lcopy(wo_h.at[half], WO.at[k, c], lws.at[4 + nl]), op)()

        def send_a(W, ss, rs, each, op):
            t = W.at[z, c]
            each(
                lambda i: getattr(rcopy(t, t, ss.at[i], rs.at[z], (p, c, rot(z + i, n))), op)()
            )

        def send_b(W, pieces, owner, ss, rs, each, op):
            for k in range(pieces):

                @pl.when(owner(k) == z)
                def _():
                    t = W.at[k, c]
                    each(
                        lambda i: getattr(
                            rcopy(t, t, ss.at[i], rs.at[k], (p, c, rot(z + i, n))), op
                        )()
                    )

        def piece_wait(W, k, rs):
            rcopy(W.at[k, c], W.at[k, c], xss.at[0], rs.at[k], sib).wait_recv()

        def mine_or_relayed(o, each):
            skip = o == z
            if far and each is peers:
                skip = jnp.logical_or(skip, jnp.logical_and(o == n - 1, z == 1))
                skip = jnp.logical_or(skip, jnp.logical_and(o == 0, z == n - 2))
            return skip

        def recv_w(W, pieces, owner, rs, each):
            for k in range(pieces):

                @pl.when(jnp.logical_not(mine_or_relayed(owner(k), each)))
                def _():
                    piece_wait(W, k, rs)

        def same(k):
            return k

        def relay_w(W, pieces, owner, ss, rs, op):
            if far:
                for k in range(pieces):
                    for at, o, to in ((1, n - 1, 0), (n - 2, 0, n - 1)):

                        @pl.when(jnp.logical_and(owner(k) == o, z == at))
                        def _():
                            t = W.at[k, c]
                            d = rcopy(t, t, ss, rs.at[k], (p, c, to))
                            if op == "start":
                                d.wait_recv()
                            getattr(d, op)()

        def pass_on(W, k, op):
            side = c if op != "wait_recv" else 1 - c
            getattr(rcopy(W.at[:, side], W.at[:, side], fws.at[k], fwr.at[k], sib), op)()

        own_w("start")
        lcopy(dy_h, DYO, loc.at[8 + nl]).start()
        lcopy(sm_h, SB.at[z], smrs.at[z]).start()

        bar = pltpu.get_barrier_semaphore()
        partners = [sib]
        for i in range(1, dp):
            partners += [(rot(p + i, dp), 0, z), (rot(p + i, dp), 1, z)]
        for i in range(1, n):
            partners.append((p, c, rot(z + i, n)))
        for d in partners:
            pl.semaphore_signal(bar, inc=1, device_id=d, device_id_type=MESH)
        pl.semaphore_wait(bar, len(partners))

        lcopy(x_h, XO, loc.at[0]).wait()
        spread(XO, X, xss, xrs, "start")
        small("start")
        own_w("wait")
        send_a(WU, wus, wur, peers, "start")
        send_a(WQ, wqs, wqr, peers, "start")

        for r in (LNA, UBA, QBA, DYA, SG):
            r[...] = jnp.zeros(r.shape, F32)

        for k in range(n):
            rcopy(SB.at[k], SB.at[k], xss.at[0], smrs.at[k], sib).wait_recv()
        for row, r in ((0, 0), (1, 1), (2, 2), (3, 3)):
            VEC[row] = jnp.concatenate([SB[k, r] for k in range(n)], axis=1)
        VEC[4] = jnp.concatenate([SB[k, 7] + SB[k, 12] for k in range(n)], axis=1)
        units = []
        for k in range(nl):
            for i in range(G_ // u if G_ >= u else 1):
                unit = ((k * dp + p) * G_) // u + i
                units.append(SB[unit // (ffs // u), 8 + rot(unit, ffs // u)])
        VEC[5] = jnp.concatenate(units, axis=1)
        for j in range(3):
            units = []
            for i in range(no):
                unit = (j * D + p * hq) // u + i
                units.append(SB[unit // 3, 4 + rot(unit, 3)])
            VEC[6, :, j * hq : (j + 1) * hq] = jnp.concatenate(units, axis=1)

        def blk(i):
            return rot(p + i // 2, spc) * 2 + rot(c + i, 2)

        def norm_step(i, _):
            b = blk(i)
            got_other(X, xrs, b, lambda b: (b - b % 2 * away == fblk - fblk % 2 * away))

            def part(k, _):
                rc = pl.ds(mult(k * RC, RC), RC)
                cen, rstd = stats(X[b, rc, :].astype(F32))
                xh = cen * rstd
                A1[b, rc, :] = (xh * VEC[0] + VEC[1]).astype(BF)
                A2[pl.ds((b * R + k * RC) // uh, RC // uh)] = (
                    (xh * VEC[2] + VEC[3]).astype(BF).reshape(RC // uh, uh, D)
                )
                return 0

            lax.fori_loop(0, R // RC, part, 0)
            return 0

        def turn(v, r0, sign):
            out = []
            ct, st = cos_r[pl.ds(r0, v.shape[0]), :], sin_r[pl.ds(r0, v.shape[0]), :]
            first = lax.broadcasted_iota(jnp.int32, ct.shape, 1) % HD < ROT // 2
            for j in range(hq // 128):
                w = v[:, j * 128 : (j + 1) * 128]
                back = st * jnp.where(
                    first, pltpu.roll(w, 128 - ROT // 2, 1), pltpu.roll(w, ROT // 2, 1)
                )
                out.append(w * ct + (back if sign > 0 else -back))
            return jnp.concatenate(out, axis=1)

        def rows(b):
            return pl.ds(mult(b * R, R), R)

        def qkv_step(i, _):
            q = rot(e + i, spc)
            a = flat(A1[pl.ds(q * 2, 2)])
            r0 = 0
            for j in range(3):
                w = flat(WQ[:, :, :, j * hq : (j + 1) * hq])
                f = nn(a, w) + VEC[6, :, j * hq : (j + 1) * hq]
                if j < 2:
                    f = turn(f, r0, 1)
                if j == 0:
                    f = f * scale
                QKV[pl.ds(mult(q * L, L), L), j * hq : (j + 1) * hq] = f.astype(BF)
            return 0


        def head_mask(h):
            lane = lax.broadcasted_iota(jnp.int32, (1, hq), 1)
            return ((lane // HD) == h).astype(F32).astype(BF)

        def attn_step(i, _):
            s = rot(e + i, spc)
            base = mult(s * L, L)
            for t in range(nqt):
                ext = (t + 1) * QT
                q = QKV[pl.ds(base + t * QT, QT), 0:hq]
                keys = QKV[pl.ds(base, ext), hq : 2 * hq]
                vals = QKV[pl.ds(base, ext), 2 * hq : 3 * hq]
                out = jnp.zeros((QT, hq), F32)
                below = lax.broadcasted_iota(jnp.int32, (QT, ext), 1) <= (
                    lax.broadcasted_iota(jnp.int32, (QT, ext), 0) + t * QT
                )
                for h in range(heads):
                    m = head_mask(h)
                    sc = jnp.where(below, nt(q * m, keys), -1e9)
                    ex = jnp.exp(sc - jnp.max(sc, axis=-1, keepdims=True))
                    pr = (ex * (1.0 / jnp.sum(ex, axis=-1, keepdims=True))).astype(BF)
                    PSS[t][s, h * QT : (h + 1) * QT, :] = pr
                    out = out + nn(pr, vals * m)
                O[pl.ds(base + t * QT, QT), :] = out.astype(BF)
            return 0

        def up_step(i, _):
            q = rot(e + i, spc)
            both = pl.ds(q * (L // uh), L // uh)
            a = flat(A2[both])
            for j in range(fq // 256):
                cs = slice(j * 256, (j + 1) * 256)
                h = nn(a, flat(WU[:, :, :, cs])) + VEC[5, :, cs]
                g, sl = gelu_parts(h)
                GA[both, :, cs] = g.astype(BF).reshape(L // uh, uh, 256)
                SL[pl.ds(q * 2, 2), :, cs] = sl.astype(BF).reshape(2, R, 256)
            return 0

        def yb(i):
            s = e + away * (1 - i // 2) + (1 - away) * (i // 2)
            h = i + (1 - away) * (i // 2) + away * (1 - i // 2)
            return rot(s, 2) * 2 + rot(h, 2)

        def give(k, lane, ss, rs, rlr, op):
            IN = (YR, ZR)[lane]
            b = yb(k)
            src = YS.at[b]

            @pl.when(away == 0)
            def _():
                if k >= 2:
                    d = rcopy(src, IN.at[1], ss.at[k], rs.at[1], (p1, z * 0 + 3 - k, z))
                    getattr(d, op)()
                else:

                    @pl.when(c == k)
                    def _():
                        d = lcopy(src, IN.at[0], ss.at[k])
                        d.start() if op == "start" else d.wait()

                    @pl.when(c != k)
                    def _():
                        getattr(rcopy(src, IN.at[0], ss.at[k], rs.at[0], sib), op)()

            @pl.when(away == 1)
            def _():
                if k < 2:
                    d = rcopy(src, RL.at[lane], ss.at[k], rlr.at[lane], ((p1, p2)[k], c, z))
                else:
                    d = rcopy(src, IN.at[2], ss.at[k], rs.at[2], (p2, z * 0 + k - 2, z))
                getattr(d, op)()

        def all_in(IN, rs):
            @pl.when(home != c)
            def _():
                rcopy(IN.at[0], IN.at[0], xss.at[0], rs.at[0], sib).wait_recv()

            for q in (1, 2):
                rcopy(IN.at[q], IN.at[q], xss.at[0], rs.at[q], sib).wait_recv()

        def add_on(lane, ss, rs, rlr):
            rcopy(RL.at[lane], RL.at[lane], xss.at[0], rlr.at[lane], sib).wait_recv()
            b = yb(3)

            def part(k, _):
                rc = pl.ds(mult(k * RC, RC), RC)
                YS[b, rc, :] = (YS[b, rc, :].astype(F32) + RL[lane, rc, :].astype(F32)).astype(BF)
                return 0

            lax.fori_loop(0, R // RC, part, 0)
            give(3, lane, ss, rs, rlr, "start")

        def y_step(i, _):
            b = yb(i)
            for j in range(D // 256):
                cs = slice(j * 256, (j + 1) * 256)
                y = nn(flat(GA[ga(b)]), flat(WD[:, :, :, cs])) + nn(
                    O[rows(b), :], flat(WO[:, :, :, cs])
                )
                YS[b, :, cs] = y.astype(BF)
            for k in range(3):

                @pl.when(i == k)
                def _():
                    give(k, 0, yss, yrs, rlr, "start")

            return 0


        def dh_step(i, _):
            b = blk(i)
            got_other(DY, drs, b)
            dy = DY[b]
            for j in range(fq // 256):
                cs = slice(j * 256, (j + 1) * 256)
                k = 256 // G_
                dg = nt(dy, flat(WD[j * k : (j + 1) * k]))
                dh = (dg * SL[b, :, cs].astype(F32)).astype(BF)
                SL[b, :, cs] = dh
                UBA[:, cs] += jnp.sum(dh.astype(F32), axis=0, keepdims=True)
            DO[rows(b), :] = nt(dy, flat(WO[...])).astype(BF)
            part = DY[b, :, pl.ds(mult(p * hq, 128), hq)]
            DYA[...] += jnp.sum(part.astype(F32), axis=0, keepdims=True)
            return 0

        relay_w(WU, n, same, rws.at[3], wur, "start")

        @pl.when(away == 1)
        def _():
            got(X, xrs, fblk + 1 - 2 * rot(fblk, 2))
            hand_on(X, xss, xrs, "start")

        lax.fori_loop(0, 2, norm_step, 0)

        @pl.when(away == 0)
        def _():
            hand_on(X, xss, xrs, "start")

        recv_w(WU, n, same, wur, peers)
        pass_on(WU, 1, "start")
        send_b(WD, nl, d_owner, wds, wdr, peers, "start")
        send_b(WO, no, o_owner, wos, wor, peers, "start")
        pass_on(WU, 1, "wait_recv")
        spread(XO, X, xss, xrs, "wait_send")
        hand_on(X, xss, xrs, "wait_send")
        lcopy(dy_h, DYO, loc.at[8 + nl]).wait()
        spread(DYO, DY, dss, drs, "start")
        lax.fori_loop(0, 1, up_step, 0)
        relay_w(WQ, n, same, rws.at[0], wqr, "start")
        lax.fori_loop(2, nb, norm_step, 0)
        lax.fori_loop(1, spc, up_step, 0)
        recv_w(WQ, n, same, wqr, peers)
        pass_on(WQ, 0, "start")
        pass_on(WQ, 0, "wait_recv")
        lax.fori_loop(0, spc, qkv_step, 0)
        hand_on(DY, dss, drs, "start")
        relay_w(WD, nl, d_owner, rws.at[1], wdr, "start")
        relay_w(WO, no, o_owner, rws.at[2], wor, "start")
        lax.fori_loop(0, 1, attn_step, 0)
        lax.fori_loop(1, spc, attn_step, 0)
        recv_w(WD, nl, d_owner, wdr, peers)
        pass_on(WD, 2, "start")
        recv_w(WO, no, o_owner, wor, peers)
        pass_on(WO, 3, "start")
        pass_on(WD, 2, "wait_recv")
        pass_on(WO, 3, "wait_recv")
        lax.fori_loop(0, nb, dh_step, 0)

        def grad(left, right, dst, rows_, cols_, tm, tc, half):
            for a in range(rows_ // tm):
                for b in range(cols_ // tc):
                    v = tn(left(a * tm, tm), right(b * tc, tc)).astype(BF)
                    k = tm // (2 * half)
                    dst[a * k : (a + 1) * k, :, :, b * tc : (b + 1) * tc] = v.reshape(
                        k, 2, half, tc
                    )

        grad(lambda o, w: flat(GA[:, :, o : o + w]), lambda o, w: flat(DY[:, :, o : o + w]),
             GD, fq, D, 512, 512, gh)

        def swap(src, dst, k, op):
            getattr(rcopy(src.at[:, 1 - c], dst, gds.at[k], gdr.at[k], sib), op)()

        swap(GD, RD, 0, "start")
        def attn_back(s, _):
            base = mult(s * L, L)
            DKA[...] = jnp.zeros(DKA.shape, F32)
            DVA[...] = jnp.zeros(DVA.shape, F32)
            for t in range(nqt):
                ext = (t + 1) * QT
                qr = pl.ds(base + t * QT, QT)
                q = QKV[qr, 0:hq]
                keys = QKV[pl.ds(base, ext), hq : 2 * hq]
                vals = QKV[pl.ds(base, ext), 2 * hq : 3 * hq]
                do = DO[qr, :]
                dq = jnp.zeros((QT, hq), F32)
                for h in range(heads):
                    m = head_mask(h)
                    hs = slice(h * QT, (h + 1) * QT)
                    pr = PSS[t][s, hs, :].astype(F32)
                    dpr = nt(do * m, vals)
                    ds = (pr * (dpr - jnp.sum(pr * dpr, axis=-1, keepdims=True))).astype(BF)
                    GQ[h * kq : (h + 1) * kq, :, :, 0:ext] = ds.reshape(kq, 2, uh, ext)
                    dq = dq + nn(ds, keys * m)
                qs = jnp.concatenate([q * head_mask(h) for h in range(heads)], axis=0)
                dos = jnp.concatenate([do * head_mask(h) for h in range(heads)], axis=0)
                for k in range(t + 1):
                    ks = slice(k * QT, (k + 1) * QT)
                    DKA[ks, :] += tn(flat(GQ[:, :, :, ks]), qs)
                    DVA[ks, :] += tn(PSS[t][s, :, ks], dos)
                dqr = turn(dq * scale, t * QT, -1).astype(BF)
                QKV[qr, 0:hq] = dqr
                QBA[:, 0:hq] += jnp.sum(dqr.astype(F32), axis=0, keepdims=True)
            for t in range(nqt):
                kr = pl.ds(base + t * QT, QT)
                ts = slice(t * QT, (t + 1) * QT)
                dk = turn(DKA[ts, :], t * QT, -1).astype(BF)
                dv = DVA[ts, :].astype(BF)
                QKV[kr, hq : 2 * hq] = dk
                QKV[kr, 2 * hq : 3 * hq] = dv
                QBA[:, hq : 2 * hq] += jnp.sum(dk.astype(F32), axis=0, keepdims=True)
                QBA[:, 2 * hq : 3 * hq] += jnp.sum(dv.astype(F32), axis=0, keepdims=True)
            return 0

        def add_half(dst, src, k, pieces):
            rcopy(src, src, gds.at[k], gdr.at[k], sib).wait_recv()

            def one(i, _):
                dst[i, c] = (dst[i, c].astype(F32) + src[i].astype(F32)).astype(BF)
                return 0

            lax.fori_loop(0, pieces, one, 0)

        def line_a(src, Z, M, ss, rs, ms, mr, op):
            def send(to, dst, sem, got_sem, dev):
                getattr(rcopy(src.at[to, c], dst, sem, got_sem, (p, c, dev)), op)()

            if far:
                for at, end, by in ((0, n - 1, 1), (n - 1, 0, n - 2)):

                    @pl.when(z == at)
                    def _():
                        send(end, M, ms, mr, by)

            for i in range(1, n):
                to = rot(z + i, n)

                def one():
                    send(to, Z.at[n - 1 - i], ss.at[i], rs.at[n - 1 - i], to)

                pl.when(jnp.logical_not(later(to)))(one) if far else one()

        def later(to):
            up = jnp.logical_and(to == n - 1, z < 2)
            return jnp.logical_or(up, jnp.logical_and(to == 0, z >= n - 2))

        def line_a_on(src, Z, M, ss, rs, ms, mr, op):
            if far:
                for at, end, i in ((1, n - 1, n - 2), (n - 2, 0, 2)):

                    @pl.when(z == at)
                    def _():
                        if op == "start":
                            rcopy(M, M, ms, mr, sib).wait_recv()
                            src[end, c] = (src[end, c].astype(F32) + M[...].astype(F32)).astype(BF)
                        d = rcopy(
                            src.at[end, c], Z.at[n - 1 - i], ss.at[i], rs.at[n - 1 - i], (p, c, end)
                        )
                        getattr(d, op)()

        def line_b(src, Z, M, pieces, owner, ss, rs, ms, mr, op):
            if M is not None:
                for k in range(pieces):
                    for at, end, by in ((0, n - 1, 1), (n - 1, 0, n - 2)):

                        @pl.when(jnp.logical_and(z == at, owner(k) == end))
                        def _():
                            getattr(rcopy(src.at[k, c], M, ms, mr, (p, c, by)), op)()

            for k in range(pieces):
                o = owner(k)
                slot = rot(z - o - 1 + n, n)

                def one():
                    d = rcopy(src.at[k, c], Z.at[slot], ss.at[k], rs.at[slot], (p, c, o))
                    getattr(d, op)()

                pl.when(jnp.logical_not(jnp.logical_or(o == z, later(o) if M is not None else o < 0)))(one)

        def line_b_on(src, Z, M, pieces, owner, ss, rs, ms, mr, op):
            for k in range(pieces):
                o = owner(k)
                slot = rot(z - o - 1 + n, n)
                for at, end in ((1, n - 1), (n - 2, 0)):

                    @pl.when(jnp.logical_and(z == at, o == end))
                    def _():
                        if op == "start":
                            rcopy(M, M, ms, mr, sib).wait_recv()
                            src[k, c] = (src[k, c].astype(F32) + M[...].astype(F32)).astype(BF)
                        d = rcopy(src.at[k, c], Z.at[slot], ss.at[k], rs.at[slot], (p, c, o))
                        getattr(d, op)()

        def line_sum(own, Z, F, rs, thin=True):
            for i in range(n - 1):

                def one():
                    rcopy(Z.at[i], Z.at[i], xss.at[0], rs.at[i], sib).wait_recv()

                def none():
                    Z[i] = jnp.zeros(Z.shape[1:], BF)

                end = {0: n - 1, n - 2: 0}.get(i)
                if far and thin and end is not None:
                    pl.when(z != end)(one)
                    pl.when(z == end)(none)
                else:
                    one()
            F[...] = (own().astype(F32) + sum_of(Z)).astype(BF)

        def sum_of(Z):
            acc = Z[0].astype(F32)
            for i in range(1, n - 1):
                acc = acc + Z[i].astype(F32)
            return acc

        def line_sum_b(src, Z, F, pieces, owner, rs, then, thin):
            for k in range(pieces):

                @pl.when(owner(k) == z)
                def _():
                    line_sum(lambda: src[k, c], Z, F, rs, thin)

            then("start")

        half_rows = pl.ds(mult(c * uh, uh), uh)
        per = ffs // G_
        o_who = (z * u) // hq
        dcols = [(0, D // 2), (D // 2, D // 2)]

        class Share:
            def __init__(self, F, place, parts, ss, rs, base, has):
                self.F, self.place, self.parts, self.ss, self.rs = F, place, parts, ss, rs
                self.base, self.has = base, has

            def when(self, w, f):
                if self.has is None:
                    f()
                else:
                    pl.when(self.has(w))(f)

            def own(self, op):
                def f():
                    for k, (o, w) in enumerate(self.parts):
                        s, t = self.F.at[:, pl.ds(o, w)], self.place(p, k)
                        for i, q in enumerate((p1, p2)):
                            d = rcopy(s, t, self.ss.at[i, k], self.rs.at[i, k], (q, c, z))
                            getattr(d, op)()
                        ld = lcopy(s, t, loc.at[self.base + k])
                        if op == "start":
                            ld.start()
                        else:
                            ld.wait()

                self.when(p, f)

            def relay(self, op):
                for i, (q, to) in enumerate(((p1, p2), (p2, p1))):

                    def f():
                        for k in range(len(self.parts)):
                            t = self.place(q, k)
                            if op == "start":
                                rcopy(t, t, xss.at[0], self.rs.at[i, k], sib).wait_recv()
                            if k % 2 == i:
                                d = rcopy(t, t, self.ss.at[2, k], self.rs.at[2, k], (to, c, z))
                                getattr(d, op)()

                    self.when(q, f)

            def last(self):
                def f():
                    for k in range(len(self.parts)):
                        t = self.place(p3, k)
                        rcopy(t, t, xss.at[0], self.rs.at[2, k], sib).wait_recv()

                self.when(p3, f)

        def slot_of(w):
            return rot(w + dp * n * per - z * per, dp)

        sq = Share(
            FQ,
            lambda w, k: gq_h.at[half_rows, pl.ds(mult(k * D + w * hq, 128), hq)],
            [(j * hq, hq) for j in range(3)], pqs, pqr, 1, None,
        )
        su = Share(
            FU,
            lambda w, k: gu_h.at[half_rows, pl.ds(mult((k * dp + w) * G_, 128), G_)],
            [(j * G_, G_) for j in range(nl)], pus, pur, 4, None,
        )
        sd = Share(
            FD,
            lambda w, k: gd_h.at[
                pl.ds(mult(slot_of(w) * G_ + c * gh, gh), gh), pl.ds(dcols[k][0], dcols[k][1])
            ],
            dcols, pds, pdr, 4 + nl, None if per >= dp else (lambda w: slot_of(w) < per),
        )
        so = Share(
            FO, lambda w, k: go_h.at[half_rows, pl.ds(dcols[k][0], dcols[k][1])],
            dcols, pos, por, 6 + nl, lambda w: o_who == w,
        )

        def shard_on(dst, k, op):
            r = half_rows if op != "wait_recv" else pl.ds(mult((1 - c) * uh, uh), uh)
            getattr(rcopy(dst.at[r], dst.at[r], pfs.at[k], pfr.at[k], sib), op)()

        def d_on(op):
            for i in range(per):
                side = c if op != "wait_recv" else 1 - c
                t = gd_h.at[pl.ds(mult(i * G_ + side * gh, gh), gh)]
                getattr(rcopy(t, t, pfs.at[3 + i], pfr.at[3 + i], sib), op)()

        def done(sh, on):
            sh.last()
            sh.own("wait_send")
            sh.relay("wait_send")
            on()

        gd_line = (GD, ZD, MD if far else None, nl, d_owner, zds, zdr, mls.at[0], mlr.at[0])
        gu_line = (GU, ZU, MU, zus, zur, mls.at[1], mlr.at[1])
        gq_line = (GQ, ZQ, MQ, zqs, zqr, mls.at[2], mlr.at[2])
        go_line = (GO, ZO, None, no, o_owner, zos, zor, None, None)
        spread(DYO, DY, dss, drs, "wait_send")
        lax.fori_loop(0, nb, y_step, 0)
        add_half(GD, RD, 0, nl)
        line_b(*gd_line, "start")
        grad(lambda o, w: flat(A2[:, :, o : o + w]), lambda o, w: flat(SL[:, :, o : o + w]),
             GU, D, fq, 512, 512, uh)
        swap(GU, RU, 1, "start")
        for i in range(1, n):
            pl.semaphore_signal(
                zfree, inc=1, device_id=(p, c, rot(z + i, n)), device_id_type=MESH
            )

        lax.fori_loop(0, 1, attn_back, 0)
        if far:
            line_b_on(*gd_line, "start")
        pl.semaphore_wait(zfree, n - 1)
        add_half(GU, RU, 1, n)
        line_a(*gu_line, "start")
        add_on(0, yss, yrs, rlr)
        lax.fori_loop(1, spc, attn_back, 0)

        for k in range(3):
            give(k, 0, yss, yrs, rlr, "wait_send")

        tfl = slice(None)
        grad(lambda o, w: O[tfl, o : o + w], lambda o, w: flat(DY[:, :, o : o + w]),
             GO, hq, D, 256, 512, uh)
        swap(GO, RO, 2, "start")
        grad(lambda o, w: flat(A1[:, :, o : o + w]), lambda o, w: QKV[tfl, o : o + w],
             GQ, D, 3 * hq, 512, 256, uh)
        swap(GQ, RQ, 3, "start")
        line_a_on(*gu_line, "start")
        line_sum_b(GD, ZD, FD, nl, d_owner, zdr, sd.own, far)
        add_half(GO, RO, 2, no)
        line_b(*go_line, "start")
        add_half(GQ, RQ, 3, n)
        line_a(*gq_line, "start")

        def dz_step(i, _):
            b = yb(i)

            def part(q, _):
                rc = pl.ds(mult(q * RC, RC), RC)
                cen, rstd = stats(X[b, rc, :].astype(F32))
                X[b, rc, :] = (cen * rstd).astype(BF)
                return 0

            lax.fori_loop(0, R // RC, part, 0)
            k = 256 // u if u <= 256 else 1
            for j in range(D // 256):
                cs = slice(j * 256, (j + 1) * 256)
                xh = X[b, :, cs].astype(F32)
                d1 = nt(QKV[rows(b), :], flat(WQ[j * k : (j + 1) * k]))
                d2 = nt(SL[b], flat(WU[j * k : (j + 1) * k]))
                LNA[0, :, cs] += jnp.sum(d1 * xh, axis=0, keepdims=True)
                LNA[1, :, cs] += jnp.sum(d1, axis=0, keepdims=True)
                LNA[2, :, cs] += jnp.sum(d2 * xh, axis=0, keepdims=True)
                LNA[3, :, cs] += jnp.sum(d2, axis=0, keepdims=True)
                YS[b, :, cs] = (d1 * VEC[0, :, cs] + d2 * VEC[2, :, cs]).astype(BF)
            for k in range(3):

                @pl.when(i == k)
                def _():
                    give(k, 1, zss, zrs, rlr, "start")

            return 0

        lax.fori_loop(0, 2, dz_step, 0)
        sd.relay("start")
        line_sum(lambda: GU[z, c], ZU, FU, zur)
        su.own("start")
        give(3, 0, yss, yrs, rlr, "wait_send")
        lax.fori_loop(2, nb, dz_step, 0)
        line_a_on(*gq_line, "start")

        add_on(1, zss, zrs, rlr)
        lcopy(x_h, A1.at[0], loc.at[0]).start()
        lcopy(dy_h, A1.at[1], loc.at[8 + nl]).start()

        all_in(YR, yrs)

        lcopy(x_h, A1.at[0], loc.at[0]).wait()
        lcopy(dy_h, A1.at[1], loc.at[8 + nl]).wait()

        def out_part(k, _):
            rc = pl.ds(mult(k * RC, RC), RC)
            acc = A1[0, rc, :].astype(F32) + VEC[4]
            for q in range(3):
                acc = acc + YR[q, rc, :].astype(F32)
            A1[2, rc, :] = acc.astype(BF)
            return 0

        lax.fori_loop(0, R // RC, out_part, 0)
        lcopy(A1.at[2], yo_h, loc.at[9 + nl]).start()


        for r in range(4):
            v = LNA[r]
            for k in range(n):
                SG[k, r] = v[:, k * u : (k + 1) * u]
        v = QBA[...]
        for j in range(3):
            for i in range(no):
                unit = (j * D + p * hq) // u + i
                SG[unit // 3, 4 + rot(unit, 3)] = v[:, j * hq + i * u : j * hq + (i + 1) * u]
        v = DYA[...]
        for i in range(no):
            SG[p * no + i, 7] = v[:, i * u : (i + 1) * u]
            SG[p * no + i, 12] = v[:, i * u : (i + 1) * u]
        v = UBA[...]
        for k in range(nl):
            for i in range(G_ // u):
                unit = ((k * dp + p) * G_) // u + i
                o = k * G_ + i * u
                SG[unit // (ffs // u), 8 + rot(unit, ffs // u)] = v[:, o : o + u]
        rcopy(SG, RSG, sgs, sgr, sib).start()


        rcopy(SG, RSG, sgs, sgr, sib).wait()
        SG[...] = SG[...] + RSG[...]

        def line_s(op):
            for i in range(1, n):
                to = rot(z + i, n)
                d = rcopy(SG.at[to], ZSG.at[n - 1 - i], zsgs.at[i], zsgr.at[n - 1 - i], (p, c, to))
                getattr(d, op)()

        line_s("start")
        su.relay("start")
        line_sum_b(GO, ZO, FO, no, o_owner, zor, so.own, False)
        line_sum(lambda: GQ[z, c], ZQ, FQ, zqr)
        sq.own("start")
        done(sd, lambda: d_on("start"))
        done(su, lambda: shard_on(gu_h, 1, "start"))

        for i in range(n - 1):
            rcopy(ZSG.at[i], ZSG.at[i], xss.at[0], zsgr.at[i], sib).wait_recv()
        FSG[...] = SG[z] + sum_of(ZSG)

        def plane_s(op):
            for i in range(1, dp):
                to = (rot(p + i, dp), c, z)
                getattr(rcopy(FSG, PSG.at[dp - 1 - i], psgs.at[i], psgr.at[dp - 1 - i], to), op)()

        plane_s("start")

        give(0, 1, zss, zrs, rlr, "wait_send")
        give(1, 1, zss, zrs, rlr, "wait_send")
        all_in(ZR, zrs)

        def token_grad(k, _):
            rc = pl.ds(mult(k * RC, RC), RC)
            cen, rstd = stats(A1[0, rc, :].astype(F32))
            xh = cen * rstd
            tot = ZR[0, rc, :].astype(F32)
            for q in range(1, 3):
                tot = tot + ZR[q, rc, :].astype(F32)
            m1 = jnp.mean(tot, axis=-1, keepdims=True)
            m2 = jnp.mean(tot * xh, axis=-1, keepdims=True)
            A1[3, rc, :] = (A1[1, rc, :].astype(F32) + rstd * (tot - m1 - xh * m2)).astype(BF)
            return 0

        lax.fori_loop(0, R // RC, token_grad, 0)
        lcopy(A1.at[3], dxo_h, loc.at[0]).start()

        so.relay("start")
        sq.relay("start")
        for i in range(dp - 1):
            rcopy(PSG.at[i], PSG.at[i], xss.at[0], psgr.at[i], sib).wait_recv()
        acc = FSG[...]
        for i in range(dp - 1):
            acc = acc + PSG[i]
        SM[...] = acc
        lcopy(SM, gs_h, loc.at[8 + nl]).start()
        done(so, lambda: shard_on(go_h, 2, "start"))
        done(sq, lambda: shard_on(gq_h, 0, "start"))

        for k in range(3):
            shard_on((gq_h, gu_h, go_h)[k], k, "wait_recv")
            shard_on((gq_h, gu_h, go_h)[k], k, "wait_send")
        d_on("wait_recv")
        d_on("wait_send")
        small("wait_send")
        send_a(WU, wus, wur, peers, "wait_send")
        relay_w(WU, n, same, rws.at[3], wur, "wait_send")
        send_a(WQ, wqs, wqr, peers, "wait_send")
        relay_w(WQ, n, same, rws.at[0], wqr, "wait_send")
        send_b(WD, nl, d_owner, wds, wdr, peers, "wait_send")
        relay_w(WD, nl, d_owner, rws.at[1], wdr, "wait_send")
        send_b(WO, no, o_owner, wos, wor, peers, "wait_send")
        relay_w(WO, no, o_owner, rws.at[2], wor, "wait_send")
        for k, W in enumerate((WQ, WU, WD, WO)):
            pass_on(W, k, "wait_send")
        hand_on(DY, dss, drs, "wait_send")
        for k, (s, d) in enumerate(((GD, RD), (GU, RU), (GO, RO), (GQ, RQ))):
            swap(s, d, k, "wait_send")
        line_b(*gd_line, "wait_send")
        if far:
            line_b_on(*gd_line, "wait_send")
        for g in (gu_line, gq_line):
            line_a(*g, "wait_send")
            line_a_on(*g, "wait_send")
        line_b(*go_line, "wait_send")
        line_s("wait_send")
        plane_s("wait_send")

        for k in range(2, nb):
            give(k, 1, zss, zrs, rlr, "wait_send")
        lcopy(A1.at[2], yo_h, loc.at[9 + nl]).wait()
        lcopy(A1.at[3], dxo_h, loc.at[0]).wait()
        lcopy(SM, gs_h, loc.at[8 + nl]).wait()

    return kernel


PLACES = ((0, 1), (1, 1), (2, 1), (3, 1), (4, 3), (7, 1), (8, 4), (12, 1))


def widen(gq, go, gu, gd, y, dx, gs):
    u = gq.shape[0]
    mats, rows_ = (gq, go, gu, gd), (y, dx)
    order = (2, 3, 0, 1)
    cuts = max(1, min(4, u // 16))

    def kernel(a, b, c, d, e, f, g, oa, ob, oc, od, oe, of, *rest):
        outs, (ia, ib, ic, id_, wa, wb, wc, wd, ve, vf, si, so, sr) = rest[: len(PLACES)], rest[len(PLACES) :]
        src, dst = (a, b, c, d), (oa, ob, oc, od)
        inn, wide = (ia, ib, ic, id_), (wa, wb, wc, wd)

        def part(m, k):
            h = mats[m].shape[0] // cuts
            return pl.ds(k * h, h)

        def load(m, k):
            return lcopy(src[m].at[part(m, k)], inn[m].at[part(m, k)], si.at[m, k])

        def store(m, k):
            return lcopy(wide[m].at[part(m, k)], dst[m].at[part(m, k)], so.at[m, k])

        for m in order:
            for k in range(cuts):
                load(m, k).start()
        for i, (h, v) in enumerate(((e, ve), (f, vf))):
            lcopy(h, v, sr.at[i]).start()
        for o, (at, k) in zip(outs, PLACES):
            o[...] = jnp.concatenate([g[at + i] for i in range(k)], axis=1)[0]
        for m in order:
            for k in range(cuts):
                load(m, k).wait()
                wide[m][part(m, k), :] = inn[m][part(m, k), :].astype(F32)
                store(m, k).start()
        for i, (h, v, o) in enumerate(((e, ve, oe), (f, vf, of))):
            lcopy(h, v, sr.at[i]).wait()
            lcopy(v, o.at[0], sr.at[2 + i]).start()
        for m in order:
            for k in range(cuts):
                store(m, k).wait()
        for i, (v, o) in enumerate(((ve, oe), (vf, of))):
            lcopy(v, o.at[0], sr.at[2 + i]).wait()

    hbm = pl.BlockSpec(memory_space=pl.ANY)
    vmem = pl.BlockSpec(memory_space=pltpu.VMEM)
    return pl.pallas_call(
        kernel,
        out_shape=tuple(jax.ShapeDtypeStruct(v.shape, F32) for v in mats)
        + tuple(jax.ShapeDtypeStruct((1,) + v.shape, BF) for v in rows_)
        + tuple(jax.ShapeDtypeStruct((k * u,), F32) for _, k in PLACES),
        in_specs=[hbm] * 6 + [vmem],
        out_specs=[hbm] * 6 + [vmem] * len(PLACES),
        scratch_shapes=[pltpu.VMEM(v.shape, BF) for v in mats]
        + [pltpu.VMEM(v.shape, F32) for v in mats]
        + [pltpu.VMEM(v.shape, BF) for v in rows_]
        + [pltpu.SemaphoreType.DMA((4, cuts))] * 2 + [pltpu.SemaphoreType.DMA((4,))],
        compiler_params=pltpu.CompilerParams(vmem_limit_bytes=63 * 2**20),
    )(gq, go, gu, gd, y, dx, gs)


def tables(length):
    freq = (np.float32(10000.0) ** (-(np.arange(ROT // 2) * 2).astype(np.float32) / ROT)).astype(
        np.float32
    )
    ang = np.arange(length, dtype=np.float32)[:, None] * freq[None, :]
    co, si = np.cos(ang).astype(np.float32), np.sin(ang).astype(np.float32)
    half = ROT // 2
    ct = np.ones((length, HD), np.float32)
    st = np.zeros((length, HD), np.float32)
    ct[:, :half], ct[:, half:ROT] = co, co
    st[:, :half], st[:, half:ROT] = -si, si
    return tuple(np.concatenate([t, t], axis=1) for t in (ct, st))


def body(mesh, tokens, cotangent, ln1_gain, ln1_bias, ln2_gain, ln2_bias, qkv_weight, qkv_bias,
         out_weight, out_bias, up_weight, up_bias, down_weight, down_bias):
    pn = Plan(mesh, tokens, qkv_weight, up_weight, down_weight)
    n, D, R, u, ffs, hq, fq, dp = pn.n, pn.D, pn.R, pn.u, pn.ffs, pn.hq, pn.fq, pn.dp
    G_, nl, no, nb, T, L, spc = pn.g, pn.nl, pn.no, pn.nb, pn.T, pn.L, pn.spc
    uh, gh = u // 2, G_ // 2
    small, at = None, 0
    for v in (ln1_gain, ln1_bias, ln2_gain, ln2_bias, qkv_bias, out_bias, up_bias, down_bias):
        w = jnp.pad(v, (at, NSMALL * u - at - v.shape[0])).astype(F32)
        small, at = w if small is None else small + w, at + v.shape[0]
    small = small.reshape(NSMALL, 1, u)
    ct, st = tables(L)
    vm = lambda *s, t=BF: pltpu.VMEM(s, t)
    dma = lambda *s: pltpu.SemaphoreType.DMA(s)
    scratch = [
        vm(nb, R, D), vm(nb, R, D), vm(nb, R, D), vm(T // uh, uh, D),
        vm(n, 2, uh, 3 * hq), vm(n, 2, uh, fq), vm(nl, 2, gh, D), vm(no, 2, uh, D),
        vm(T, 3 * hq), vm(T, hq), vm(T, hq),
        vm(spc, pn.heads * QT, QT), vm(spc, pn.heads * QT, 2 * QT), vm(spc, pn.heads * QT, 3 * QT),
        vm(T // uh, uh, fq), vm(nb, R, fq), vm(nb, R, D), vm(3, R, D), vm(3, R, D), vm(2, R, D),
        vm(n, 2, uh, 3 * hq), vm(n, 2, uh, fq), vm(nl, 2, gh, D), vm(no, 2, uh, D),
        vm(n, uh, fq), vm(nl, gh, D),
        vm(n - 1, gh, D),
        vm(uh, fq), vm(gh, D),
        vm(NSMALL, 1, u, t=F32), vm(n, NSMALL, 1, u, t=F32), vm(7, 1, max(D, fq), t=F32),
        vm(n, NSMALL, 1, u, t=F32), vm(n, NSMALL, 1, u, t=F32), vm(n - 1, NSMALL, 1, u, t=F32),
        vm(NSMALL, 1, u, t=F32), vm(dp - 1, NSMALL, 1, u, t=F32),
        vm(4, 1, D, t=F32), vm(1, fq, t=F32), vm(1, 3 * hq, t=F32), vm(1, hq, t=F32),
        vm(L, hq, t=F32), vm(L, hq, t=F32),
        dma(dp), dma(nb), dma(dp), dma(nb), dma(n), dma(n),
        dma(n), dma(n), dma(n), dma(n), dma(n), dma(nl), dma(n), dma(no), dma(4), dma(4),
        dma(nb), dma(3), dma(nb), dma(3),
        dma(4), dma(4), dma(n), dma(n), dma(n), dma(n), dma(nl), dma(n), dma(no), dma(n),
        dma(3, 3), dma(3, 3), dma(3, nl), dma(3, nl), dma(3, 2), dma(3, 2), dma(3, 2), dma(3, 2),
        dma(3 + ffs // G_), dma(3 + ffs // G_),
        pltpu.SemaphoreType.DMA, pltpu.SemaphoreType.DMA, dma(n), dma(n), dma(dp), dma(dp), dma(10 + nl),
        pltpu.SemaphoreType.REGULAR, dma(5 + nl), dma(4), dma(2), vm(gh, D), dma(3), dma(3),
    ]
    hbm = pl.BlockSpec(memory_space=pl.ANY)
    vmem = pl.BlockSpec(memory_space=pltpu.VMEM)
    sds = jax.ShapeDtypeStruct
    y, dx, gq, go, gu, gd, gs = pl.pallas_call(
        make_kernel(pn),
        out_shape=(
            sds((R, D), BF), sds((R, D), BF), sds((u, 3 * D), BF), sds((u, D), BF),
            sds((u, pn.FF), BF), sds((ffs, D), BF), sds((NSMALL, 1, u), F32),
        ),
        in_specs=[hbm] * 7 + [vmem] * 2,
        out_specs=[hbm] * 7,
        scratch_shapes=scratch,
        compiler_params=pltpu.CompilerParams(
            collective_id=0, has_side_effects=True, vmem_limit_bytes=63 * 2**20
        ),
    )(tokens[0], cotangent[0], small, qkv_weight, out_weight, up_weight, down_weight,
      jnp.asarray(ct), jnp.asarray(st))
    gq, go, gu, gd, y, dx, *sv = widen(gq, go, gu, gd, y, dx, gs)
    return (
        y, dx, sv[0], sv[1], sv[2], sv[3], gq, sv[4], go, sv[5], gu, sv[6], gd, sv[7],
    )


def solution(mesh):
    row = P(("dp", "fsdp"), "ctx", None)
    vec, mat = P("fsdp"), P("fsdp", None)
    in_specs = (row, row, vec, vec, vec, vec, mat, vec, mat, vec, mat, vec, mat, vec)
    out_specs = (row, row, vec, vec, vec, vec, mat, vec, mat, vec, mat, vec, mat, vec)
    return jax.shard_map(
        functools.partial(body, mesh), mesh=mesh, in_specs=in_specs, out_specs=out_specs, check_vma=False
    )
```
